512 devices in a mesh: grp: 8 (over z_lo, core), slab: 64 (over y, z_hi, x).
Axes of the slice: x: 4, y: 4, z: 16 (z_hi: 4, z_lo: 4; z = z_hi * 4 + z_lo), core: 2. Of those that a mesh axis runs over, the one named last changes fastest.
Arguments:
- adjoint: float32 [9, 128, 128, 128], P(None, 'grp', 'slab'), may hold values from -6 to 6
- source: float32 [9, 128, 128, 128], P(None, 'grp', 'slab'), may hold values from -6 to 6
- contrast: float32 [7, 9, 9], replicated, may hold values from -2 to 2
- phase_id: int32 [128, 128, 128], P('grp', 'slab'), may hold values 0 or 1
- grain_id: int32 [128, 128, 128], P('grp', 'slab'), may hold values from 0 to 4095
- orientation: int32 [4096], replicated, may hold values from 0 to 5
Outputs:
- updated: float32 [9, 128, 128, 128], P(None, 'grp', 'slab')
The draws below stay inside these ranges and needn't reach their ends.
Inputs may be any that keep to these rules, and one draw needn't show every extreme that they name: `phase_id`: 1 marks a ceramic voxel, 0 a polymer voxel.
All inputs are finite; a program needn't handle non-finite values. No bound on the sum of `phase_id` on one device may be relied on, other than what follows from the above.
Results may differ from the reference program's by a relative error of at most 0.0001.
Values sent between devices are 32-bit elements; how exact they have to be, the bound alone decides.
A program may use at most 64 MiB of HBM per device.

```python
import math
import jax
import jax.numpy as jnp
from jax import lax

NX = 128
NY = 128
NZ = 128
COMPS = 9
VARIANTS = 6
GRAINS = 4096
ENTRIES = 7


def place_ends(entries, rng, low, largest):
    longest = entries.shape.index(max(entries.shape))
    spots = []
    for shift in (0, 1):
        where = [jax.random.randint(jax.random.fold_in(rng, axis), (), 0, length) for axis, length in enumerate(entries.shape)]
        where[longest] = (where[longest] + shift) % entries.shape[longest]
        spots.append(tuple(where))
    return entries.at[spots[0]].set(low).at[spots[1]].set(largest)


def shard_levels(key, shape, shards, smallest, high):
    gain = 1.0
    for dim, blocks in shards:
        draws = jax.random.uniform(jax.random.fold_in(jax.random.fold_in(key, 6), dim), (blocks,), jnp.float32, smallest / len(shards), high / len(shards))
        gain = gain * jnp.repeat(jnp.exp(draws), shape[dim] // blocks).reshape((-1,) + (1,) * (len(shape) - 1 - dim))
    return gain


def gaussian(rng, dims, width, reach, split=(), kind=jnp.bfloat16):
    loudness = shard_levels(rng, dims, split, -0.22, 0.18) if split else 1.0
    values = jax.random.normal(rng, dims, jnp.float32) * width * loudness
    return jnp.minimum(jnp.maximum(values, -reach), reach).astype(kind)


def setup_inputs(seed: int = 0) -> dict:
    seeds = jax.random.split(jax.random.key(seed), 7)
    adjoint = gaussian(seeds[0], (COMPS, NY, NZ, NX), 1.0, 6.0, ((1, 8), (2, 64)), jnp.float32)
    source = gaussian(seeds[1], (COMPS, NY, NZ, NX), 1.0, 6.0, ((1, 8), (2, 64)), jnp.float32)
    contrast = gaussian(seeds[2], (ENTRIES, COMPS, COMPS), COMPS ** -0.5, 2.0, (), jnp.float32)
    phase_id = place_ends((jax.random.randint(seeds[3], (NY, NZ, NX), 0, 5) < 3).astype(jnp.int32), jax.random.fold_in(seeds[3], 1), 0, 1)
    grain_id = place_ends(jax.random.randint(seeds[4], (NY, NZ, NX), 0, GRAINS), jax.random.fold_in(seeds[4], 1), 0, GRAINS - 1).astype(jnp.int32)
    orientation = place_ends(jax.random.randint(seeds[5], (GRAINS,), 0, VARIANTS), jax.random.fold_in(seeds[5], 1), 0, VARIANTS - 1).astype(jnp.int32)
    return {"adjoint": adjoint, "source": source, "contrast": contrast, "phase_id": phase_id, "grain_id": grain_id, "orientation": orientation}


REF_SHEAR = 1.5
REF_PERMIT = 0.8
ROOT_HALF = math.sqrt(0.5)

def symbol(count, length, target):
    angles = jnp.arange(count, dtype=jnp.int32).astype(jnp.float32) * (2.0 * math.pi / length)
    return lax.complex(jnp.cos(angles) - 1.0, jnp.sin(angles)).reshape(target)

def reference(adjoint, source, contrast, phase_id, grain_id, orientation):
    spectrum = jnp.fft.rfftn(adjoint, axes=(1, 2, 3))
    half_x = NX // 2 + 1
    along_x = symbol(half_x, NX, (1, 1, half_x))
    along_y = symbol(NY, NY, (NY, 1, 1))
    along_z = symbol(NZ, NZ, (1, NZ, 1))
    conj_x = jnp.conj(along_x)
    conj_y = jnp.conj(along_y)
    conj_z = jnp.conj(along_z)
    parts = [spectrum[i] for i in range(9)]
    force_x = conj_x * parts[0] + ROOT_HALF * (conj_z * parts[4] + conj_y * parts[5])
    force_y = conj_y * parts[1] + ROOT_HALF * (conj_z * parts[3] + conj_x * parts[5])
    force_z = conj_z * parts[2] + ROOT_HALF * (conj_y * parts[3] + conj_x * parts[4])
    force_e = -(conj_x * parts[6] + conj_y * parts[7] + conj_z * parts[8])
    squares = (along_x * conj_x).real + (along_y * conj_y).real + (along_z * conj_z).real
    anchor = (jnp.arange(NY).reshape(NY, 1, 1) == 0) & (jnp.arange(NZ).reshape(1, NZ, 1) == 0) & (jnp.arange(half_x).reshape(1, 1, half_x) == 0)
    inverse = jnp.where(anchor, 0.0, 1.0 / jnp.where(anchor, 1.0, squares))
    projected = conj_x * force_x + conj_y * force_y + conj_z * force_z
    half_inverse = 0.5 * inverse
    shear_inverse = inverse / REF_SHEAR
    disp_x = (force_x - along_x * projected * half_inverse) * shear_inverse
    disp_y = (force_y - along_y * projected * half_inverse) * shear_inverse
    disp_z = (force_z - along_z * projected * half_inverse) * shear_inverse
    potential = force_e * (inverse / REF_PERMIT)
    green_hat = jnp.stack([along_x * disp_x, along_y * disp_y, along_z * disp_z, ROOT_HALF * (along_y * disp_z + along_z * disp_y), ROOT_HALF * (along_x * disp_z + along_z * disp_x), ROOT_HALF * (along_x * disp_y + along_y * disp_x), -along_x * potential, -along_y * potential, -along_z * potential])
    green = jnp.fft.irfftn(green_hat, s=(NY, NZ, NX), axes=(1, 2, 3)).astype(jnp.float32)
    table_index = jnp.where(phase_id == 1, orientation[grain_id], VARIANTS).astype(jnp.int32)
    combined = jnp.zeros_like(source)
    for variant in range(ENTRIES):
        mapped = jnp.einsum('ji,jyzx->iyzx', contrast[variant], green, precision=lax.Precision.HIGHEST)
        combined = combined + jnp.where(table_index == variant, mapped, 0.0)
    return source - combined
```

```python
import functools

import jax
import jax.numpy as jnp
import ml_dtypes
import numpy as np
from jax import lax
from jax.experimental import pallas as pl
from jax.experimental.pallas import tpu as pltpu
from jax.sharding import PartitionSpec as P

N = 128
GRP = 8
SLAB = 64
F32 = jnp.float32
BF16 = jnp.bfloat16
ROOT_HALF = float(np.sqrt(0.5))
MESH = pl.DeviceIdType.MESH


def split_const(matrix, axis):
    high = matrix.astype(ml_dtypes.bfloat16)
    low = (matrix - high.astype(np.float64)).astype(ml_dtypes.bfloat16)
    return np.concatenate([high, high, low], axis=axis)


def angle(a, b, length=N):
    return 2.0 * np.pi * ((np.asarray(a) * np.asarray(b)) % length) / length


def x_tables():
    x = np.arange(N)
    forward = np.zeros((SLAB, 2, N))
    inverse = np.zeros((SLAB, 2, N))
    for k in range(1, SLAB):
        forward[k, 0] = np.cos(angle(k, x))
        forward[k, 1] = -np.sin(angle(k, x))
    forward[0, 0] = 1.0
    forward[0, 1] = (-1.0) ** x
    inverse[1:] = 2.0 * forward[1:]
    inverse[0] = forward[0]
    return forward.reshape(N, N), inverse.reshape(N, N)


def z_tables(first):
    z = np.arange(N).reshape(SLAB, 2)
    forward = np.zeros((2, GRP, 2, 8, 2, SLAB, 2))
    inverse = np.zeros((2, SLAB, 2, 2, GRP, 2, 8))
    for m in range(SLAB):
        hi, lo = divmod(m, 8)
        for h in range(2):
            for z2 in range(2):
                if first:
                    cos, sin = np.cos(angle(m, z[:, z2])), np.sin(angle(m, z[:, z2]))
                    if m == 0:
                        alt = (-1.0) ** z[:, z2]
                        forward[h, hi, 0, lo, z2, :, h] = 1.0
                        forward[h, hi, 1, lo, z2, :, h] = alt
                        inverse[z2, :, h, h, hi, 0, lo] = 1.0
                        inverse[z2, :, h, h, hi, 1, lo] = alt
                    else:
                        forward[h, hi, 0, lo, z2, :, h] = cos
                        forward[h, hi, 1, lo, z2, :, h] = -sin
                        inverse[z2, :, h, h, hi, 0, lo] = 2.0 * cos
                        inverse[z2, :, h, h, hi, 1, lo] = -2.0 * sin
                else:
                    k = m if h == 0 else (64 if m == 0 else N - m)
                    cos, sin = np.cos(angle(k, z[:, z2])), np.sin(angle(k, z[:, z2]))
                    forward[h, hi, 0, lo, z2, :, 0] = cos
                    forward[h, hi, 0, lo, z2, :, 1] = sin
                    forward[h, hi, 1, lo, z2, :, 0] = -sin
                    forward[h, hi, 1, lo, z2, :, 1] = cos
                    inverse[z2, :, 0, h, hi, 0, lo] = cos
                    inverse[z2, :, 0, h, hi, 1, lo] = -sin
                    inverse[z2, :, 1, h, hi, 0, lo] = sin
                    inverse[z2, :, 1, h, hi, 1, lo] = cos
    return forward.reshape(256, 256), inverse.reshape(256, 256)


def y_outer_tables(corner):
    forward = np.zeros((2, 72, GRP, 2, 8))
    inverse = np.zeros((GRP, 2, 8, 2, 72))
    g = np.arange(GRP)
    for k1 in range(8):
        cos, sin = np.cos(angle(k1, g, 8)), np.sin(angle(k1, g, 8))
        for kz in range(8):
            row = k1 * 8 + kz
            if corner and kz == 0:
                for source, target in ((0, row), (1, 64 + k1)):
                    forward[0, target, :, source, kz] = cos
                    forward[1, target, :, source, kz] = -sin
                    inverse[:, source, kz, 0, target] = cos
                    inverse[:, source, kz, 1, target] = -sin
            else:
                forward[0, row, :, 0, kz] = cos
                forward[0, row, :, 1, kz] = sin
                forward[1, row, :, 0, kz] = -sin
                forward[1, row, :, 1, kz] = cos
                inverse[:, 0, kz, 0, row] = cos
                inverse[:, 0, kz, 1, row] = -sin
                inverse[:, 1, kz, 0, row] = sin
                inverse[:, 1, kz, 1, row] = cos
    return forward.reshape(144, 128), inverse.reshape(128, 144)


def lane_parts():
    lane = np.arange(N)
    return lane // 32, lane // 2 % 16, lane % 2


def y_inner_tables():
    c, y, h = lane_parts()
    same = (c[:, None] == c[None, :]) & (h[:, None] == h[None, :])
    cos = np.where(same, np.cos(angle(y[:, None], y[None, :], 16)), 0.0)
    sin = np.where(same, np.sin(angle(y[:, None], y[None, :], 16)), 0.0)
    forward = np.block([[cos, -sin], [sin, cos]])
    inverse = np.block([[cos, sin], [-sin, cos]])
    return forward, inverse


def row_k1():
    return np.concatenate([np.repeat(np.arange(8), 8), np.arange(8)])


def twiddle_tables():
    _, y, _ = lane_parts()
    turn = angle(row_k1()[:, None], y[None, :])
    return np.stack([np.cos(turn), np.sin(turn)]).astype(np.float32)


def symbol(k):
    turn = 2.0 * np.pi * (np.asarray(k) % N) / N
    return np.stack([np.cos(turn) - 1.0, np.sin(turn)]).astype(np.float32)


def symbol_tables():
    _, k2, h = lane_parts()
    along_y = symbol(row_k1()[:, None] + 8 * k2[None, :])
    along_x = np.zeros((SLAB, 2, 8, N), np.float32)
    for s in range(SLAB):
        k = np.where(h == 0, 0, 64) if s == 0 else np.full(N, s)
        along_x[s] = np.broadcast_to(symbol(k)[:, None, :], (2, 8, N))
    along_z = np.zeros((2 * GRP, 2, 16, N), np.float32)
    for first in range(2):
        for g in range(GRP):
            for row in range(16):
                m = g * 8 + row
                if row >= 8:
                    k = np.full(N, 64)
                elif first:
                    k = np.full(N, m)
                else:
                    k = np.where(h == 0, m, 64 if m == 0 else N - m)
                along_z[first * GRP + g, :, row] = symbol(k)
    return along_x, along_y, along_z


@functools.cache
def constants():
    x_forward, x_inverse = x_tables()
    z_pairs = [z_tables(first) for first in (False, True)]
    y_pairs = [y_outer_tables(corner) for corner in (False, True)]
    inner_forward, inner_inverse = y_inner_tables()
    along_x, along_y, along_z = symbol_tables()
    return dict(
        wx=split_const(x_forward, 1),
        wxi=split_const(x_inverse, 0),
        wz=np.stack([split_const(pair[0], 1) for pair in z_pairs]),
        wzi=np.stack([split_const(pair[1], 1) for pair in z_pairs]),
        wy=np.stack([split_const(pair[0], 1) for pair in y_pairs]),
        wyi=np.stack([split_const(pair[1], 1) for pair in y_pairs]),
        wl=split_const(inner_forward, 0),
        wli=split_const(inner_inverse, 0),
        tw=twiddle_tables(),
        dx=along_x,
        dy=along_y,
        dz=along_z,
    )


CONSTANTS = ("wx", "wxi", "wz", "wzi", "wy", "wyi", "wl", "wli", "tw", "dx", "dy", "dz")


def thirds(value, axis):
    high = value.astype(BF16)
    low = (value - high.astype(F32)).astype(BF16)
    return jnp.concatenate([high, low, high], axis=axis)


def dot(left, right, contract):
    return lax.dot_general(left, right, (contract, ((), ())), preferred_element_type=F32)


def even_lanes(shape):
    return lax.broadcasted_iota(jnp.int32, shape, 1) % 2 == 0


def x_forward(forces, wx):
    return dot(wx, thirds(forces, 1), ((1,), (1,)))


def x_inverse(rows, wxi):
    return dot(thirds(rows.T, 1), wxi, ((1,), (0,)))


def z_transform(rows, wz):
    pair = jnp.concatenate([rows, jnp.roll(rows, -1, axis=1)], axis=0)
    both = dot(wz, thirds(pair, 0), ((1,), (0,)))
    return jnp.where(even_lanes((N, N)), both[:N], jnp.roll(both[N:], 1, axis=1))


def y_forward(rows, wy, wl, tw):
    outer = dot(wy, thirds(rows, 0), ((1,), (0,)))
    real, imag = outer[:72], outer[72:]
    turned = jnp.concatenate([real * tw[0] + imag * tw[1], imag * tw[0] - real * tw[1]], axis=1)
    inner = dot(thirds(turned, 1), wl, ((1,), (0,)))
    return inner[:, :N], inner[:, N:]


def y_inverse(real, imag, wyi, wli, tw):
    inner = dot(thirds(jnp.concatenate([real, imag], axis=1), 1), wli, ((1,), (0,)))
    real, imag = inner[:, :N], inner[:, N:]
    turned = jnp.concatenate([real * tw[0] - imag * tw[1], imag * tw[0] + real * tw[1]], axis=0)
    return dot(wyi, thirds(turned, 0), ((1,), (0,)))


def operator_tables(dx, dy, dz):
    def rows(main, extra):
        return jnp.concatenate([main] * 8 + [extra], axis=0)

    along_x = [rows(dx[i], dx[i]) for i in range(2)]
    along_z = [rows(dz[i][:8], dz[i][8:]) for i in range(2)]
    along_y = [dy[0], dy[1]]
    squares = (
        along_x[0] * along_x[0]
        + along_x[1] * along_x[1]
        + (along_y[0] * along_y[0] + along_y[1] * along_y[1])
        + (along_z[0] * along_z[0] + along_z[1] * along_z[1])
    )
    some = squares > 0.0
    inverse = jnp.where(some, 1.0 / jnp.where(some, squares, 1.0), 0.0)
    part = lax.broadcasted_iota(jnp.int32, squares.shape, 1) // 32
    own = [
        jnp.where(part == 0, along_x[i], jnp.where(part == 1, along_y[i], jnp.where(part == 2, along_z[i], 0.0)))
        for i in range(2)
    ]
    scale = 1.0 / (N * N * N)
    alpha = inverse * jnp.where(part == 3, scale / 0.8, scale / 1.5)
    beta = inverse * inverse * (scale / 3.0)
    return own[0], own[1], alpha, beta


def operator(real, imag, own_real, own_imag, alpha, beta):
    projected = []
    for value in (own_real * real + own_imag * imag, own_real * imag - own_imag * real):
        value = value + jnp.roll(value, 64, axis=1)
        value = value + jnp.roll(value, 32, axis=1)
        projected.append(value * beta)
    return (
        real * alpha - (own_real * projected[0] - own_imag * projected[1]),
        imag * alpha - (own_real * projected[1] + own_imag * projected[0]),
    )


def kernel(adjoint, source, contrast, phase, grain, orientation, *rest):
    tables = dict(zip(CONSTANTS, rest[: len(CONSTANTS)]))
    (
        out,
        wx, wxi, wz, wzi, wy, wyi, wl, wli, tw, dx, dy, dz,
        fields, right_side,
        halo_z_out, halo_z_in, halo_y_out, halo_y_in,
        shift_z, shift_y,
        back_z_out, back_z_in, back_y_out, back_y_in,
        send1, recv1, send2, recv2, send3, recv3, send4, recv4,
        coef, own_real, own_imag, alpha, beta, potential,
        load_sems, halo_send, halo_recv, send_sems, recv_sems,
    ) = rest[len(CONSTANTS):]
    g = lax.axis_index("grp")
    s = lax.axis_index("slab")
    first = jnp.where(s == 0, 1, 0)
    corner = jnp.where((s == 0) & (g == 0), 1, 0)

    loads = [
        pltpu.make_async_copy(adjoint, fields, load_sems.at[0]),
        pltpu.make_async_copy(tables["wx"], wx, load_sems.at[1]),
        pltpu.make_async_copy(source, right_side, load_sems.at[2]),
        pltpu.make_async_copy(tables["wz"].at[first], wz, load_sems.at[3]),
        pltpu.make_async_copy(tables["wy"].at[corner], wy, load_sems.at[4]),
        pltpu.make_async_copy(tables["wl"], wl, load_sems.at[5]),
        pltpu.make_async_copy(tables["tw"], tw, load_sems.at[6]),
        pltpu.make_async_copy(tables["dx"].at[s], dx, load_sems.at[7]),
        pltpu.make_async_copy(tables["dy"], dy, load_sems.at[8]),
        pltpu.make_async_copy(tables["dz"].at[first * GRP + g], dz, load_sems.at[9]),
        pltpu.make_async_copy(tables["wli"], wli, load_sems.at[10]),
        pltpu.make_async_copy(tables["wyi"].at[corner], wyi, load_sems.at[11]),
        pltpu.make_async_copy(tables["wzi"].at[first], wzi, load_sems.at[12]),
        pltpu.make_async_copy(tables["wxi"], wxi, load_sems.at[13]),
    ]
    for load in loads:
        load.start()

    barrier = pltpu.get_barrier_semaphore()

    def greet_slab(step, carry):
        pl.semaphore_signal(
            barrier, inc=1, device_id={"slab": lax.rem(s + step, SLAB)}, device_id_type=MESH
        )
        return carry

    def greet_grp(step, carry):
        pl.semaphore_signal(
            barrier, inc=1, device_id={"grp": lax.rem(g + step, GRP)}, device_id_type=MESH
        )
        return carry

    lax.fori_loop(1, SLAB, greet_slab, 0)
    lax.fori_loop(1, GRP, greet_grp, 0)

    loads[0].wait()
    for slot, part in enumerate((4, 3, 2, 8)):
        halo_z_out[slot] = fields[part, pl.ds(1, 16, stride=2), :]
    for slot, part in enumerate((5, 1, 3, 7)):
        halo_y_out[slot] = fields[part, 30:32, :]
    pl.semaphore_wait(barrier, SLAB - 1 + GRP - 1)

    halos = [
        pltpu.make_async_remote_copy(
            halo_z_out, halo_z_in, halo_send.at[0], halo_recv.at[0],
            device_id={"slab": lax.rem(s + 1, SLAB)}, device_id_type=MESH,
        ),
        pltpu.make_async_remote_copy(
            halo_y_out, halo_y_in, halo_send.at[1], halo_recv.at[1],
            device_id={"grp": lax.rem(g + 1, GRP)}, device_id_type=MESH,
        ),
    ]
    for halo in halos:
        halo.start()

    for slot, part in enumerate((4, 3, 2, 8)):
        shift_z[slot, pl.ds(1, 16, stride=2), :] = fields[part, pl.ds(0, 16, stride=2), :]
    for slot, part in enumerate((5, 1, 3, 7)):
        shift_y[slot, 2:32, :] = fields[part, 0:30, :]

    halos[0].wait_recv()
    halos[1].wait_recv()
    for slot in range(4):
        shift_z[slot, pl.ds(0, 16, stride=2), :] = halo_z_in[slot]
        shift_y[slot, 0:2, :] = halo_y_in[slot]

    def along_x(part):
        value = fields[part]
        return jnp.roll(value, 1, axis=1) - value

    def along_y(slot):
        return shift_y[slot] - fields[(5, 1, 3, 7)[slot]]

    def along_z(slot):
        return shift_z[slot] - fields[(4, 3, 2, 8)[slot]]

    forces = jnp.concatenate(
        [
            along_x(0) + ROOT_HALF * (along_z(0) + along_y(0)),
            along_y(1) + ROOT_HALF * (along_z(1) + along_x(5)),
            along_z(2) + ROOT_HALF * (along_y(2) + along_x(4)),
            -(along_x(6) + along_y(3) + along_z(3)),
        ],
        axis=0,
    )

    loads[1].wait()
    send1[...] = x_forward(forces, wx[...]).reshape(SLAB, 2, N)

    def exchange_slab(sent, landed, which):
        def start(step, carry):
            peer = lax.rem(s + step, SLAB)
            pltpu.make_async_remote_copy(
                sent.at[peer], landed.at[s], send_sems.at[which], recv_sems.at[which],
                device_id={"slab": peer}, device_id_type=MESH,
            ).start()
            return carry

        lax.fori_loop(1, SLAB, start, 0)
        landed[s] = sent[s]

    def exchange_grp(sent, landed, which):
        def start(step, carry):
            peer = lax.rem(g + step, GRP)
            pltpu.make_async_remote_copy(
                sent.at[peer], landed.at[g], send_sems.at[which], recv_sems.at[which],
                device_id={"grp": peer}, device_id_type=MESH,
            ).start()
            return carry

        lax.fori_loop(1, GRP, start, 0)
        landed[g] = sent[g]

    def arrived(landed, which, count):
        block = landed.at[pl.ds(0, count)]
        pltpu.make_async_copy(block, block, recv_sems.at[which]).wait()

    def gone(sent, which, count):
        block = sent.at[pl.ds(0, count)]
        pltpu.make_async_copy(block, block, send_sems.at[which]).wait()

    exchange_slab(send1, recv1, 0)

    ids = grain[...]
    high, low = ids // N, ids % N
    entry = jnp.zeros((32, N), jnp.int32)
    for row in range(32):
        line = jnp.broadcast_to(orientation[row : row + 1, :], (32, N))
        entry = jnp.where(high == row, jnp.take_along_axis(line, low, axis=1), entry)
    entry = jnp.where(phase[...] == 1, entry, 6)
    masks = [entry == t for t in range(6)]
    for pair in range(81):
        value = jnp.full((32, N), contrast[6, pair], F32)
        for t in range(6):
            value = jnp.where(masks[t], contrast[t, pair], value)
        coef[pair] = value

    arrived(recv1, 0, SLAB - 1)
    loads[3].wait()
    send2[...] = z_transform(recv1[...].reshape(N, N), wz[...]).reshape(GRP, 16, N)
    exchange_grp(send2, recv2, 1)

    for load in loads[4:14]:
        load.wait()
    own_real[...], own_imag[...], alpha[...], beta[...] = operator_tables(dx, dy, dz)

    arrived(recv2, 1, GRP - 1)
    real, imag = y_forward(recv2[...].reshape(N, N), wy[...], wl[...], tw)
    real, imag = operator(real, imag, own_real[...], own_imag[...], alpha[...], beta[...])
    send3[...] = y_inverse(real, imag, wyi[...], wli[...], tw).reshape(GRP, 16, N)
    exchange_grp(send3, recv3, 2)

    arrived(recv3, 2, GRP - 1)
    send4[...] = z_transform(recv3[...].reshape(N, N), wzi[...]).reshape(SLAB, 2, N)
    exchange_slab(send4, recv4, 3)

    arrived(recv4, 3, SLAB - 1)
    potential[...] = x_inverse(recv4[...].reshape(N, N), wxi[...]).reshape(4, 32, N)

    for part in range(4):
        back_z_out[part] = potential[part, pl.ds(0, 16, stride=2), :]
        back_y_out[part] = potential[part, 0:2, :]
    backs = [
        pltpu.make_async_remote_copy(
            back_z_out, back_z_in, halo_send.at[2], halo_recv.at[2],
            device_id={"slab": lax.rem(s + SLAB - 1, SLAB)}, device_id_type=MESH,
        ),
        pltpu.make_async_remote_copy(
            back_y_out, back_y_in, halo_send.at[3], halo_recv.at[3],
            device_id={"grp": lax.rem(g + GRP - 1, GRP)}, device_id_type=MESH,
        ),
    ]
    for back in backs:
        back.start()
    for part in range(4):
        shift_z[part, pl.ds(0, 16, stride=2), :] = potential[part, pl.ds(1, 16, stride=2), :]
        shift_y[part, 0:30, :] = potential[part, 2:32, :]
    loads[2].wait()
    for back in backs:
        back.wait_recv()
    for part in range(4):
        shift_z[part, pl.ds(1, 16, stride=2), :] = back_z_in[part]
        shift_y[part, 30:32, :] = back_y_in[part]

    values = [potential[part] for part in range(4)]
    grad_x = [jnp.roll(value, N - 1, axis=1) - value for value in values]
    grad_y = [shift_y[part] - values[part] for part in range(4)]
    grad_z = [shift_z[part] - values[part] for part in range(4)]
    green = [
        grad_x[0],
        grad_y[1],
        grad_z[2],
        ROOT_HALF * (grad_y[2] + grad_z[1]),
        ROOT_HALF * (grad_x[2] + grad_z[0]),
        ROOT_HALF * (grad_x[1] + grad_y[0]),
        -grad_x[3],
        -grad_y[3],
        -grad_z[3],
    ]
    for i in range(9):
        total = right_side[i]
        for j in range(9):
            total = total - coef[j * 9 + i] * green[j]
        out[i] = total

    for halo in halos + backs:
        halo.wait_send()
    gone(send1, 0, SLAB - 1)
    gone(send2, 1, GRP - 1)
    gone(send3, 2, GRP - 1)
    gone(send4, 3, SLAB - 1)


def per_device(adjoint, source, contrast, phase_id, grain_id, orientation):
    table = constants()
    vmem = pl.BlockSpec(memory_space=pltpu.VMEM)
    smem = pl.BlockSpec(memory_space=pltpu.SMEM)
    anywhere = pl.BlockSpec(memory_space=pl.ANY)
    flat = (9, 32, N)
    result = pl.pallas_call(
        kernel,
        out_shape=jax.ShapeDtypeStruct(flat, F32),
        in_specs=[anywhere, anywhere, smem, vmem, vmem, vmem] + [anywhere] * len(CONSTANTS),
        out_specs=vmem,
        scratch_shapes=[
            pltpu.VMEM((128, 384), BF16),
            pltpu.VMEM((384, 128), BF16),
            pltpu.VMEM((256, 768), BF16),
            pltpu.VMEM((256, 768), BF16),
            pltpu.VMEM((144, 384), BF16),
            pltpu.VMEM((128, 432), BF16),
            pltpu.VMEM((768, 256), BF16),
            pltpu.VMEM((768, 256), BF16),
            pltpu.VMEM((2, 72, N), F32),
            pltpu.VMEM((2, 8, N), F32),
            pltpu.VMEM((2, 72, N), F32),
            pltpu.VMEM((2, 16, N), F32),
            pltpu.VMEM(flat, F32),
            pltpu.VMEM(flat, F32),
            pltpu.VMEM((4, 16, N), F32),
            pltpu.VMEM((4, 16, N), F32),
            pltpu.VMEM((4, 2, N), F32),
            pltpu.VMEM((4, 2, N), F32),
            pltpu.VMEM((4, 32, N), F32),
            pltpu.VMEM((4, 32, N), F32),
            pltpu.VMEM((4, 16, N), F32),
            pltpu.VMEM((4, 16, N), F32),
            pltpu.VMEM((4, 2, N), F32),
            pltpu.VMEM((4, 2, N), F32),
            pltpu.VMEM((SLAB, 2, N), F32),
            pltpu.VMEM((SLAB, 2, N), F32),
            pltpu.VMEM((GRP, 16, N), F32),
            pltpu.VMEM((GRP, 16, N), F32),
            pltpu.VMEM((GRP, 16, N), F32),
            pltpu.VMEM((GRP, 16, N), F32),
            pltpu.VMEM((SLAB, 2, N), F32),
            pltpu.VMEM((SLAB, 2, N), F32),
            pltpu.VMEM((81, 32, N), F32),
            pltpu.VMEM((72, N), F32),
            pltpu.VMEM((72, N), F32),
            pltpu.VMEM((72, N), F32),
            pltpu.VMEM((72, N), F32),
            pltpu.VMEM((4, 32, N), F32),
            pltpu.SemaphoreType.DMA((14,)),
            pltpu.SemaphoreType.DMA((4,)),
            pltpu.SemaphoreType.DMA((4,)),
            pltpu.SemaphoreType.DMA((4,)),
            pltpu.SemaphoreType.DMA((4,)),
        ],
        compiler_params=pltpu.CompilerParams(
            collective_id=0, has_side_effects=True, vmem_limit_bytes=32 * 1024 * 1024
        ),
    )(
        adjoint.reshape(flat),
        source.reshape(flat),
        contrast.reshape(7, 81),
        phase_id.reshape(32, N),
        grain_id.reshape(32, N),
        orientation.reshape(32, N),
        *[jnp.asarray(table[name]) for name in CONSTANTS],
    )
    return result.reshape(adjoint.shape)


def solution(mesh):
    placed = (
        P(None, "grp", "slab", None),
        P(None, "grp", "slab", None),
        P(),
        P("grp", "slab", None),
        P("grp", "slab", None),
        P(),
    )
    return jax.shard_map(
        per_device,
        mesh=mesh,
        in_specs=placed,
        out_specs=P(None, "grp", "slab", None),
        check_vma=False,
    )
```

```python
import functools

import jax
import jax.numpy as jnp
import ml_dtypes
import numpy as np
from jax import lax
from jax.experimental import pallas as pl
from jax.experimental.pallas import tpu as pltpu
from jax.sharding import PartitionSpec as P

N = 128
GRP = 8
SLAB = 64
F32 = jnp.float32
BF16 = jnp.bfloat16
ROOT_HALF = float(np.sqrt(0.5))
MESH = pl.DeviceIdType.MESH


def split_const(matrix, axis):
    high = matrix.astype(ml_dtypes.bfloat16)
    low = (matrix - high.astype(np.float64)).astype(ml_dtypes.bfloat16)
    return np.concatenate([high, high, low], axis=axis)


def angle(a, b, length=N):
    return 2.0 * np.pi * ((np.asarray(a) * np.asarray(b)) % length) / length


def x_tables():
    x = np.arange(N)
    forward = np.zeros((SLAB, 2, N))
    inverse = np.zeros((SLAB, 2, N))
    for k in range(1, SLAB):
        forward[k, 0] = np.cos(angle(k, x))
        forward[k, 1] = -np.sin(angle(k, x))
    forward[0, 0] = 1.0
    forward[0, 1] = (-1.0) ** x
    inverse[1:] = 2.0 * forward[1:]
    inverse[0] = forward[0]
    return forward.reshape(N, N), inverse.reshape(N, N)


def z_tables(first):
    z = (2 * np.arange(SLAB)[:, None] + np.arange(3)[None, :]) % N
    forward = np.zeros((2, GRP, 2, 8, 3, SLAB, 2))
    inverse = np.zeros((3, SLAB, 2, 2, GRP, 2, 8))
    for m in range(SLAB):
        hi, lo = divmod(m, 8)
        for h in range(2):
            for z2 in range(3):
                if first:
                    cos, sin = np.cos(angle(m, z[:, z2])), np.sin(angle(m, z[:, z2]))
                    if m == 0:
                        alt = (-1.0) ** z[:, z2]
                        forward[h, hi, 0, lo, z2, :, h] = 1.0
                        forward[h, hi, 1, lo, z2, :, h] = alt
                        inverse[z2, :, h, h, hi, 0, lo] = 1.0
                        inverse[z2, :, h, h, hi, 1, lo] = alt
                    else:
                        forward[h, hi, 0, lo, z2, :, h] = cos
                        forward[h, hi, 1, lo, z2, :, h] = -sin
                        inverse[z2, :, h, h, hi, 0, lo] = 2.0 * cos
                        inverse[z2, :, h, h, hi, 1, lo] = -2.0 * sin
                else:
                    k = m if h == 0 else (64 if m == 0 else N - m)
                    cos, sin = np.cos(angle(k, z[:, z2])), np.sin(angle(k, z[:, z2]))
                    forward[h, hi, 0, lo, z2, :, 0] = cos
                    forward[h, hi, 0, lo, z2, :, 1] = sin
                    forward[h, hi, 1, lo, z2, :, 0] = -sin
                    forward[h, hi, 1, lo, z2, :, 1] = cos
                    inverse[z2, :, 0, h, hi, 0, lo] = cos
                    inverse[z2, :, 0, h, hi, 1, lo] = -sin
                    inverse[z2, :, 1, h, hi, 0, lo] = sin
                    inverse[z2, :, 1, h, hi, 1, lo] = cos
    return forward.reshape(256, 384), inverse.reshape(384, 256)


def y_outer_tables(corner):
    forward = np.zeros((2, 72, GRP, 2, 8))
    inverse = np.zeros((GRP, 2, 8, 2, 72))
    g = np.arange(GRP)
    for k1 in range(8):
        cos, sin = np.cos(angle(k1, g, 8)), np.sin(angle(k1, g, 8))
        for kz in range(8):
            row = k1 * 8 + kz
            if corner and kz == 0:
                for source, target in ((0, row), (1, 64 + k1)):
                    forward[0, target, :, source, kz] = cos
                    forward[1, target, :, source, kz] = -sin
                    inverse[:, source, kz, 0, target] = cos
                    inverse[:, source, kz, 1, target] = -sin
            else:
                forward[0, row, :, 0, kz] = cos
                forward[0, row, :, 1, kz] = sin
                forward[1, row, :, 0, kz] = -sin
                forward[1, row, :, 1, kz] = cos
                inverse[:, 0, kz, 0, row] = cos
                inverse[:, 0, kz, 1, row] = -sin
                inverse[:, 1, kz, 0, row] = sin
                inverse[:, 1, kz, 1, row] = cos
    return forward.reshape(144, 128), inverse.reshape(128, 144)


def y_edge_tables():
    turn = angle(np.arange(8)[:, None], np.arange(8)[None, :] + 1, 8)
    forward = np.zeros((2, 2, 8, 8, 2))
    for ri in range(2):
        forward[ri, 0, :, :, ri] = np.cos(turn)
        forward[ri, 1, :, :, ri] = np.sin(turn)
    inverse = np.concatenate([np.cos(turn).T, np.sin(turn).T])
    return forward.reshape(32, 16).astype(np.float32), inverse.astype(np.float32)


def lane_parts():
    lane = np.arange(N)
    return lane // 16 % 4, lane % 16, lane // 64


def edge_parts():
    lane = np.arange(N)
    return lane // 8 % 4, lane // 32 % 2, lane // 64


def y_inner_tables():
    c, y, h = lane_parts()
    same = (c[:, None] == c[None, :]) & (h[:, None] == h[None, :])
    cos = np.where(same, np.cos(angle(y[:, None], y[None, :], 16)), 0.0)
    sin = np.where(same, np.sin(angle(y[:, None], y[None, :], 16)), 0.0)
    edge_c, edge_h, edge_real = edge_parts()
    meet = (edge_c[:, None] == c[None, :]) & (edge_h[:, None] == h[None, :])
    to_real = (meet & (edge_real[:, None] == 1)).astype(np.float64)
    to_imag = (meet & (edge_real[:, None] == 0)).astype(np.float64)
    forward = np.block([[cos, -sin], [sin, cos], [to_real, to_imag]])
    inverse = np.block([[cos, sin, to_real.T], [-sin, cos, to_imag.T]])
    return forward, inverse


def row_k1():
    return np.concatenate([np.repeat(np.arange(8), 8), np.arange(8)])


def twiddle_tables():
    _, y, _ = lane_parts()
    turn = angle(row_k1()[:, None], y[None, :])
    return np.stack([np.cos(turn), np.sin(turn)]).astype(np.float32)


def symbol(k):
    turn = 2.0 * np.pi * (np.asarray(k) % N) / N
    return np.stack([np.cos(turn) - 1.0, np.sin(turn)]).astype(np.float32)


def symbol_tables():
    _, k2, h = lane_parts()
    along_y = symbol(row_k1()[:, None] + 8 * k2[None, :])
    along_x = np.zeros((SLAB, 2, 8, N), np.float32)
    for s in range(SLAB):
        k = np.where(h == 0, 0, 64) if s == 0 else np.full(N, s)
        along_x[s] = np.broadcast_to(symbol(k)[:, None, :], (2, 8, N))
    along_z = np.zeros((2 * GRP, 2, 16, N), np.float32)
    for first in range(2):
        for g in range(GRP):
            for row in range(16):
                m = g * 8 + row
                if row >= 8:
                    k = np.full(N, 64)
                elif first:
                    k = np.full(N, m)
                else:
                    k = np.where(h == 0, m, 64 if m == 0 else N - m)
                along_z[first * GRP + g, :, row] = symbol(k)
    return along_x, along_y, along_z


@functools.cache
def constants():
    x_forward, x_inverse = x_tables()
    z_pairs = [z_tables(first) for first in (False, True)]
    y_pairs = [y_outer_tables(corner) for corner in (False, True)]
    inner_forward, inner_inverse = y_inner_tables()
    along_x, along_y, along_z = symbol_tables()
    return dict(
        wx=split_const(x_forward, 1),
        wxi=split_const(x_inverse, 0),
        wz=np.stack([split_const(pair[0], 1) for pair in z_pairs]),
        wzi=np.stack([split_const(pair[1], 1) for pair in z_pairs]),
        wy=np.stack([split_const(pair[0], 1) for pair in y_pairs]),
        wyi=np.stack([split_const(pair[1], 1) for pair in y_pairs]),
        wl=split_const(inner_forward, 0),
        wli=split_const(inner_inverse, 0),
        we=y_edge_tables()[0],
        wei=y_edge_tables()[1],
        tw=twiddle_tables(),
        dx=along_x,
        dy=along_y,
        dz=along_z,
    )


CONSTANTS = ("wx", "wxi", "wz", "wzi", "wy", "wyi", "wl", "wli", "we", "wei", "tw", "dx", "dy", "dz")


def thirds(value, axis):
    high = value.astype(BF16)
    low = (value - high.astype(F32)).astype(BF16)
    return jnp.concatenate([high, low, high], axis=axis)


def dot(left, right, contract):
    return lax.dot_general(left, right, (contract, ((), ())), preferred_element_type=F32)


def lanes(shape):
    return lax.broadcasted_iota(jnp.int32, shape, len(shape) - 1)


def sublanes(shape):
    return lax.broadcasted_iota(jnp.int32, shape, len(shape) - 2)


def force_lines(take):
    edge = sublanes((16, N)) == 0

    def along_x(part, z2):
        value = take(part, z2)
        return jnp.roll(value, 1, axis=1) - value

    def along_y(part, z2):
        value = take(part, z2)
        return jnp.where(edge, 0.0, jnp.roll(value, 1, axis=0)) - value

    def along_z(part, z2):
        return take(part, 0) - take(part, 1) if z2 == 1 else -take(part, 0)

    lines = []
    for z2 in range(2):
        lines += [
            along_x(0, z2) + ROOT_HALF * (along_z(4, z2) + along_y(5, z2)),
            along_y(1, z2) + ROOT_HALF * (along_z(3, z2) + along_x(5, z2)),
            along_z(2, z2) + ROOT_HALF * (along_y(3, z2) + along_x(4, z2)),
            -(along_x(6, z2) + along_y(7, z2) + along_z(8, z2)),
        ]
    lines += [ROOT_HALF * take(4, 1), ROOT_HALF * take(3, 1), take(2, 1), -take(8, 1)]
    for z2 in range(2):
        for scale, part in ((ROOT_HALF, 5), (1.0, 1), (ROOT_HALF, 3), (-1.0, 7)):
            lines.append(jnp.broadcast_to(scale * take(part, z2)[15:16], (8, N)))
    return jnp.concatenate(lines, axis=0)


def x_forward(lines, wx):
    return dot(wx, thirds(lines, 1), ((1,), (1,)))


def x_inverse(rows, wxi):
    return dot(thirds(rows.T, 1), wxi, ((1,), (0,)))


def z_forward(rows, wz):
    lane = lanes((N, N))
    low = lane < 64
    main, rest = rows[:, :N], rows[:, N:]
    parts = jnp.concatenate(
        [
            jnp.where(low, main, rest),
            jnp.where(low, jnp.roll(main, 64, axis=1), jnp.roll(rest, 96, axis=1)),
            jnp.where(low, rest, 0.0),
        ],
        axis=0,
    )
    both = dot(wz, thirds(parts, 0), ((1,), (0,)))
    first, second = both[:N], both[N:]
    edge = jnp.where(lane < 96, first, jnp.roll(second, 32, axis=1))
    edge = jnp.where((lane % 8 == sublanes((N, N)) % 8) & (lane >= 64), edge, 0.0)
    return jnp.where(low, first, jnp.roll(second, 64, axis=1)), edge.reshape(16, 8, N).sum(axis=1)


def z_inverse(rows, edge, wzi):
    lane = lanes((N, N))
    low = lane < 64
    edge = jnp.broadcast_to(edge[:, None, :], (16, 8, N)).reshape(N, N)
    edge = jnp.where(lane % 8 == sublanes((N, N)) % 8, edge, 0.0)
    parts = jnp.concatenate(
        [jnp.where(low, rows, edge), jnp.where(low, jnp.roll(rows, 64, axis=1), jnp.roll(edge, 96, axis=1))], axis=0
    )
    planes = dot(wzi, thirds(parts, 0), ((1,), (0,)))
    first, second, third = planes[:N], planes[N : 2 * N], planes[2 * N :]
    main = jnp.where(low, first, jnp.roll(second, 64, axis=1))
    rest = jnp.where(low, third, jnp.where(lane < 96, first, jnp.roll(second, 32, axis=1)))
    return jnp.concatenate([main, rest], axis=1)


def exact_dot(left, right):
    return lax.dot_general(
        left, right, (((1,), (0,)), ((), ())), precision=lax.Precision.HIGHEST, preferred_element_type=F32
    )


def y_forward(rows, edge, corner, wy, wl, we, tw):
    outer = dot(wy, thirds(rows, 0), ((1,), (0,)))
    real, imag = outer[:72], outer[72:]
    turns = exact_dot(we, edge)
    lane = lanes((8, N))
    packed = (lane % 8 == 0) & (corner == 1)
    edge_real = turns[:8] + jnp.where(packed, 0.0, turns[24:])
    edge_imag = jnp.where(packed, 0.0, turns[16:24]) - turns[8:16]
    mixed = jnp.where(lane < 64, jnp.roll(edge_imag, 64, axis=1), edge_real)
    extra = jnp.where(packed, jnp.where(lane < 64, -jnp.roll(turns[24:], 64, axis=1), turns[16:24]), 0.0)
    spread = jnp.broadcast_to(mixed[:, None, :], (8, 8, N)).reshape(64, N)
    spread = jnp.where(lanes((64, N)) % 8 == sublanes((64, N)) % 8, spread, 0.0)
    turned = jnp.concatenate(
        [real * tw[0] + imag * tw[1], imag * tw[0] - real * tw[1], jnp.concatenate([spread, extra], axis=0)], axis=1
    )
    inner = dot(thirds(turned, 1), wl, ((1,), (0,)))
    return inner[:, :N], inner[:, N:]


def y_inverse(real, imag, corner, wyi, wli, wei, tw):
    inner = dot(thirds(jnp.concatenate([real, imag], axis=1), 1), wli, ((1,), (0,)))
    real, imag, mixed = inner[:, :N], inner[:, N : 2 * N], inner[:, 2 * N :]
    turned = jnp.concatenate([real * tw[0] - imag * tw[1], imag * tw[0] + real * tw[1]], axis=0)
    rows = dot(wyi, thirds(turned, 0), ((1,), (0,)))
    lane = lanes((8, N))
    packed = (lane % 8 == 0) & (corner == 1)
    spread = jnp.where(lanes((64, N)) % 8 == sublanes((64, N)) % 8, mixed[:64], 0.0)
    turns = exact_dot(wei, jnp.concatenate([spread.reshape(8, 8, N).sum(axis=1), mixed[64:]], axis=1))
    edge_real = turns[:8, :N] - jnp.roll(turns[8:, :N], 64, axis=1)
    edge_imag = turns[8:, :N] + jnp.roll(turns[:8, :N], 64, axis=1)
    extra = turns[:8, N:] - jnp.roll(turns[8:, N:], 64, axis=1)
    return rows, edge_real, jnp.where(packed, extra, edge_imag)


def gradients(lines):
    last = sublanes((16, N)) == 15
    grad_x, grad_y, grad_z = [], [], []
    for c in range(4):
        along = [[], [], []]
        for z2 in range(2):
            start = z2 * 64 + c * 16
            value = lines[start : start + 16]
            above = lines[start + 64 : start + 80]
            begin = 192 + z2 * 32 + c * 8
            edge = jnp.sum(lines[begin : begin + 8], axis=0, keepdims=True)
            along[0].append(jnp.roll(value, N - 1, axis=1) - value)
            along[1].append(jnp.where(last, edge, jnp.roll(value, 15, axis=0)) - value)
            along[2].append(above - value)
        for grad, pair in zip((grad_x, grad_y, grad_z), along):
            grad.append(jnp.concatenate(pair, axis=0))
    return [
        grad_x[0],
        grad_y[1],
        grad_z[2],
        ROOT_HALF * (grad_y[2] + grad_z[1]),
        ROOT_HALF * (grad_x[2] + grad_z[0]),
        ROOT_HALF * (grad_x[1] + grad_y[0]),
        -grad_x[3],
        -grad_y[3],
        -grad_z[3],
    ]


def operator_tables(dx, dy, dz):
    def rows(main, extra):
        return jnp.concatenate([main] * 8 + [extra], axis=0)

    along_x = [rows(dx[i], dx[i]) for i in range(2)]
    along_z = [rows(dz[i][:8], dz[i][8:]) for i in range(2)]
    along_y = [dy[0], dy[1]]
    squares = (
        along_x[0] * along_x[0]
        + along_x[1] * along_x[1]
        + (along_y[0] * along_y[0] + along_y[1] * along_y[1])
        + (along_z[0] * along_z[0] + along_z[1] * along_z[1])
    )
    some = squares > 0.0
    inverse = jnp.where(some, 1.0 / jnp.where(some, squares, 1.0), 0.0)
    part = lanes(squares.shape) // 16 % 4
    own = [
        jnp.where(part == 0, along_x[i], jnp.where(part == 1, along_y[i], jnp.where(part == 2, along_z[i], 0.0)))
        for i in range(2)
    ]
    scale = 1.0 / (N * N * N)
    alpha = inverse * jnp.where(part == 3, scale / 0.8, scale / 1.5)
    beta = inverse * inverse * (scale / 3.0)
    return own[0], own[1], alpha, beta


def operator(real, imag, own_real, own_imag, alpha, beta):
    projected = []
    lane = lanes(real.shape)
    for value in (own_real * real + own_imag * imag, own_real * imag - own_imag * real):
        for width in (32, 16):
            lower = lane % (2 * width) < width
            value = value + jnp.where(lower, jnp.roll(value, N - width, axis=1), jnp.roll(value, width, axis=1))
        projected.append(value * beta)
    return (
        real * alpha - (own_real * projected[0] - own_imag * projected[1]),
        imag * alpha - (own_real * projected[1] + own_imag * projected[0]),
    )


def kernel(adjoint, source, contrast_in, phase_in, grain_in, orientation_in, *rest):
    tables = dict(zip(CONSTANTS, rest[: len(CONSTANTS)]))
    (
        out,
        wx, wxi, wz, wzi, wy, wyi, wl, wli, we, wei, tw, dx, dy, dz,
        fields, right_side, contrast, phase, grain, orientation,
        send1, recv1, send2, recv2, send3, recv3, send4, recv4,
        coef, own_real, own_imag, alpha, beta,
        load_sems, send_sems, recv_sems,
    ) = rest[len(CONSTANTS):]
    g = lax.axis_index("grp")
    s = lax.axis_index("slab")
    first = jnp.where(s == 0, 1, 0)
    corner = jnp.where((s == 0) & (g == 0), 1, 0)

    pairs = [
        (adjoint, fields),
        (tables["wx"], wx),
        (orientation_in, orientation),
        (grain_in, grain),
        (phase_in, phase),
        (contrast_in, contrast),
        (tables["wz"].at[first], wz),
        (tables["dx"].at[s], dx),
        (tables["dy"], dy),
        (tables["dz"].at[first * GRP + g], dz),
        (tables["wy"].at[corner], wy),
        (tables["wl"], wl),
        (tables["we"], we),
        (tables["tw"], tw),
        (tables["wli"], wli),
        (tables["wyi"].at[corner], wyi),
        (tables["wei"], wei),
        (tables["wzi"].at[first], wzi),
        (tables["wxi"], wxi),
        (source, right_side),
    ]
    loads = [pltpu.make_async_copy(*pair, load_sems.at[i]) for i, pair in enumerate(pairs)]
    for load in loads:
        load.start()

    digit_y, digit_z, digit_x = s // 16, lax.rem(s // 4, 4), lax.rem(s, 4)

    def slab_peers(visit):
        for step_z in (2, 1, 3, 0):
            base = lax.rem(digit_z + step_z, 4) * 4

            def row(step_y, carry):
                start = lax.rem(digit_y + step_y, 4) * 16 + base
                for step_x in range(4):
                    visit(start + lax.rem(digit_x + step_x, 4))
                return carry

            if step_z == 0:
                for step_x in range(1, 4):
                    visit(digit_y * 16 + base + lax.rem(digit_x + step_x, 4))
            lax.fori_loop(1 if step_z == 0 else 0, 4, row, 0)

    def grp_peers(visit):
        def one(step, carry):
            visit(lax.rem(g + step, GRP))
            return carry

        lax.fori_loop(1, GRP, one, 0)

    barrier = pltpu.get_barrier_semaphore()
    slab_peers(lambda peer: pl.semaphore_signal(barrier, inc=1, device_id={"slab": peer}, device_id_type=MESH))
    grp_peers(lambda peer: pl.semaphore_signal(barrier, inc=1, device_id={"grp": peer}, device_id_type=MESH))

    def exchange_slab(sent, landed, which):
        def start(peer):
            pltpu.make_async_remote_copy(
                sent.at[peer], landed.at[s], send_sems.at[which], recv_sems.at[which],
                device_id={"slab": peer}, device_id_type=MESH,
            ).start()

        slab_peers(start)
        landed[s] = sent[s]

    def exchange_grp(sent, landed, which):
        def start(peer):
            pltpu.make_async_remote_copy(
                sent.at[peer], landed.at[g], send_sems.at[which], recv_sems.at[which],
                device_id={"grp": peer}, device_id_type=MESH,
            ).start()

        grp_peers(start)
        landed[g] = sent[g]

    def arrived(landed, which, count):
        block = landed.at[pl.ds(0, count)]
        pltpu.make_async_copy(block, block, recv_sems.at[which]).wait()

    def gone(sent, which, count):
        block = sent.at[pl.ds(0, count)]
        pltpu.make_async_copy(block, block, send_sems.at[which]).wait()

    loads[0].wait()
    lines = force_lines(lambda part, z2: fields[part, pl.ds(z2, 16, stride=2), :])
    loads[1].wait()
    send1[...] = x_forward(lines, wx[...]).reshape(SLAB, 2, 2 * N)
    pl.semaphore_wait(barrier, SLAB - 1 + GRP - 1)
    exchange_slab(send1, recv1, 0)

    for load in loads[2:6]:
        load.wait()
    ids = jnp.concatenate([grain[pl.ds(z2, 16, stride=2), :] for z2 in range(2)], axis=0)
    high, low = ids // N, ids % N
    entry = jnp.zeros((32, N), jnp.int32)
    for row in range(32):
        line = jnp.broadcast_to(orientation[row : row + 1, :], (32, N))
        entry = jnp.where(high == row, jnp.take_along_axis(line, low, axis=1), entry)
    ceramic = jnp.concatenate([phase[pl.ds(z2, 16, stride=2), :] for z2 in range(2)], axis=0) == 1
    entry = jnp.where(ceramic, entry, 6)
    masks = [entry == t for t in range(6)]
    for pair in range(81):
        value = jnp.full((32, N), contrast[pair // 9, 6, pair % 9], F32)
        for t in range(6):
            value = jnp.where(masks[t], contrast[pair // 9, t, pair % 9], value)
        coef[pair] = value
    for load in loads[6:]:
        load.wait()
    own_real[...], own_imag[...], alpha[...], beta[...] = operator_tables(dx, dy, dz)

    arrived(recv1, 0, SLAB - 1)
    rows, edge = z_forward(recv1[...].reshape(N, 2 * N), wz[...])
    send2[:, 0:16, :] = rows.reshape(GRP, 16, N)
    send2[:, 16:18, :] = edge.reshape(GRP, 2, N)
    exchange_grp(send2, recv2, 1)

    arrived(recv2, 1, GRP - 1)
    real, imag = y_forward(
        recv2[:, 0:16, :].reshape(N, N), recv2[:, 16:18, :].reshape(16, N), corner, wy[...], wl[...], we[...], tw
    )
    real, imag = operator(real, imag, own_real[...], own_imag[...], alpha[...], beta[...])
    rows, edge_real, edge_imag = y_inverse(real, imag, corner, wyi[...], wli[...], wei[...], tw)
    send3[:, 0:16, :] = rows.reshape(GRP, 16, N)
    send3[:, 16:17, :] = edge_real.reshape(GRP, 1, N)
    send3[:, 17:18, :] = edge_imag.reshape(GRP, 1, N)
    exchange_grp(send3, recv3, 2)

    arrived(recv3, 2, GRP - 1)
    send4[...] = z_inverse(
        recv3[:, 0:16, :].reshape(N, N), recv3[:, 16:18, :].reshape(16, N), wzi[...]
    ).reshape(SLAB, 2, 2 * N)
    exchange_slab(send4, recv4, 3)

    arrived(recv4, 3, SLAB - 1)
    green = gradients(x_inverse(recv4[...].reshape(N, 2 * N), wxi[...]))
    for i in range(9):
        total = jnp.concatenate([right_side[i, pl.ds(z2, 16, stride=2), :] for z2 in range(2)], axis=0)
        for j in range(9):
            total = total - coef[j * 9 + i] * green[j]
        for z2 in range(2):
            out[i, pl.ds(z2, 16, stride=2), :] = total[z2 * 16 : z2 * 16 + 16]

    gone(send1, 0, SLAB - 1)
    gone(send2, 1, GRP - 1)
    gone(send3, 2, GRP - 1)
    gone(send4, 3, SLAB - 1)


def per_device(adjoint, source, contrast, phase_id, grain_id, orientation):
    table = constants()
    vmem = pl.BlockSpec(memory_space=pltpu.VMEM)
    hbm = pl.BlockSpec(memory_space=pltpu.HBM)
    flat = (9, 32, N)
    result = pl.pallas_call(
        kernel,
        out_shape=jax.ShapeDtypeStruct(flat, F32),
        in_specs=[hbm] * (6 + len(CONSTANTS)),
        out_specs=vmem,
        scratch_shapes=[
            pltpu.VMEM((128, 384), BF16),
            pltpu.VMEM((384, 128), BF16),
            pltpu.VMEM((256, 1152), BF16),
            pltpu.VMEM((384, 768), BF16),
            pltpu.VMEM((144, 384), BF16),
            pltpu.VMEM((128, 432), BF16),
            pltpu.VMEM((1152, 256), BF16),
            pltpu.VMEM((768, 384), BF16),
            pltpu.VMEM((32, 16), F32),
            pltpu.VMEM((16, 8), F32),
            pltpu.VMEM((2, 72, N), F32),
            pltpu.VMEM((2, 8, N), F32),
            pltpu.VMEM((2, 72, N), F32),
            pltpu.VMEM((2, 16, N), F32),
            pltpu.VMEM(flat, F32),
            pltpu.VMEM(flat, F32),
            pltpu.SMEM((9, 7, 9), F32),
            pltpu.VMEM((32, N), jnp.int32),
            pltpu.VMEM((32, N), jnp.int32),
            pltpu.VMEM((32, N), jnp.int32),
            pltpu.VMEM((SLAB, 2, 2 * N), F32),
            pltpu.VMEM((SLAB, 2, 2 * N), F32),
            pltpu.VMEM((GRP, 24, N), F32),
            pltpu.VMEM((GRP, 24, N), F32),
            pltpu.VMEM((GRP, 24, N), F32),
            pltpu.VMEM((GRP, 24, N), F32),
            pltpu.VMEM((SLAB, 2, 2 * N), F32),
            pltpu.VMEM((SLAB, 2, 2 * N), F32),
            pltpu.VMEM((81, 32, N), F32),
            pltpu.VMEM((72, N), F32),
            pltpu.VMEM((72, N), F32),
            pltpu.VMEM((72, N), F32),
            pltpu.VMEM((72, N), F32),
            pltpu.SemaphoreType.DMA((20,)),
            pltpu.SemaphoreType.DMA((4,)),
            pltpu.SemaphoreType.DMA((4,)),
        ],
        compiler_params=pltpu.CompilerParams(
            collective_id=0, has_side_effects=True, vmem_limit_bytes=60 * 1024 * 1024
        ),
    )(
        adjoint.reshape(flat),
        source.reshape(flat),
        contrast.transpose(1, 0, 2),
        phase_id.reshape(32, N),
        grain_id.reshape(32, N),
        orientation.reshape(32, N),
        *[jnp.asarray(table[name]) for name in CONSTANTS],
    )
    return result.reshape(adjoint.shape)


def solution(mesh):
    placed = (
        P(None, "grp", "slab", None),
        P(None, "grp", "slab", None),
        P(),
        P("grp", "slab", None),
        P("grp", "slab", None),
        P(),
    )
    return jax.shard_map(
        per_device,
        mesh=mesh,
        in_specs=placed,
        out_specs=P(None, "grp", "slab", None),
        check_vma=False,
    )
```

```python
import functools

import jax
import jax.numpy as jnp
import ml_dtypes
import numpy as np
from jax import lax
from jax.experimental import pallas as pl
from jax.experimental.pallas import tpu as pltpu
from jax.sharding import PartitionSpec as P

N = 128
GRP = 8
SLAB = 64
F32 = jnp.float32
BF16 = jnp.bfloat16
ROOT_HALF = float(np.sqrt(0.5))
MESH = pl.DeviceIdType.MESH


def split_const(matrix, axis):
    high = matrix.astype(ml_dtypes.bfloat16)
    low = (matrix - high.astype(np.float64)).astype(ml_dtypes.bfloat16)
    return np.concatenate([high, high, low], axis=axis)


def angle(a, b, length=N):
    return 2.0 * np.pi * ((np.asarray(a) * np.asarray(b)) % length) / length


def x_tables():
    x = np.arange(N)
    forward = np.zeros((SLAB, 2, N))
    inverse = np.zeros((SLAB, 2, N))
    for k in range(1, SLAB):
        forward[k, 0] = np.cos(angle(k, x))
        forward[k, 1] = -np.sin(angle(k, x))
    forward[0, 0] = 1.0
    forward[0, 1] = (-1.0) ** x
    inverse[1:] = 2.0 * forward[1:]
    inverse[0] = forward[0]
    return forward.reshape(N, N), inverse.reshape(N, N)


def z_tables(first):
    z = (2 * np.arange(SLAB)[:, None] + np.arange(3)[None, :]) % N
    forward = np.zeros((2, GRP, 2, 8, 3, SLAB, 2))
    inverse = np.zeros((3, SLAB, 2, 2, GRP, 2, 8))
    for m in range(SLAB):
        hi, lo = divmod(m, 8)
        for h in range(2):
            for z2 in range(3):
                if first:
                    cos, sin = np.cos(angle(m, z[:, z2])), np.sin(angle(m, z[:, z2]))
                    if m == 0:
                        alt = (-1.0) ** z[:, z2]
                        forward[h, hi, 0, lo, z2, :, h] = 1.0
                        forward[h, hi, 1, lo, z2, :, h] = alt
                        inverse[z2, :, h, h, hi, 0, lo] = 1.0
                        inverse[z2, :, h, h, hi, 1, lo] = alt
                    else:
                        forward[h, hi, 0, lo, z2, :, h] = cos
                        forward[h, hi, 1, lo, z2, :, h] = -sin
                        inverse[z2, :, h, h, hi, 0, lo] = 2.0 * cos
                        inverse[z2, :, h, h, hi, 1, lo] = -2.0 * sin
                else:
                    k = m if h == 0 else (64 if m == 0 else N - m)
                    cos, sin = np.cos(angle(k, z[:, z2])), np.sin(angle(k, z[:, z2]))
                    forward[h, hi, 0, lo, z2, :, 0] = cos
                    forward[h, hi, 0, lo, z2, :, 1] = sin
                    forward[h, hi, 1, lo, z2, :, 0] = -sin
                    forward[h, hi, 1, lo, z2, :, 1] = cos
                    inverse[z2, :, 0, h, hi, 0, lo] = cos
                    inverse[z2, :, 0, h, hi, 1, lo] = -sin
                    inverse[z2, :, 1, h, hi, 0, lo] = sin
                    inverse[z2, :, 1, h, hi, 1, lo] = cos
    return forward.reshape(256, 384), inverse.reshape(384, 256)


def y_outer_tables(corner):
    forward = np.zeros((2, 72, GRP, 2, 8))
    inverse = np.zeros((GRP, 2, 8, 2, 72))
    g = np.arange(GRP)
    for k1 in range(8):
        cos, sin = np.cos(angle(k1, g, 8)), np.sin(angle(k1, g, 8))
        for kz in range(8):
            row = k1 * 8 + kz
            if corner and kz == 0:
                for source, target in ((0, row), (1, 64 + k1)):
                    forward[0, target, :, source, kz] = cos
                    forward[1, target, :, source, kz] = -sin
                    inverse[:, source, kz, 0, target] = cos
                    inverse[:, source, kz, 1, target] = -sin
            else:
                forward[0, row, :, 0, kz] = cos
                forward[0, row, :, 1, kz] = sin
                forward[1, row, :, 0, kz] = -sin
                forward[1, row, :, 1, kz] = cos
                inverse[:, 0, kz, 0, row] = cos
                inverse[:, 0, kz, 1, row] = -sin
                inverse[:, 1, kz, 0, row] = sin
                inverse[:, 1, kz, 1, row] = cos
    return forward.reshape(144, 128), inverse.reshape(128, 144)


def y_edge_tables():
    turn = angle(np.arange(8)[:, None], np.arange(8)[None, :] + 1, 8)
    forward = np.zeros((2, 2, 8, 8, 2))
    for ri in range(2):
        forward[ri, 0, :, :, ri] = np.cos(turn)
        forward[ri, 1, :, :, ri] = np.sin(turn)
    inverse = np.concatenate([np.cos(turn).T, np.sin(turn).T])
    return forward.reshape(32, 16).astype(np.float32), inverse.astype(np.float32)


def lane_parts():
    lane = np.arange(N)
    return lane // 16 % 4, lane % 16, lane // 64


def edge_parts():
    lane = np.arange(N)
    return lane // 8 % 4, lane // 32 % 2, lane // 64


def y_inner_tables():
    c, y, h = lane_parts()
    same = (c[:, None] == c[None, :]) & (h[:, None] == h[None, :])
    cos = np.where(same, np.cos(angle(y[:, None], y[None, :], 16)), 0.0)
    sin = np.where(same, np.sin(angle(y[:, None], y[None, :], 16)), 0.0)
    edge_c, edge_h, edge_real = edge_parts()
    meet = (edge_c[:, None] == c[None, :]) & (edge_h[:, None] == h[None, :])
    to_real = (meet & (edge_real[:, None] == 1)).astype(np.float64)
    to_imag = (meet & (edge_real[:, None] == 0)).astype(np.float64)
    forward = np.block([[cos, -sin], [sin, cos], [to_real, to_imag]])
    inverse = np.block([[cos, sin, to_real.T], [-sin, cos, to_imag.T]])
    return forward, inverse


def row_k1():
    return np.concatenate([np.repeat(np.arange(8), 8), np.arange(8)])


def twiddle_tables():
    _, y, _ = lane_parts()
    turn = angle(row_k1()[:, None], y[None, :])
    return np.stack([np.cos(turn), np.sin(turn)]).astype(np.float32)


def symbol(k):
    turn = 2.0 * np.pi * (np.asarray(k) % N) / N
    return np.stack([np.cos(turn) - 1.0, np.sin(turn)]).astype(np.float32)


def symbol_tables():
    _, k2, h = lane_parts()
    along_y = symbol(row_k1()[:, None] + 8 * k2[None, :])
    along_x = np.zeros((SLAB, 2, 8, N), np.float32)
    for s in range(SLAB):
        k = np.where(h == 0, 0, 64) if s == 0 else np.full(N, s)
        along_x[s] = np.broadcast_to(symbol(k)[:, None, :], (2, 8, N))
    along_z = np.zeros((2 * GRP, 2, 16, N), np.float32)
    for first in range(2):
        for g in range(GRP):
            for row in range(16):
                m = g * 8 + row
                if row >= 8:
                    k = np.full(N, 64)
                elif first:
                    k = np.full(N, m)
                else:
                    k = np.where(h == 0, m, 64 if m == 0 else N - m)
                along_z[first * GRP + g, :, row] = symbol(k)
    return along_x, along_y, along_z


@functools.cache
def constants():
    x_forward, x_inverse = x_tables()
    z_pairs = [z_tables(first) for first in (False, True)]
    y_pairs = [y_outer_tables(corner) for corner in (False, True)]
    inner_forward, inner_inverse = y_inner_tables()
    along_x, along_y, along_z = symbol_tables()
    return dict(
        wx=split_const(x_forward, 1),
        wxi=split_const(x_inverse, 0),
        wz=np.stack([split_const(pair[0], 1) for pair in z_pairs]),
        wzi=np.stack([split_const(pair[1], 1) for pair in z_pairs]),
        wy=np.stack([split_const(pair[0], 1) for pair in y_pairs]),
        wyi=np.stack([split_const(pair[1], 1) for pair in y_pairs]),
        wl=split_const(inner_forward, 0),
        wli=split_const(inner_inverse, 0),
        we=y_edge_tables()[0],
        wei=y_edge_tables()[1],
        tw=twiddle_tables(),
        dx=along_x,
        dy=along_y,
        dz=along_z,
    )


CONSTANTS = ("wx", "wxi", "wz", "wzi", "wy", "wyi", "wl", "wli", "we", "wei", "tw", "dx", "dy", "dz")


def thirds(value, axis):
    high = value.astype(BF16)
    low = (value - high.astype(F32)).astype(BF16)
    return jnp.concatenate([high, low, high], axis=axis)


def dot(left, right, contract):
    return lax.dot_general(left, right, (contract, ((), ())), preferred_element_type=F32)


def lanes(shape):
    return lax.broadcasted_iota(jnp.int32, shape, len(shape) - 1)


def sublanes(shape):
    return lax.broadcasted_iota(jnp.int32, shape, len(shape) - 2)


def force_lines(take):
    edge = sublanes((16, N)) == 0

    def along_x(part, z2):
        value = take(part, z2)
        return jnp.roll(value, 1, axis=1) - value

    def along_y(part, z2):
        value = take(part, z2)
        return jnp.where(edge, 0.0, jnp.roll(value, 1, axis=0)) - value

    def along_z(part, z2):
        return take(part, 0) - take(part, 1) if z2 == 1 else -take(part, 0)

    lines = []
    for z2 in range(2):
        lines += [
            along_x(0, z2) + ROOT_HALF * (along_z(4, z2) + along_y(5, z2)),
            along_y(1, z2) + ROOT_HALF * (along_z(3, z2) + along_x(5, z2)),
            along_z(2, z2) + ROOT_HALF * (along_y(3, z2) + along_x(4, z2)),
            -(along_x(6, z2) + along_y(7, z2) + along_z(8, z2)),
        ]
    lines += [ROOT_HALF * take(4, 1), ROOT_HALF * take(3, 1), take(2, 1), -take(8, 1)]
    for z2 in range(2):
        for scale, part in ((ROOT_HALF, 5), (1.0, 1), (ROOT_HALF, 3), (-1.0, 7)):
            lines.append(jnp.broadcast_to(scale * take(part, z2)[15:16], (8, N)))
    return jnp.concatenate(lines, axis=0)


def x_forward(lines, wx):
    return dot(wx, thirds(lines, 1), ((1,), (1,)))


def x_inverse(rows, wxi):
    return dot(thirds(rows.T, 1), wxi, ((1,), (0,)))


def z_forward(rows, wz):
    lane = lanes((N, N))
    low = lane < 64
    main, rest = rows[:, :N], rows[:, N:]
    parts = jnp.concatenate(
        [
            jnp.where(low, main, rest),
            jnp.where(low, jnp.roll(main, 64, axis=1), jnp.roll(rest, 96, axis=1)),
            jnp.where(low, rest, 0.0),
        ],
        axis=0,
    )
    both = dot(wz, thirds(parts, 0), ((1,), (0,)))
    first, second = both[:N], both[N:]
    edge = jnp.where(lane < 96, first, jnp.roll(second, 32, axis=1))
    edge = jnp.where((lane % 8 == sublanes((N, N)) % 8) & (lane >= 64), edge, 0.0)
    return jnp.where(low, first, jnp.roll(second, 64, axis=1)), edge.reshape(16, 8, N).sum(axis=1)


def z_inverse(rows, edge, wzi):
    lane = lanes((N, N))
    low = lane < 64
    edge = jnp.broadcast_to(edge[:, None, :], (16, 8, N)).reshape(N, N)
    edge = jnp.where(lane % 8 == sublanes((N, N)) % 8, edge, 0.0)
    parts = jnp.concatenate(
        [jnp.where(low, rows, edge), jnp.where(low, jnp.roll(rows, 64, axis=1), jnp.roll(edge, 96, axis=1))], axis=0
    )
    planes = dot(wzi, thirds(parts, 0), ((1,), (0,)))
    first, second, third = planes[:N], planes[N : 2 * N], planes[2 * N :]
    main = jnp.where(low, first, jnp.roll(second, 64, axis=1))
    rest = jnp.where(low, third, jnp.where(lane < 96, first, jnp.roll(second, 32, axis=1)))
    return jnp.concatenate([main, rest], axis=1)


def exact_dot(left, right):
    return lax.dot_general(
        left, right, (((1,), (0,)), ((), ())), precision=lax.Precision.HIGHEST, preferred_element_type=F32
    )


def y_forward(rows, edge, corner, wy, wl, we, tw):
    outer = dot(wy, thirds(rows, 0), ((1,), (0,)))
    real, imag = outer[:72], outer[72:]
    turns = exact_dot(we, edge)
    lane = lanes((8, N))
    packed = (lane % 8 == 0) & (corner == 1)
    edge_real = turns[:8] + jnp.where(packed, 0.0, turns[24:])
    edge_imag = jnp.where(packed, 0.0, turns[16:24]) - turns[8:16]
    mixed = jnp.where(lane < 64, jnp.roll(edge_imag, 64, axis=1), edge_real)
    extra = jnp.where(packed, jnp.where(lane < 64, -jnp.roll(turns[24:], 64, axis=1), turns[16:24]), 0.0)
    spread = jnp.broadcast_to(mixed[:, None, :], (8, 8, N)).reshape(64, N)
    spread = jnp.where(lanes((64, N)) % 8 == sublanes((64, N)) % 8, spread, 0.0)
    turned = jnp.concatenate(
        [real * tw[0] + imag * tw[1], imag * tw[0] - real * tw[1], jnp.concatenate([spread, extra], axis=0)], axis=1
    )
    inner = dot(thirds(turned, 1), wl, ((1,), (0,)))
    return inner[:, :N], inner[:, N:]


def y_inverse(real, imag, corner, wyi, wli, wei, tw):
    inner = dot(thirds(jnp.concatenate([real, imag], axis=1), 1), wli, ((1,), (0,)))
    real, imag, mixed = inner[:, :N], inner[:, N : 2 * N], inner[:, 2 * N :]
    turned = jnp.concatenate([real * tw[0] - imag * tw[1], imag * tw[0] + real * tw[1]], axis=0)
    rows = dot(wyi, thirds(turned, 0), ((1,), (0,)))
    lane = lanes((8, N))
    packed = (lane % 8 == 0) & (corner == 1)
    spread = jnp.where(lanes((64, N)) % 8 == sublanes((64, N)) % 8, mixed[:64], 0.0)
    turns = exact_dot(wei, jnp.concatenate([spread.reshape(8, 8, N).sum(axis=1), mixed[64:]], axis=1))
    edge_real = turns[:8, :N] - jnp.roll(turns[8:, :N], 64, axis=1)
    edge_imag = turns[8:, :N] + jnp.roll(turns[:8, :N], 64, axis=1)
    extra = turns[:8, N:] - jnp.roll(turns[8:, N:], 64, axis=1)
    return rows, edge_real, jnp.where(packed, extra, edge_imag)


def gradients(lines):
    last = sublanes((16, N)) == 15
    grad_x, grad_y, grad_z = [], [], []
    for c in range(4):
        along = [[], [], []]
        for z2 in range(2):
            start = z2 * 64 + c * 16
            value = lines[start : start + 16]
            above = lines[start + 64 : start + 80]
            begin = 192 + z2 * 32 + c * 8
            edge = jnp.sum(lines[begin : begin + 8], axis=0, keepdims=True)
            along[0].append(jnp.roll(value, N - 1, axis=1) - value)
            along[1].append(jnp.where(last, edge, jnp.roll(value, 15, axis=0)) - value)
            along[2].append(above - value)
        for grad, pair in zip((grad_x, grad_y, grad_z), along):
            grad.append(jnp.concatenate(pair, axis=0))
    return [
        grad_x[0],
        grad_y[1],
        grad_z[2],
        ROOT_HALF * (grad_y[2] + grad_z[1]),
        ROOT_HALF * (grad_x[2] + grad_z[0]),
        ROOT_HALF * (grad_x[1] + grad_y[0]),
        -grad_x[3],
        -grad_y[3],
        -grad_z[3],
    ]


def operator_tables(dx, dy, dz):
    def rows(main, extra):
        return jnp.concatenate([main] * 8 + [extra], axis=0)

    along_x = [rows(dx[i], dx[i]) for i in range(2)]
    along_z = [rows(dz[i][:8], dz[i][8:]) for i in range(2)]
    along_y = [dy[0], dy[1]]
    squares = (
        along_x[0] * along_x[0]
        + along_x[1] * along_x[1]
        + (along_y[0] * along_y[0] + along_y[1] * along_y[1])
        + (along_z[0] * along_z[0] + along_z[1] * along_z[1])
    )
    some = squares > 0.0
    inverse = jnp.where(some, 1.0 / jnp.where(some, squares, 1.0), 0.0)
    part = lanes(squares.shape) // 16 % 4
    own = [
        jnp.where(part == 0, along_x[i], jnp.where(part == 1, along_y[i], jnp.where(part == 2, along_z[i], 0.0)))
        for i in range(2)
    ]
    scale = 1.0 / (N * N * N)
    alpha = inverse * jnp.where(part == 3, scale / 0.8, scale / 1.5)
    beta = inverse * inverse * (scale / 3.0)
    return own[0], own[1], alpha, beta


def operator(real, imag, own_real, own_imag, alpha, beta):
    projected = []
    lane = lanes(real.shape)
    for value in (own_real * real + own_imag * imag, own_real * imag - own_imag * real):
        for width in (32, 16):
            lower = lane % (2 * width) < width
            value = value + jnp.where(lower, jnp.roll(value, N - width, axis=1), jnp.roll(value, width, axis=1))
        projected.append(value * beta)
    return (
        real * alpha - (own_real * projected[0] - own_imag * projected[1]),
        imag * alpha - (own_real * projected[1] + own_imag * projected[0]),
    )


def kernel(adjoint, source, contrast_in, phase_in, grain_in, orientation_in, *rest):
    tables = dict(zip(CONSTANTS, rest[: len(CONSTANTS)]))
    (
        out,
        wx, wxi, wz, wzi, wy, wyi, wl, wli, we, wei, tw, dx, dy, dz,
        fields, right_side, contrast, phase, grain, orientation,
        send1, recv1, send2, recv2, send3, recv3, send4, recv4,
        coef, own_real, own_imag, alpha, beta,
        load_sems, send_sems, recv_sems,
    ) = rest[len(CONSTANTS):]
    g = lax.axis_index("grp")
    s = lax.axis_index("slab")
    first = jnp.where(s == 0, 1, 0)
    corner = jnp.where((s == 0) & (g == 0), 1, 0)

    pairs = [
        (adjoint, fields),
        (tables["wx"], wx),
        (orientation_in, orientation),
        (grain_in, grain),
        (phase_in, phase),
        (contrast_in, contrast),
        (tables["wz"].at[first], wz),
        (tables["dx"].at[s], dx),
        (tables["dy"], dy),
        (tables["dz"].at[first * GRP + g], dz),
        (tables["wy"].at[corner], wy),
        (tables["wl"], wl),
        (tables["we"], we),
        (tables["tw"], tw),
        (tables["wli"], wli),
        (tables["wyi"].at[corner], wyi),
        (tables["wei"], wei),
        (tables["wzi"].at[first], wzi),
        (tables["wxi"], wxi),
        (source, right_side),
    ]
    loads = [pltpu.make_async_copy(*pair, load_sems.at[i]) for i, pair in enumerate(pairs)]
    for load in loads:
        load.start()

    digit_y, digit_z, digit_x = s // 16, lax.rem(s // 4, 4), lax.rem(s, 4)

    def slab_peers(visit):
        for steps_z in ((2,), (1, 3), (0,)):
            bases = [lax.rem(digit_z + step_z, 4) * 4 for step_z in steps_z]

            def row(step_y, carry):
                start = lax.rem(digit_y + step_y, 4) * 16
                for step_x in range(4):
                    for base in bases:
                        visit(start + base + lax.rem(digit_x + step_x, 4))
                return carry

            if steps_z == (0,):
                for step_x in range(1, 4):
                    visit(digit_y * 16 + bases[0] + lax.rem(digit_x + step_x, 4))
            lax.fori_loop(1 if steps_z == (0,) else 0, 4, row, 0)

    def grp_peers(visit):
        def one(step, carry):
            visit(lax.rem(g + step, GRP))
            return carry

        lax.fori_loop(1, GRP, one, 0)

    barrier = pltpu.get_barrier_semaphore()
    slab_peers(lambda peer: pl.semaphore_signal(barrier, inc=1, device_id={"slab": peer}, device_id_type=MESH))
    grp_peers(lambda peer: pl.semaphore_signal(barrier, inc=1, device_id={"grp": peer}, device_id_type=MESH))

    def exchange_slab(sent, landed, which):
        def start(peer):
            pltpu.make_async_remote_copy(
                sent.at[peer], landed.at[s], send_sems.at[which], recv_sems.at[which],
                device_id={"slab": peer}, device_id_type=MESH,
            ).start()

        slab_peers(start)
        landed[s] = sent[s]

    def exchange_grp(sent, landed, which):
        def start(peer):
            pltpu.make_async_remote_copy(
                sent.at[peer], landed.at[g], send_sems.at[which], recv_sems.at[which],
                device_id={"grp": peer}, device_id_type=MESH,
            ).start()

        grp_peers(start)
        landed[g] = sent[g]

    def arrived(landed, which, count):
        block = landed.at[pl.ds(0, count)]
        pltpu.make_async_copy(block, block, recv_sems.at[which]).wait()

    def gone(sent, which, count):
        block = sent.at[pl.ds(0, count)]
        pltpu.make_async_copy(block, block, send_sems.at[which]).wait()

    loads[0].wait()
    lines = force_lines(lambda part, z2: fields[part, pl.ds(z2, 16, stride=2), :])
    loads[1].wait()
    send1[...] = x_forward(lines, wx[...]).reshape(SLAB, 2, 2 * N)
    pl.semaphore_wait(barrier, SLAB - 1 + GRP - 1)
    exchange_slab(send1, recv1, 0)

    for load in loads[2:6]:
        load.wait()
    ids = jnp.concatenate([grain[pl.ds(z2, 16, stride=2), :] for z2 in range(2)], axis=0)
    high, low = ids // N, ids % N
    entry = jnp.zeros((32, N), jnp.int32)
    for row in range(32):
        line = jnp.broadcast_to(orientation[row : row + 1, :], (32, N))
        entry = jnp.where(high == row, jnp.take_along_axis(line, low, axis=1), entry)
    ceramic = jnp.concatenate([phase[pl.ds(z2, 16, stride=2), :] for z2 in range(2)], axis=0) == 1
    entry = jnp.where(ceramic, entry, 6)
    masks = [entry == t for t in range(6)]
    for pair in range(81):
        value = jnp.full((32, N), contrast[pair // 9, 6, pair % 9], F32)
        for t in range(6):
            value = jnp.where(masks[t], contrast[pair // 9, t, pair % 9], value)
        coef[pair] = value
    for load in loads[6:]:
        load.wait()
    own_real[...], own_imag[...], alpha[...], beta[...] = operator_tables(dx, dy, dz)

    arrived(recv1, 0, SLAB - 1)
    rows, edge = z_forward(recv1[...].reshape(N, 2 * N), wz[...])
    send2[:, 0:16, :] = rows.reshape(GRP, 16, N)
    send2[:, 16:18, :] = edge.reshape(GRP, 2, N)
    exchange_grp(send2, recv2, 1)

    arrived(recv2, 1, GRP - 1)
    real, imag = y_forward(
        recv2[:, 0:16, :].reshape(N, N), recv2[:, 16:18, :].reshape(16, N), corner, wy[...], wl[...], we[...], tw
    )
    real, imag = operator(real, imag, own_real[...], own_imag[...], alpha[...], beta[...])
    rows, edge_real, edge_imag = y_inverse(real, imag, corner, wyi[...], wli[...], wei[...], tw)
    send3[:, 0:16, :] = rows.reshape(GRP, 16, N)
    send3[:, 16:17, :] = edge_real.reshape(GRP, 1, N)
    send3[:, 17:18, :] = edge_imag.reshape(GRP, 1, N)
    exchange_grp(send3, recv3, 2)

    arrived(recv3, 2, GRP - 1)
    send4[...] = z_inverse(
        recv3[:, 0:16, :].reshape(N, N), recv3[:, 16:18, :].reshape(16, N), wzi[...]
    ).reshape(SLAB, 2, 2 * N)
    exchange_slab(send4, recv4, 3)

    arrived(recv4, 3, SLAB - 1)
    green = gradients(x_inverse(recv4[...].reshape(N, 2 * N), wxi[...]))
    for i in range(9):
        total = jnp.concatenate([right_side[i, pl.ds(z2, 16, stride=2), :] for z2 in range(2)], axis=0)
        for j in range(9):
            total = total - coef[j * 9 + i] * green[j]
        for z2 in range(2):
            out[i, pl.ds(z2, 16, stride=2), :] = total[z2 * 16 : z2 * 16 + 16]

    gone(send1, 0, SLAB - 1)
    gone(send2, 1, GRP - 1)
    gone(send3, 2, GRP - 1)
    gone(send4, 3, SLAB - 1)


def per_device(adjoint, source, contrast, phase_id, grain_id, orientation):
    table = constants()
    vmem = pl.BlockSpec(memory_space=pltpu.VMEM)
    hbm = pl.BlockSpec(memory_space=pltpu.HBM)
    flat = (9, 32, N)
    result = pl.pallas_call(
        kernel,
        out_shape=pltpu.VMEM(flat, F32),
        in_specs=[hbm] * (6 + len(CONSTANTS)),
        out_specs=vmem,
        scratch_shapes=[
            pltpu.VMEM((128, 384), BF16),
            pltpu.VMEM((384, 128), BF16),
            pltpu.VMEM((256, 1152), BF16),
            pltpu.VMEM((384, 768), BF16),
            pltpu.VMEM((144, 384), BF16),
            pltpu.VMEM((128, 432), BF16),
            pltpu.VMEM((1152, 256), BF16),
            pltpu.VMEM((768, 384), BF16),
            pltpu.VMEM((32, 16), F32),
            pltpu.VMEM((16, 8), F32),
            pltpu.VMEM((2, 72, N), F32),
            pltpu.VMEM((2, 8, N), F32),
            pltpu.VMEM((2, 72, N), F32),
            pltpu.VMEM((2, 16, N), F32),
            pltpu.VMEM(flat, F32),
            pltpu.VMEM(flat, F32),
            pltpu.SMEM((9, 7, 9), F32),
            pltpu.VMEM((32, N), jnp.int32),
            pltpu.VMEM((32, N), jnp.int32),
            pltpu.VMEM((32, N), jnp.int32),
            pltpu.VMEM((SLAB, 2, 2 * N), F32),
            pltpu.VMEM((SLAB, 2, 2 * N), F32),
            pltpu.VMEM((GRP, 24, N), F32),
            pltpu.VMEM((GRP, 24, N), F32),
            pltpu.VMEM((GRP, 24, N), F32),
            pltpu.VMEM((GRP, 24, N), F32),
            pltpu.VMEM((SLAB, 2, 2 * N), F32),
            pltpu.VMEM((SLAB, 2, 2 * N), F32),
            pltpu.VMEM((81, 32, N), F32),
            pltpu.VMEM((72, N), F32),
            pltpu.VMEM((72, N), F32),
            pltpu.VMEM((72, N), F32),
            pltpu.VMEM((72, N), F32),
            pltpu.SemaphoreType.DMA((20,)),
            pltpu.SemaphoreType.DMA((4,)),
            pltpu.SemaphoreType.DMA((4,)),
        ],
        compiler_params=pltpu.CompilerParams(
            collective_id=0, has_side_effects=True, vmem_limit_bytes=60 * 1024 * 1024
        ),
    )(
        adjoint.reshape(flat),
        source.reshape(flat),
        contrast.transpose(1, 0, 2),
        phase_id.reshape(32, N),
        grain_id.reshape(32, N),
        orientation.reshape(32, N),
        *[jnp.asarray(table[name]) for name in CONSTANTS],
    )
    return result.reshape(adjoint.shape)


def solution(mesh):
    placed = (
        P(None, "grp", "slab", None),
        P(None, "grp", "slab", None),
        P(),
        P("grp", "slab", None),
        P("grp", "slab", None),
        P(),
    )
    return jax.shard_map(
        per_device,
        mesh=mesh,
        in_specs=placed,
        out_specs=P(None, "grp", "slab", None),
        check_vma=False,
    )
```

```python
import functools

import jax
import jax.numpy as jnp
import ml_dtypes
import numpy as np
from jax import lax
from jax.experimental import pallas as pl
from jax.experimental.pallas import tpu as pltpu
from jax.sharding import PartitionSpec as P

N = 128
GRP = 8
SLAB = 64
F32 = jnp.float32
BF16 = jnp.bfloat16
ROOT_HALF = float(np.sqrt(0.5))
MESH = pl.DeviceIdType.MESH
SLOTS = np.arange(SLAB).reshape(4, 4, 4).transpose(1, 0, 2).reshape(SLAB)


def split_const(matrix, axis):
    high = matrix.astype(ml_dtypes.bfloat16)
    low = (matrix - high.astype(np.float64)).astype(ml_dtypes.bfloat16)
    return np.concatenate([high, high, low], axis=axis)


def angle(a, b, length=N):
    return 2.0 * np.pi * ((np.asarray(a) * np.asarray(b)) % length) / length


def x_tables():
    x = np.arange(N)
    forward = np.zeros((SLAB, 2, N))
    inverse = np.zeros((SLAB, 2, N))
    for k in range(1, SLAB):
        forward[k, 0] = np.cos(angle(k, x))
        forward[k, 1] = -np.sin(angle(k, x))
    forward[0, 0] = 1.0
    forward[0, 1] = (-1.0) ** x
    inverse[1:] = 2.0 * forward[1:]
    inverse[0] = forward[0]
    return forward[SLOTS].reshape(N, N), inverse[SLOTS].reshape(N, N)


def z_tables(first):
    z = (2 * np.arange(SLAB)[:, None] + np.arange(3)[None, :]) % N
    forward = np.zeros((2, GRP, 2, 8, 3, SLAB, 2))
    inverse = np.zeros((3, SLAB, 2, 2, GRP, 2, 8))
    for m in range(SLAB):
        hi, lo = divmod(m, 8)
        for h in range(2):
            for z2 in range(3):
                if first:
                    cos, sin = np.cos(angle(m, z[:, z2])), np.sin(angle(m, z[:, z2]))
                    if m == 0:
                        alt = (-1.0) ** z[:, z2]
                        forward[h, hi, 0, lo, z2, :, h] = 1.0
                        forward[h, hi, 1, lo, z2, :, h] = alt
                        inverse[z2, :, h, h, hi, 0, lo] = 1.0
                        inverse[z2, :, h, h, hi, 1, lo] = alt
                    else:
                        forward[h, hi, 0, lo, z2, :, h] = cos
                        forward[h, hi, 1, lo, z2, :, h] = -sin
                        inverse[z2, :, h, h, hi, 0, lo] = 2.0 * cos
                        inverse[z2, :, h, h, hi, 1, lo] = -2.0 * sin
                else:
                    k = m if h == 0 else (64 if m == 0 else N - m)
                    cos, sin = np.cos(angle(k, z[:, z2])), np.sin(angle(k, z[:, z2]))
                    forward[h, hi, 0, lo, z2, :, 0] = cos
                    forward[h, hi, 0, lo, z2, :, 1] = sin
                    forward[h, hi, 1, lo, z2, :, 0] = -sin
                    forward[h, hi, 1, lo, z2, :, 1] = cos
                    inverse[z2, :, 0, h, hi, 0, lo] = cos
                    inverse[z2, :, 0, h, hi, 1, lo] = -sin
                    inverse[z2, :, 1, h, hi, 0, lo] = sin
                    inverse[z2, :, 1, h, hi, 1, lo] = cos
    forward = forward[..., SLOTS, :].reshape(256, 3, 4, 32).transpose(2, 0, 1, 3).reshape(4, 256, 96)
    inverse = inverse[:, SLOTS].reshape(3, 4, 32, 256).transpose(1, 0, 2, 3).reshape(4, 96, 256)
    return forward, inverse


def y_outer_tables(corner):
    forward = np.zeros((2, 72, GRP, 2, 8))
    inverse = np.zeros((GRP, 2, 8, 2, 72))
    g = np.arange(GRP)
    for k1 in range(8):
        cos, sin = np.cos(angle(k1, g, 8)), np.sin(angle(k1, g, 8))
        for kz in range(8):
            row = k1 * 8 + kz
            if corner and kz == 0:
                for source, target in ((0, row), (1, 64 + k1)):
                    forward[0, target, :, source, kz] = cos
                    forward[1, target, :, source, kz] = -sin
                    inverse[:, source, kz, 0, target] = cos
                    inverse[:, source, kz, 1, target] = -sin
            else:
                forward[0, row, :, 0, kz] = cos
                forward[0, row, :, 1, kz] = sin
                forward[1, row, :, 0, kz] = -sin
                forward[1, row, :, 1, kz] = cos
                inverse[:, 0, kz, 0, row] = cos
                inverse[:, 0, kz, 1, row] = -sin
                inverse[:, 1, kz, 0, row] = sin
                inverse[:, 1, kz, 1, row] = cos
    return forward.reshape(144, 128), inverse.reshape(128, 144)


def y_edge_tables():
    turn = angle(np.arange(8)[:, None], np.arange(8)[None, :] + 1, 8)
    forward = np.zeros((2, 2, 8, 8, 2))
    for ri in range(2):
        forward[ri, 0, :, :, ri] = np.cos(turn)
        forward[ri, 1, :, :, ri] = np.sin(turn)
    inverse = np.concatenate([np.cos(turn).T, np.sin(turn).T])
    return forward.reshape(32, 16).astype(np.float32), inverse.astype(np.float32)


def lane_parts():
    lane = np.arange(N)
    return lane // 16 % 4, lane % 16, lane // 64


def edge_parts():
    lane = np.arange(N)
    return lane // 8 % 4, lane // 32 % 2, lane // 64


def y_inner_tables():
    c, y, h = lane_parts()
    same = (c[:, None] == c[None, :]) & (h[:, None] == h[None, :])
    cos = np.where(same, np.cos(angle(y[:, None], y[None, :], 16)), 0.0)
    sin = np.where(same, np.sin(angle(y[:, None], y[None, :], 16)), 0.0)
    edge_c, edge_h, edge_real = edge_parts()
    meet = (edge_c[:, None] == c[None, :]) & (edge_h[:, None] == h[None, :])
    to_real = (meet & (edge_real[:, None] == 1)).astype(np.float64)
    to_imag = (meet & (edge_real[:, None] == 0)).astype(np.float64)
    forward = np.block([[cos, -sin], [sin, cos], [to_real, to_imag]])
    inverse = np.block([[cos, sin, to_real.T], [-sin, cos, to_imag.T]])
    return forward, inverse


def row_k1():
    return np.concatenate([np.repeat(np.arange(8), 8), np.arange(8)])


def twiddle_tables():
    _, y, _ = lane_parts()
    turn = angle(row_k1()[:, None], y[None, :])
    return np.stack([np.cos(turn), np.sin(turn)]).astype(np.float32)


def symbol(k):
    turn = 2.0 * np.pi * (np.asarray(k) % N) / N
    return np.stack([np.cos(turn) - 1.0, np.sin(turn)]).astype(np.float32)


def symbol_tables():
    _, k2, h = lane_parts()
    along_y = symbol(row_k1()[:, None] + 8 * k2[None, :])
    along_x = np.zeros((SLAB, 2, 8, N), np.float32)
    for s in range(SLAB):
        k = np.where(h == 0, 0, 64) if s == 0 else np.full(N, s)
        along_x[s] = np.broadcast_to(symbol(k)[:, None, :], (2, 8, N))
    along_z = np.zeros((2 * GRP, 2, 16, N), np.float32)
    for first in range(2):
        for g in range(GRP):
            for row in range(16):
                m = g * 8 + row
                if row >= 8:
                    k = np.full(N, 64)
                elif first:
                    k = np.full(N, m)
                else:
                    k = np.where(h == 0, m, 64 if m == 0 else N - m)
                along_z[first * GRP + g, :, row] = symbol(k)
    return along_x, along_y, along_z


@functools.cache
def constants():
    x_forward, x_inverse = x_tables()
    z_pairs = [z_tables(first) for first in (False, True)]
    y_pairs = [y_outer_tables(corner) for corner in (False, True)]
    inner_forward, inner_inverse = y_inner_tables()
    along_x, along_y, along_z = symbol_tables()
    return dict(
        wx=split_const(x_forward, 1),
        wxi=split_const(x_inverse, 0),
        wz=np.stack([split_const(pair[0], 2) for pair in z_pairs]),
        wzi=np.stack([split_const(pair[1], 2) for pair in z_pairs]),
        wy=np.stack([split_const(pair[0], 1) for pair in y_pairs]),
        wyi=np.stack([split_const(pair[1], 1) for pair in y_pairs]),
        wl=split_const(inner_forward, 0),
        wli=split_const(inner_inverse, 0),
        we=y_edge_tables()[0],
        wei=y_edge_tables()[1],
        tw=twiddle_tables(),
        dx=along_x,
        dy=along_y,
        dz=along_z,
    )


CONSTANTS = ("wx", "wxi", "wz", "wzi", "wy", "wyi", "wl", "wli", "we", "wei", "tw", "dx", "dy", "dz")


def thirds(value, axis):
    high = value.astype(BF16)
    low = (value - high.astype(F32)).astype(BF16)
    return jnp.concatenate([high, low, high], axis=axis)


def dot(left, right, contract):
    return lax.dot_general(left, right, (contract, ((), ())), preferred_element_type=F32)


def lanes(shape):
    return lax.broadcasted_iota(jnp.int32, shape, len(shape) - 1)


def sublanes(shape):
    return lax.broadcasted_iota(jnp.int32, shape, len(shape) - 2)


def force_lines(take):
    edge = sublanes((16, N)) == 0

    def along_x(part, z2):
        value = take(part, z2)
        return jnp.roll(value, 1, axis=1) - value

    def along_y(part, z2):
        value = take(part, z2)
        return jnp.where(edge, 0.0, jnp.roll(value, 1, axis=0)) - value

    def along_z(part, z2):
        return take(part, 0) - take(part, 1) if z2 == 1 else -take(part, 0)

    lines = []
    for z2 in range(2):
        lines += [
            along_x(0, z2) + ROOT_HALF * (along_z(4, z2) + along_y(5, z2)),
            along_y(1, z2) + ROOT_HALF * (along_z(3, z2) + along_x(5, z2)),
            along_z(2, z2) + ROOT_HALF * (along_y(3, z2) + along_x(4, z2)),
            -(along_x(6, z2) + along_y(7, z2) + along_z(8, z2)),
        ]
    lines += [ROOT_HALF * take(4, 1), ROOT_HALF * take(3, 1), take(2, 1), -take(8, 1)]
    for z2 in range(2):
        for scale, part in ((ROOT_HALF, 5), (1.0, 1), (ROOT_HALF, 3), (-1.0, 7)):
            lines.append(jnp.broadcast_to(scale * take(part, z2)[15:16], (8, N)))
    return jnp.concatenate(lines, axis=0)


def x_forward(lines, wx):
    return dot(wx, thirds(lines, 1), ((1,), (1,)))


def x_inverse(rows, wxi):
    return dot(thirds(rows.T, 1), wxi, ((1,), (0,)))


def z_forward_part(rows, wz):
    low = lanes((32, N)) < 64
    main, rest = rows[:, :N], rows[:, N:]
    parts = jnp.concatenate(
        [
            jnp.where(low, main, rest),
            jnp.where(low, jnp.roll(main, 64, axis=1), jnp.roll(rest, 96, axis=1)),
            jnp.where(low, rest, 0.0),
        ],
        axis=0,
    )
    return dot(wz, thirds(parts, 0), ((1,), (0,)))


def z_forward_end(both):
    lane = lanes((N, N))
    first, second = both[:N], both[N:]
    edge = jnp.where(lane < 96, first, jnp.roll(second, 32, axis=1))
    edge = jnp.where((lane % 8 == sublanes((N, N)) % 8) & (lane >= 64), edge, 0.0)
    return jnp.where(lane < 64, first, jnp.roll(second, 64, axis=1)), edge.reshape(16, 8, N).sum(axis=1)


def z_inverse_begin(rows, edge):
    lane = lanes((N, N))
    low = lane < 64
    edge = jnp.broadcast_to(edge[:, None, :], (16, 8, N)).reshape(N, N)
    edge = jnp.where(lane % 8 == sublanes((N, N)) % 8, edge, 0.0)
    parts = jnp.concatenate(
        [jnp.where(low, rows, edge), jnp.where(low, jnp.roll(rows, 64, axis=1), jnp.roll(edge, 96, axis=1))], axis=0
    )
    return thirds(parts, 0)


def z_inverse_part(parts, wzi):
    lane = lanes((32, N))
    low = lane < 64
    planes = dot(wzi, parts, ((1,), (0,)))
    first, second, third = planes[:32], planes[32:64], planes[64:]
    main = jnp.where(low, first, jnp.roll(second, 64, axis=1))
    rest = jnp.where(low, third, jnp.where(lane < 96, first, jnp.roll(second, 32, axis=1)))
    return jnp.concatenate([main, rest], axis=1)


def exact_dot(left, right):
    return lax.dot_general(
        left, right, (((1,), (0,)), ((), ())), precision=lax.Precision.HIGHEST, preferred_element_type=F32
    )


def y_forward(rows, edge, corner, wy, wl, we, tw):
    outer = dot(wy, thirds(rows, 0), ((1,), (0,)))
    real, imag = outer[:72], outer[72:]
    turns = exact_dot(we, edge)
    lane = lanes((8, N))
    packed = (lane % 8 == 0) & (corner == 1)
    edge_real = turns[:8] + jnp.where(packed, 0.0, turns[24:])
    edge_imag = jnp.where(packed, 0.0, turns[16:24]) - turns[8:16]
    mixed = jnp.where(lane < 64, jnp.roll(edge_imag, 64, axis=1), edge_real)
    extra = jnp.where(packed, jnp.where(lane < 64, -jnp.roll(turns[24:], 64, axis=1), turns[16:24]), 0.0)
    spread = jnp.broadcast_to(mixed[:, None, :], (8, 8, N)).reshape(64, N)
    spread = jnp.where(lanes((64, N)) % 8 == sublanes((64, N)) % 8, spread, 0.0)
    turned = jnp.concatenate(
        [real * tw[0] + imag * tw[1], imag * tw[0] - real * tw[1], jnp.concatenate([spread, extra], axis=0)], axis=1
    )
    inner = dot(thirds(turned, 1), wl, ((1,), (0,)))
    return inner[:, :N], inner[:, N:]


def y_inverse(real, imag, corner, wyi, wli, wei, tw):
    inner = dot(thirds(jnp.concatenate([real, imag], axis=1), 1), wli, ((1,), (0,)))
    real, imag, mixed = inner[:, :N], inner[:, N : 2 * N], inner[:, 2 * N :]
    turned = jnp.concatenate([real * tw[0] - imag * tw[1], imag * tw[0] + real * tw[1]], axis=0)
    rows = dot(wyi, thirds(turned, 0), ((1,), (0,)))
    lane = lanes((8, N))
    packed = (lane % 8 == 0) & (corner == 1)
    spread = jnp.where(lanes((64, N)) % 8 == sublanes((64, N)) % 8, mixed[:64], 0.0)
    turns = exact_dot(wei, jnp.concatenate([spread.reshape(8, 8, N).sum(axis=1), mixed[64:]], axis=1))
    edge_real = turns[:8, :N] - jnp.roll(turns[8:, :N], 64, axis=1)
    edge_imag = turns[8:, :N] + jnp.roll(turns[:8, :N], 64, axis=1)
    extra = turns[:8, N:] - jnp.roll(turns[8:, N:], 64, axis=1)
    return rows, edge_real, jnp.where(packed, extra, edge_imag)


def gradients(lines):
    last = sublanes((16, N)) == 15
    grad_x, grad_y, grad_z = [], [], []
    for c in range(4):
        along = [[], [], []]
        for z2 in range(2):
            start = z2 * 64 + c * 16
            value = lines[start : start + 16]
            above = lines[start + 64 : start + 80]
            begin = 192 + z2 * 32 + c * 8
            edge = jnp.sum(lines[begin : begin + 8], axis=0, keepdims=True)
            along[0].append(jnp.roll(value, N - 1, axis=1) - value)
            along[1].append(jnp.where(last, edge, jnp.roll(value, 15, axis=0)) - value)
            along[2].append(above - value)
        for grad, pair in zip((grad_x, grad_y, grad_z), along):
            grad.append(jnp.concatenate(pair, axis=0))
    return [
        grad_x[0],
        grad_y[1],
        grad_z[2],
        ROOT_HALF * (grad_y[2] + grad_z[1]),
        ROOT_HALF * (grad_x[2] + grad_z[0]),
        ROOT_HALF * (grad_x[1] + grad_y[0]),
        -grad_x[3],
        -grad_y[3],
        -grad_z[3],
    ]


def operator_tables(dx, dy, dz):
    def rows(main, extra):
        return jnp.concatenate([main] * 8 + [extra], axis=0)

    along_x = [rows(dx[i], dx[i]) for i in range(2)]
    along_z = [rows(dz[i][:8], dz[i][8:]) for i in range(2)]
    along_y = [dy[0], dy[1]]
    squares = (
        along_x[0] * along_x[0]
        + along_x[1] * along_x[1]
        + (along_y[0] * along_y[0] + along_y[1] * along_y[1])
        + (along_z[0] * along_z[0] + along_z[1] * along_z[1])
    )
    some = squares > 0.0
    inverse = jnp.where(some, 1.0 / jnp.where(some, squares, 1.0), 0.0)
    part = lanes(squares.shape) // 16 % 4
    own = [
        jnp.where(part == 0, along_x[i], jnp.where(part == 1, along_y[i], jnp.where(part == 2, along_z[i], 0.0)))
        for i in range(2)
    ]
    scale = 1.0 / (N * N * N)
    alpha = inverse * jnp.where(part == 3, scale / 0.8, scale / 1.5)
    beta = inverse * inverse * (scale / 3.0)
    return own[0], own[1], alpha, beta


def operator(real, imag, own_real, own_imag, alpha, beta):
    projected = []
    lane = lanes(real.shape)
    for value in (own_real * real + own_imag * imag, own_real * imag - own_imag * real):
        for width in (32, 16):
            lower = lane % (2 * width) < width
            value = value + jnp.where(lower, jnp.roll(value, N - width, axis=1), jnp.roll(value, width, axis=1))
        projected.append(value * beta)
    return (
        real * alpha - (own_real * projected[0] - own_imag * projected[1]),
        imag * alpha - (own_real * projected[1] + own_imag * projected[0]),
    )


def kernel(adjoint, source, contrast_in, phase_in, grain_in, orientation_in, *rest):
    tables = dict(zip(CONSTANTS, rest[: len(CONSTANTS)]))
    (
        out,
        wx, wxi, wz, wzi, wy, wyi, wl, wli, we, wei, tw, dx, dy, dz,
        fields, right_side, contrast, phase, grain, orientation,
        send1, recv1, send2, recv2, send3, recv3, send4, recv4,
        edge2_out, edge2_in, edge3_out, edge3_in,
        coef, own_real, own_imag, alpha, beta,
        load_sems, send_sems, recv_sems, slab_send, slab_recv,
    ) = rest[len(CONSTANTS):]
    g = lax.axis_index("grp")
    s = lax.axis_index("slab")
    first = jnp.where(s == 0, 1, 0)
    corner = jnp.where((s == 0) & (g == 0), 1, 0)

    pairs = [
        (adjoint, fields),
        (tables["wx"], wx),
        (orientation_in, orientation),
        (grain_in, grain),
        (phase_in, phase),
        (contrast_in, contrast),
        (tables["wz"].at[first], wz),
        (tables["dx"].at[s], dx),
        (tables["dy"], dy),
        (tables["dz"].at[first * GRP + g], dz),
        (tables["wy"].at[corner], wy),
        (tables["wl"], wl),
        (tables["we"], we),
        (tables["tw"], tw),
        (tables["wli"], wli),
        (tables["wyi"].at[corner], wyi),
        (tables["wei"], wei),
        (tables["wzi"].at[first], wzi),
        (tables["wxi"], wxi),
        (source, right_side),
    ]
    loads = [pltpu.make_async_copy(*pair, load_sems.at[i]) for i, pair in enumerate(pairs)]
    for load in loads:
        load.start()

    digit_y, digit_z, digit_x = s // 16, lax.rem(s // 4, 4), lax.rem(s, 4)

    my_slot = digit_z * 16 + digit_y * 4 + digit_x
    core = lax.rem(g, 2)

    def slab_peers(visit, steps_z):
        places = [lax.rem(digit_z + step_z, 4) for step_z in steps_z]

        def row(step_y, carry):
            y = lax.rem(digit_y + step_y, 4)
            for step_x in range(4):
                x = lax.rem(digit_x + step_x, 4)
                for place in places:
                    visit(y * 16 + place * 4 + x, place * 16 + y * 4 + x)
            return carry

        if steps_z == (0,):
            for step_x in range(1, 4):
                x = lax.rem(digit_x + step_x, 4)
                visit(digit_y * 16 + digit_z * 4 + x, digit_z * 16 + digit_y * 4 + x)
        lax.fori_loop(1 if steps_z == (0,) else 0, 4, row, 0)

    def grp_peers(visit):
        def one(step, carry):
            visit(lax.rem(g + step, GRP))
            return carry

        lax.fori_loop(1, GRP, one, 0)

    barrier = pltpu.get_barrier_semaphore()
    for steps_z in ((2,), (1, 3), (0,)):
        slab_peers(
            lambda peer, slot: pl.semaphore_signal(barrier, inc=1, device_id={"slab": peer}, device_id_type=MESH),
            steps_z,
        )
    grp_peers(lambda peer: pl.semaphore_signal(barrier, inc=1, device_id={"grp": peer}, device_id_type=MESH))

    def send_slab(sent, landed, which, steps_z):
        sem = which * 3 + steps_z[0]

        def start(peer, slot):
            pltpu.make_async_remote_copy(
                sent.at[slot], landed.at[my_slot], slab_send.at[sem], slab_recv.at[sem],
                device_id={"slab": peer}, device_id_type=MESH,
            ).start()

        slab_peers(start, steps_z)

    def exchange_grp(sent, landed, sem):
        def start(peer):
            pltpu.make_async_remote_copy(
                sent.at[peer], landed.at[g], send_sems.at[sem], recv_sems.at[sem],
                device_id={"grp": peer}, device_id_type=MESH,
            ).start()

        grp_peers(start)
        landed[g] = sent[g]

    def finish(buffer, sem, count):
        block = buffer.at[pl.ds(0, count)]
        pltpu.make_async_copy(block, block, sem).wait()

    loads[0].wait()
    lines = force_lines(lambda part, z2: fields[part, pl.ds(z2, 16, stride=2), :])
    loads[1].wait()
    send1[...] = x_forward(lines, wx[...]).reshape(SLAB, 2, 2 * N)
    pl.semaphore_wait(barrier, SLAB - 1 + GRP - 1)

    @pl.when(core == 0)
    def _():
        send_slab(send1, recv1, 0, (2,))
        send_slab(send1, recv1, 0, (1, 3))

    @pl.when(core == 1)
    def _():
        send_slab(send1, recv1, 0, (1, 3))
        send_slab(send1, recv1, 0, (2,))

    send_slab(send1, recv1, 0, (0,))
    recv1[my_slot] = send1[my_slot]

    for load in loads[2:6]:
        load.wait()
    ids = jnp.concatenate([grain[pl.ds(z2, 16, stride=2), :] for z2 in range(2)], axis=0)
    high, low = ids // N, ids % N
    entry = jnp.zeros((32, N), jnp.int32)
    for row in range(32):
        line = jnp.broadcast_to(orientation[row : row + 1, :], (32, N))
        entry = jnp.where(high == row, jnp.take_along_axis(line, low, axis=1), entry)
    ceramic = jnp.concatenate([phase[pl.ds(z2, 16, stride=2), :] for z2 in range(2)], axis=0) == 1
    entry = jnp.where(ceramic, entry, 6)
    masks = [entry == t for t in range(6)]
    for pair in range(81):
        value = jnp.full((32, N), contrast[pair // 9, 6, pair % 9], F32)
        for t in range(6):
            value = jnp.where(masks[t], contrast[pair // 9, t, pair % 9], value)
        coef[pair] = value
    for load in loads[6:]:
        load.wait()
    own_real[...], own_imag[...], alpha[...], beta[...] = operator_tables(dx, dy, dz)

    def part1(step_z):
        place = lax.rem(digit_z + step_z, 4)
        return z_forward_part(recv1[pl.ds(place * 16, 16)].reshape(32, 2 * N), wz[place])

    finish(recv1, slab_recv.at[0], 15)
    total = part1(0)
    finish(recv1, slab_recv.at[1], 32)
    total = total + part1(1) + part1(3)
    finish(recv1, slab_recv.at[2], 16)
    rows, edge = z_forward_end(total + part1(2))
    send2[...] = rows.reshape(GRP, 16, N)
    exchange_grp(send2, recv2, 0)
    edge2_out[...] = edge.reshape(GRP, 2, N)
    exchange_grp(edge2_out, edge2_in, 1)

    finish(recv2, recv_sems.at[0], GRP - 1)
    finish(edge2_in, recv_sems.at[1], GRP - 1)
    real, imag = y_forward(
        recv2[...].reshape(N, N), edge2_in[...].reshape(16, N), corner, wy[...], wl[...], we[...], tw
    )
    real, imag = operator(real, imag, own_real[...], own_imag[...], alpha[...], beta[...])
    rows, edge_real, edge_imag = y_inverse(real, imag, corner, wyi[...], wli[...], wei[...], tw)
    send3[...] = rows.reshape(GRP, 16, N)
    exchange_grp(send3, recv3, 2)
    edge3_out[:, 0:1, :] = edge_real.reshape(GRP, 1, N)
    edge3_out[:, 1:2, :] = edge_imag.reshape(GRP, 1, N)
    exchange_grp(edge3_out, edge3_in, 3)

    finish(recv3, recv_sems.at[2], GRP - 1)
    finish(edge3_in, recv_sems.at[3], GRP - 1)
    parts = z_inverse_begin(recv3[...].reshape(N, N), edge3_in[...].reshape(16, N))

    def part4(step_z):
        place = lax.rem(digit_z + step_z, 4)
        send4[pl.ds(place * 16, 16)] = z_inverse_part(parts, wzi[place]).reshape(16, 2, 2 * N)

    part4(2)

    @pl.when(core == 0)
    def _():
        send_slab(send4, recv4, 1, (2,))

    part4(1)
    part4(3)
    send_slab(send4, recv4, 1, (1, 3))

    @pl.when(core == 1)
    def _():
        send_slab(send4, recv4, 1, (2,))

    part4(0)
    send_slab(send4, recv4, 1, (0,))
    recv4[my_slot] = send4[my_slot]

    for sem, count in ((3, 15), (4, 32), (5, 16)):
        finish(recv4, slab_recv.at[sem], count)
    green = gradients(x_inverse(recv4[...].reshape(N, 2 * N), wxi[...]))
    for i in range(9):
        total = jnp.concatenate([right_side[i, pl.ds(z2, 16, stride=2), :] for z2 in range(2)], axis=0)
        for j in range(9):
            total = total - coef[j * 9 + i] * green[j]
        for z2 in range(2):
            out[i, pl.ds(z2, 16, stride=2), :] = total[z2 * 16 : z2 * 16 + 16]

    for which, sent in enumerate((send1, send4)):
        for sem, count in enumerate((15, 32, 16)):
            finish(sent, slab_send.at[which * 3 + sem], count)
    for sem, sent in enumerate((send2, edge2_out, send3, edge3_out)):
        finish(sent, send_sems.at[sem], GRP - 1)


def per_device(adjoint, source, contrast, phase_id, grain_id, orientation):
    table = constants()
    vmem = pl.BlockSpec(memory_space=pltpu.VMEM)
    hbm = pl.BlockSpec(memory_space=pltpu.HBM)
    flat = (9, 32, N)
    result = pl.pallas_call(
        kernel,
        out_shape=pltpu.VMEM(flat, F32),
        in_specs=[hbm] * (6 + len(CONSTANTS)),
        out_specs=vmem,
        scratch_shapes=[
            pltpu.VMEM((128, 384), BF16),
            pltpu.VMEM((384, 128), BF16),
            pltpu.VMEM((4, 256, 288), BF16),
            pltpu.VMEM((4, 96, 768), BF16),
            pltpu.VMEM((144, 384), BF16),
            pltpu.VMEM((128, 432), BF16),
            pltpu.VMEM((1152, 256), BF16),
            pltpu.VMEM((768, 384), BF16),
            pltpu.VMEM((32, 16), F32),
            pltpu.VMEM((16, 8), F32),
            pltpu.VMEM((2, 72, N), F32),
            pltpu.VMEM((2, 8, N), F32),
            pltpu.VMEM((2, 72, N), F32),
            pltpu.VMEM((2, 16, N), F32),
            pltpu.VMEM(flat, F32),
            pltpu.VMEM(flat, F32),
            pltpu.SMEM((9, 7, 9), F32),
            pltpu.VMEM((32, N), jnp.int32),
            pltpu.VMEM((32, N), jnp.int32),
            pltpu.VMEM((32, N), jnp.int32),
            pltpu.VMEM((SLAB, 2, 2 * N), F32),
            pltpu.VMEM((SLAB, 2, 2 * N), F32),
            pltpu.VMEM((GRP, 16, N), F32),
            pltpu.VMEM((GRP, 16, N), F32),
            pltpu.VMEM((GRP, 16, N), F32),
            pltpu.VMEM((GRP, 16, N), F32),
            pltpu.VMEM((SLAB, 2, 2 * N), F32),
            pltpu.VMEM((SLAB, 2, 2 * N), F32),
            pltpu.VMEM((GRP, 2, N), F32),
            pltpu.VMEM((GRP, 2, N), F32),
            pltpu.VMEM((GRP, 2, N), F32),
            pltpu.VMEM((GRP, 2, N), F32),
            pltpu.VMEM((81, 32, N), F32),
            pltpu.VMEM((72, N), F32),
            pltpu.VMEM((72, N), F32),
            pltpu.VMEM((72, N), F32),
            pltpu.VMEM((72, N), F32),
            pltpu.SemaphoreType.DMA((20,)),
            pltpu.SemaphoreType.DMA((4,)),
            pltpu.SemaphoreType.DMA((4,)),
            pltpu.SemaphoreType.DMA((6,)),
            pltpu.SemaphoreType.DMA((6,)),
        ],
        compiler_params=pltpu.CompilerParams(
            collective_id=0, has_side_effects=True, vmem_limit_bytes=60 * 1024 * 1024
        ),
    )(
        adjoint.reshape(flat),
        source.reshape(flat),
        contrast.transpose(1, 0, 2),
        phase_id.reshape(32, N),
        grain_id.reshape(32, N),
        orientation.reshape(32, N),
        *[jnp.asarray(table[name]) for name in CONSTANTS],
    )
    return result.reshape(adjoint.shape)


def solution(mesh):
    placed = (
        P(None, "grp", "slab", None),
        P(None, "grp", "slab", None),
        P(),
        P("grp", "slab", None),
        P("grp", "slab", None),
        P(),
    )
    return jax.shard_map(
        per_device,
        mesh=mesh,
        in_specs=placed,
        out_specs=P(None, "grp", "slab", None),
        check_vma=False,
    )
```

```python
import functools

import jax
import jax.numpy as jnp
import ml_dtypes
import numpy as np
from jax import lax
from jax.experimental import pallas as pl
from jax.experimental.pallas import tpu as pltpu
from jax.sharding import PartitionSpec as P

N = 128
GRP = 8
SLAB = 64
F32 = jnp.float32
BF16 = jnp.bfloat16
ROOT_HALF = float(np.sqrt(0.5))
MESH = pl.DeviceIdType.MESH
SLOTS = np.arange(SLAB).reshape(4, 4, 4).transpose(1, 0, 2).reshape(SLAB)


def split_const(matrix, axis):
    high = matrix.astype(ml_dtypes.bfloat16)
    low = (matrix - high.astype(np.float64)).astype(ml_dtypes.bfloat16)
    return np.concatenate([high, high, low], axis=axis)


def angle(a, b, length=N):
    return 2.0 * np.pi * ((np.asarray(a) * np.asarray(b)) % length) / length


def x_tables():
    x = np.arange(N)
    forward = np.zeros((SLAB, 2, N))
    inverse = np.zeros((SLAB, 2, N))
    for k in range(1, SLAB):
        forward[k, 0] = np.cos(angle(k, x))
        forward[k, 1] = -np.sin(angle(k, x))
    forward[0, 0] = 1.0
    forward[0, 1] = (-1.0) ** x
    inverse[1:] = 2.0 * forward[1:]
    inverse[0] = forward[0]
    return forward[SLOTS].reshape(N, N), inverse[SLOTS].reshape(N, N)


def z_tables(first):
    z = (2 * np.arange(SLAB)[:, None] + np.arange(3)[None, :]) % N
    forward = np.zeros((2, GRP, 2, 8, 3, SLAB, 2))
    inverse = np.zeros((3, SLAB, 2, 2, GRP, 2, 8))
    for m in range(SLAB):
        hi, lo = divmod(m, 8)
        for h in range(2):
            for z2 in range(3):
                if first:
                    cos, sin = np.cos(angle(m, z[:, z2])), np.sin(angle(m, z[:, z2]))
                    if m == 0:
                        alt = (-1.0) ** z[:, z2]
                        forward[h, hi, 0, lo, z2, :, h] = 1.0
                        forward[h, hi, 1, lo, z2, :, h] = alt
                        inverse[z2, :, h, h, hi, 0, lo] = 1.0
                        inverse[z2, :, h, h, hi, 1, lo] = alt
                    else:
                        forward[h, hi, 0, lo, z2, :, h] = cos
                        forward[h, hi, 1, lo, z2, :, h] = -sin
                        inverse[z2, :, h, h, hi, 0, lo] = 2.0 * cos
                        inverse[z2, :, h, h, hi, 1, lo] = -2.0 * sin
                else:
                    k = m if h == 0 else (64 if m == 0 else N - m)
                    cos, sin = np.cos(angle(k, z[:, z2])), np.sin(angle(k, z[:, z2]))
                    forward[h, hi, 0, lo, z2, :, 0] = cos
                    forward[h, hi, 0, lo, z2, :, 1] = sin
                    forward[h, hi, 1, lo, z2, :, 0] = -sin
                    forward[h, hi, 1, lo, z2, :, 1] = cos
                    inverse[z2, :, 0, h, hi, 0, lo] = cos
                    inverse[z2, :, 0, h, hi, 1, lo] = -sin
                    inverse[z2, :, 1, h, hi, 0, lo] = sin
                    inverse[z2, :, 1, h, hi, 1, lo] = cos
    forward = forward[..., SLOTS, :].reshape(256, 3, 4, 32).transpose(2, 0, 1, 3).reshape(4, 256, 96)
    inverse = inverse[:, SLOTS].reshape(3, 4, 32, 256).transpose(1, 0, 2, 3).reshape(4, 96, 256)
    return forward, inverse


def y_outer_tables(corner):
    forward = np.zeros((2, 72, GRP, 2, 8))
    inverse = np.zeros((GRP, 2, 8, 2, 72))
    g = np.arange(GRP)
    for k1 in range(8):
        cos, sin = np.cos(angle(k1, g, 8)), np.sin(angle(k1, g, 8))
        for kz in range(8):
            row = k1 * 8 + kz
            if corner and kz == 0:
                for source, target in ((0, row), (1, 64 + k1)):
                    forward[0, target, :, source, kz] = cos
                    forward[1, target, :, source, kz] = -sin
                    inverse[:, source, kz, 0, target] = cos
                    inverse[:, source, kz, 1, target] = -sin
            else:
                forward[0, row, :, 0, kz] = cos
                forward[0, row, :, 1, kz] = sin
                forward[1, row, :, 0, kz] = -sin
                forward[1, row, :, 1, kz] = cos
                inverse[:, 0, kz, 0, row] = cos
                inverse[:, 0, kz, 1, row] = -sin
                inverse[:, 1, kz, 0, row] = sin
                inverse[:, 1, kz, 1, row] = cos
    return forward.reshape(144, 128), inverse.reshape(128, 144)


def y_edge_tables():
    turn = angle(np.arange(8)[:, None], np.arange(8)[None, :] + 1, 8)
    forward = np.zeros((2, 2, 8, 8, 2))
    for ri in range(2):
        forward[ri, 0, :, :, ri] = np.cos(turn)
        forward[ri, 1, :, :, ri] = np.sin(turn)
    inverse = np.concatenate([np.cos(turn).T, np.sin(turn).T])
    return forward.reshape(32, 16).astype(np.float32), inverse.astype(np.float32)


def lane_parts():
    lane = np.arange(N)
    return lane // 16 % 4, lane % 16, lane // 64


def edge_parts():
    lane = np.arange(N)
    return lane // 8 % 4, lane // 32 % 2, lane // 64


def y_inner_tables():
    c, y, h = lane_parts()
    same = (c[:, None] == c[None, :]) & (h[:, None] == h[None, :])
    cos = np.where(same, np.cos(angle(y[:, None], y[None, :], 16)), 0.0)
    sin = np.where(same, np.sin(angle(y[:, None], y[None, :], 16)), 0.0)
    edge_c, edge_h, edge_real = edge_parts()
    meet = (edge_c[:, None] == c[None, :]) & (edge_h[:, None] == h[None, :])
    to_real = (meet & (edge_real[:, None] == 1)).astype(np.float64)
    to_imag = (meet & (edge_real[:, None] == 0)).astype(np.float64)
    forward = np.block([[cos, -sin], [sin, cos], [to_real, to_imag]])
    inverse = np.block([[cos, sin, to_real.T], [-sin, cos, to_imag.T]])
    return forward, inverse


def row_k1():
    return np.concatenate([np.repeat(np.arange(8), 8), np.arange(8)])


def twiddle_tables():
    _, y, _ = lane_parts()
    turn = angle(row_k1()[:, None], y[None, :])
    return np.stack([np.cos(turn), np.sin(turn)]).astype(np.float32)


def symbol(k):
    turn = 2.0 * np.pi * (np.asarray(k) % N) / N
    return np.stack([np.cos(turn) - 1.0, np.sin(turn)]).astype(np.float32)


def symbol_tables():
    _, k2, h = lane_parts()
    along_y = symbol(row_k1()[:, None] + 8 * k2[None, :])
    along_x = np.zeros((SLAB, 2, 8, N), np.float32)
    for s in range(SLAB):
        k = np.where(h == 0, 0, 64) if s == 0 else np.full(N, s)
        along_x[s] = np.broadcast_to(symbol(k)[:, None, :], (2, 8, N))
    along_z = np.zeros((2 * GRP, 2, 16, N), np.float32)
    for first in range(2):
        for g in range(GRP):
            for row in range(16):
                m = g * 8 + row
                if row >= 8:
                    k = np.full(N, 64)
                elif first:
                    k = np.full(N, m)
                else:
                    k = np.where(h == 0, m, 64 if m == 0 else N - m)
                along_z[first * GRP + g, :, row] = symbol(k)
    return along_x, along_y, along_z


@functools.cache
def constants():
    x_forward, x_inverse = x_tables()
    z_pairs = [z_tables(first) for first in (False, True)]
    y_pairs = [y_outer_tables(corner) for corner in (False, True)]
    inner_forward, inner_inverse = y_inner_tables()
    along_x, along_y, along_z = symbol_tables()
    return dict(
        wx=split_const(x_forward, 1),
        wxi=split_const(x_inverse, 0),
        wz=np.stack([split_const(pair[0], 2) for pair in z_pairs]),
        wzi=np.stack([split_const(pair[1], 2) for pair in z_pairs]),
        wy=np.stack([split_const(pair[0], 1) for pair in y_pairs]),
        wyi=np.stack([split_const(pair[1], 1) for pair in y_pairs]),
        wl=split_const(inner_forward, 0),
        wli=split_const(inner_inverse, 0),
        we=y_edge_tables()[0],
        wei=y_edge_tables()[1],
        tw=twiddle_tables(),
        dx=along_x,
        dy=along_y,
        dz=along_z,
    )


CONSTANTS = ("wx", "wxi", "wz", "wzi", "wy", "wyi", "wl", "wli", "we", "wei", "tw", "dx", "dy", "dz")


def thirds(value, axis):
    high = value.astype(BF16)
    low = (value - high.astype(F32)).astype(BF16)
    return jnp.concatenate([high, low, high], axis=axis)


def dot(left, right, contract):
    return lax.dot_general(left, right, (contract, ((), ())), preferred_element_type=F32)


def lanes(shape):
    return lax.broadcasted_iota(jnp.int32, shape, len(shape) - 1)


def sublanes(shape):
    return lax.broadcasted_iota(jnp.int32, shape, len(shape) - 2)


def force_lines(take):
    edge = sublanes((16, N)) == 0

    def along_x(part, z2):
        value = take(part, z2)
        return jnp.roll(value, 1, axis=1) - value

    def along_y(part, z2):
        value = take(part, z2)
        return jnp.where(edge, 0.0, jnp.roll(value, 1, axis=0)) - value

    def along_z(part, z2):
        return take(part, 0) - take(part, 1) if z2 == 1 else -take(part, 0)

    lines = []
    for z2 in range(2):
        lines += [
            along_x(0, z2) + ROOT_HALF * (along_z(4, z2) + along_y(5, z2)),
            along_y(1, z2) + ROOT_HALF * (along_z(3, z2) + along_x(5, z2)),
            along_z(2, z2) + ROOT_HALF * (along_y(3, z2) + along_x(4, z2)),
            -(along_x(6, z2) + along_y(7, z2) + along_z(8, z2)),
        ]
    lines += [ROOT_HALF * take(4, 1), ROOT_HALF * take(3, 1), take(2, 1), -take(8, 1)]
    for z2 in range(2):
        for scale, part in ((ROOT_HALF, 5), (1.0, 1), (ROOT_HALF, 3), (-1.0, 7)):
            lines.append(jnp.broadcast_to(scale * take(part, z2)[15:16], (8, N)))
    return jnp.concatenate(lines, axis=0)


def x_forward(lines, wx):
    return dot(wx, thirds(lines, 1), ((1,), (1,)))


def x_inverse(rows, wxi):
    return dot(thirds(rows.T, 1), wxi, ((1,), (0,)))


def z_forward_part(rows, wz):
    low = lanes((32, N)) < 64
    main, rest = rows[:, :N], rows[:, N:]
    parts = jnp.concatenate(
        [
            jnp.where(low, main, rest),
            jnp.where(low, jnp.roll(main, 64, axis=1), jnp.roll(rest, 96, axis=1)),
            jnp.where(low, rest, 0.0),
        ],
        axis=0,
    )
    return dot(wz, thirds(parts, 0), ((1,), (0,)))


def z_forward_end(both):
    lane = lanes((N, N))
    first, second = both[:N], both[N:]
    edge = jnp.where(lane < 96, first, jnp.roll(second, 32, axis=1))
    edge = jnp.where((lane % 8 == sublanes((N, N)) % 8) & (lane >= 64), edge, 0.0)
    return jnp.where(lane < 64, first, jnp.roll(second, 64, axis=1)), edge.reshape(16, 8, N).sum(axis=1)


def z_inverse_begin(rows, edge):
    lane = lanes((N, N))
    low = lane < 64
    edge = jnp.broadcast_to(edge[:, None, :], (16, 8, N)).reshape(N, N)
    edge = jnp.where(lane % 8 == sublanes((N, N)) % 8, edge, 0.0)
    parts = jnp.concatenate(
        [jnp.where(low, rows, edge), jnp.where(low, jnp.roll(rows, 64, axis=1), jnp.roll(edge, 96, axis=1))], axis=0
    )
    return thirds(parts, 0)


def z_inverse_part(parts, wzi):
    lane = lanes((32, N))
    low = lane < 64
    planes = dot(wzi, parts, ((1,), (0,)))
    first, second, third = planes[:32], planes[32:64], planes[64:]
    main = jnp.where(low, first, jnp.roll(second, 64, axis=1))
    rest = jnp.where(low, third, jnp.where(lane < 96, first, jnp.roll(second, 32, axis=1)))
    return jnp.concatenate([main, rest], axis=1)


def exact_dot(left, right):
    return lax.dot_general(
        left, right, (((1,), (0,)), ((), ())), precision=lax.Precision.HIGHEST, preferred_element_type=F32
    )


def y_forward(rows, edge, corner, wy, wl, we, tw):
    outer = dot(wy, thirds(rows, 0), ((1,), (0,)))
    real, imag = outer[:72], outer[72:]
    turns = exact_dot(we, edge)
    lane = lanes((8, N))
    packed = (lane % 8 == 0) & (corner == 1)
    edge_real = turns[:8] + jnp.where(packed, 0.0, turns[24:])
    edge_imag = jnp.where(packed, 0.0, turns[16:24]) - turns[8:16]
    mixed = jnp.where(lane < 64, jnp.roll(edge_imag, 64, axis=1), edge_real)
    extra = jnp.where(packed, jnp.where(lane < 64, -jnp.roll(turns[24:], 64, axis=1), turns[16:24]), 0.0)
    spread = jnp.broadcast_to(mixed[:, None, :], (8, 8, N)).reshape(64, N)
    spread = jnp.where(lanes((64, N)) % 8 == sublanes((64, N)) % 8, spread, 0.0)
    turned = jnp.concatenate(
        [real * tw[0] + imag * tw[1], imag * tw[0] - real * tw[1], jnp.concatenate([spread, extra], axis=0)], axis=1
    )
    inner = dot(thirds(turned, 1), wl, ((1,), (0,)))
    return inner[:, :N], inner[:, N:]


def y_inverse(real, imag, corner, wyi, wli, wei, tw):
    inner = dot(thirds(jnp.concatenate([real, imag], axis=1), 1), wli, ((1,), (0,)))
    real, imag, mixed = inner[:, :N], inner[:, N : 2 * N], inner[:, 2 * N :]
    turned = jnp.concatenate([real * tw[0] - imag * tw[1], imag * tw[0] + real * tw[1]], axis=0)
    rows = dot(wyi, thirds(turned, 0), ((1,), (0,)))
    lane = lanes((8, N))
    packed = (lane % 8 == 0) & (corner == 1)
    spread = jnp.where(lanes((64, N)) % 8 == sublanes((64, N)) % 8, mixed[:64], 0.0)
    turns = exact_dot(wei, jnp.concatenate([spread.reshape(8, 8, N).sum(axis=1), mixed[64:]], axis=1))
    edge_real = turns[:8, :N] - jnp.roll(turns[8:, :N], 64, axis=1)
    edge_imag = turns[8:, :N] + jnp.roll(turns[:8, :N], 64, axis=1)
    extra = turns[:8, N:] - jnp.roll(turns[8:, N:], 64, axis=1)
    return rows, edge_real, jnp.where(packed, extra, edge_imag)


def gradients(lines):
    last = sublanes((16, N)) == 15
    grad_x, grad_y, grad_z = [], [], []
    for c in range(4):
        along = [[], [], []]
        for z2 in range(2):
            start = z2 * 64 + c * 16
            value = lines[start : start + 16]
            above = lines[start + 64 : start + 80]
            begin = 192 + z2 * 32 + c * 8
            edge = jnp.sum(lines[begin : begin + 8], axis=0, keepdims=True)
            along[0].append(jnp.roll(value, N - 1, axis=1) - value)
            along[1].append(jnp.where(last, edge, jnp.roll(value, 15, axis=0)) - value)
            along[2].append(above - value)
        for grad, pair in zip((grad_x, grad_y, grad_z), along):
            grad.append(jnp.concatenate(pair, axis=0))
    return [
        grad_x[0],
        grad_y[1],
        grad_z[2],
        ROOT_HALF * (grad_y[2] + grad_z[1]),
        ROOT_HALF * (grad_x[2] + grad_z[0]),
        ROOT_HALF * (grad_x[1] + grad_y[0]),
        -grad_x[3],
        -grad_y[3],
        -grad_z[3],
    ]


def operator_tables(dx, dy, dz):
    def rows(main, extra):
        return jnp.concatenate([main] * 8 + [extra], axis=0)

    along_x = [rows(dx[i], dx[i]) for i in range(2)]
    along_z = [rows(dz[i][:8], dz[i][8:]) for i in range(2)]
    along_y = [dy[0], dy[1]]
    squares = (
        along_x[0] * along_x[0]
        + along_x[1] * along_x[1]
        + (along_y[0] * along_y[0] + along_y[1] * along_y[1])
        + (along_z[0] * along_z[0] + along_z[1] * along_z[1])
    )
    some = squares > 0.0
    inverse = jnp.where(some, 1.0 / jnp.where(some, squares, 1.0), 0.0)
    part = lanes(squares.shape) // 16 % 4
    own = [
        jnp.where(part == 0, along_x[i], jnp.where(part == 1, along_y[i], jnp.where(part == 2, along_z[i], 0.0)))
        for i in range(2)
    ]
    scale = 1.0 / (N * N * N)
    alpha = inverse * jnp.where(part == 3, scale / 0.8, scale / 1.5)
    beta = inverse * inverse * (scale / 3.0)
    return own[0], own[1], alpha, beta


def operator(real, imag, own_real, own_imag, alpha, beta):
    projected = []
    lane = lanes(real.shape)
    for value in (own_real * real + own_imag * imag, own_real * imag - own_imag * real):
        for width in (32, 16):
            lower = lane % (2 * width) < width
            value = value + jnp.where(lower, jnp.roll(value, N - width, axis=1), jnp.roll(value, width, axis=1))
        projected.append(value * beta)
    return (
        real * alpha - (own_real * projected[0] - own_imag * projected[1]),
        imag * alpha - (own_real * projected[1] + own_imag * projected[0]),
    )


def kernel(adjoint, source, contrast_in, phase_in, grain_in, orientation_in, *rest):
    tables = dict(zip(CONSTANTS, rest[: len(CONSTANTS)]))
    (
        out,
        wx, wxi, wz, wzi, wy, wyi, wl, wli, we, wei, tw, dx, dy, dz,
        fields, right_side, contrast, phase, grain, orientation,
        send1, recv1, send2, recv2, send3, recv3, send4, recv4,
        edge2_out, edge2_in, edge3_out, edge3_in,
        coef, own_real, own_imag, alpha, beta,
        load_sems, send_sems, recv_sems, slab_send, slab_recv,
    ) = rest[len(CONSTANTS):]
    g = lax.axis_index("grp")
    s = lax.axis_index("slab")
    first = jnp.where(s == 0, 1, 0)
    corner = jnp.where((s == 0) & (g == 0), 1, 0)

    pairs = [
        (adjoint, fields),
        (tables["wx"], wx),
        (orientation_in, orientation),
        (grain_in, grain),
        (phase_in, phase),
        (contrast_in, contrast),
        (tables["wz"].at[first], wz),
        (tables["dx"].at[s], dx),
        (tables["dy"], dy),
        (tables["dz"].at[first * GRP + g], dz),
        (tables["wy"].at[corner], wy),
        (tables["wl"], wl),
        (tables["we"], we),
        (tables["tw"], tw),
        (tables["wli"], wli),
        (tables["wyi"].at[corner], wyi),
        (tables["wei"], wei),
        (tables["wzi"].at[first], wzi),
        (tables["wxi"], wxi),
        (source, right_side),
    ]
    loads = [pltpu.make_async_copy(*pair, load_sems.at[i]) for i, pair in enumerate(pairs)]
    for load in loads:
        load.start()

    digit_y, digit_z, digit_x = s // 16, lax.rem(s // 4, 4), lax.rem(s, 4)

    my_slot = digit_z * 16 + digit_y * 4 + digit_x
    core = lax.rem(g, 2)

    def slab_peers(visit, steps_z):
        places = [lax.rem(digit_z + step_z, 4) for step_z in steps_z]

        def row(step_y, carry):
            y = lax.rem(digit_y + step_y, 4)
            for step_x in range(4):
                x = lax.rem(digit_x + step_x, 4)
                for place in places:
                    visit(y * 16 + place * 4 + x, place * 16 + y * 4 + x)
            return carry

        if steps_z == (0,):
            for step_x in range(1, 4):
                x = lax.rem(digit_x + step_x, 4)
                visit(digit_y * 16 + digit_z * 4 + x, digit_z * 16 + digit_y * 4 + x)
        lax.fori_loop(1 if steps_z == (0,) else 0, 4, row, 0)

    def grp_peers(visit):
        def one(step, carry):
            visit(lax.rem(g + step, GRP))
            return carry

        lax.fori_loop(1, GRP, one, 0)

    barrier = pltpu.get_barrier_semaphore()
    for steps_z in ((2,), (1, 3), (0,)):
        slab_peers(
            lambda peer, slot: pl.semaphore_signal(barrier, inc=1, device_id={"slab": peer}, device_id_type=MESH),
            steps_z,
        )
    grp_peers(lambda peer: pl.semaphore_signal(barrier, inc=1, device_id={"grp": peer}, device_id_type=MESH))

    def send_slab(sent, landed, which, steps_z):
        sem = which * 3 + steps_z[0]

        def start(peer, slot):
            pltpu.make_async_remote_copy(
                sent.at[slot], landed.at[my_slot], slab_send.at[sem], slab_recv.at[sem],
                device_id={"slab": peer}, device_id_type=MESH,
            ).start()

        slab_peers(start, steps_z)

    def exchange_grp(sent, landed, sem):
        def start(peer):
            pltpu.make_async_remote_copy(
                sent.at[peer], landed.at[g], send_sems.at[sem], recv_sems.at[sem],
                device_id={"grp": peer}, device_id_type=MESH,
            ).start()

        grp_peers(start)
        landed[g] = sent[g]

    def finish(buffer, sem, count):
        block = buffer.at[pl.ds(0, count)]
        pltpu.make_async_copy(block, block, sem).wait()

    loads[0].wait()
    lines = force_lines(lambda part, z2: fields[part, pl.ds(z2, 16, stride=2), :])
    loads[1].wait()
    send1[...] = x_forward(lines, wx[...]).reshape(SLAB, 2, 2 * N)
    pl.semaphore_wait(barrier, SLAB - 1 + GRP - 1)

    send_slab(send1, recv1, 0, (2,))

    for load in loads[2:6]:
        load.wait()
    ids = jnp.concatenate([grain[pl.ds(z2, 16, stride=2), :] for z2 in range(2)], axis=0)
    high, low = ids // N, ids % N
    entry = jnp.zeros((32, N), jnp.int32)
    for row in range(32):
        line = jnp.broadcast_to(orientation[row : row + 1, :], (32, N))
        entry = jnp.where(high == row, jnp.take_along_axis(line, low, axis=1), entry)
    ceramic = jnp.concatenate([phase[pl.ds(z2, 16, stride=2), :] for z2 in range(2)], axis=0) == 1
    entry = jnp.where(ceramic, entry, 6)
    masks = [entry == t for t in range(6)]
    for pair in range(81):
        value = jnp.full((32, N), contrast[pair // 9, 6, pair % 9], F32)
        for t in range(6):
            value = jnp.where(masks[t], contrast[pair // 9, t, pair % 9], value)
        coef[pair] = value
    send_slab(send1, recv1, 0, (1, 3))
    send_slab(send1, recv1, 0, (0,))
    recv1[my_slot] = send1[my_slot]
    for load in loads[6:]:
        load.wait()
    own_real[...], own_imag[...], alpha[...], beta[...] = operator_tables(dx, dy, dz)

    def part1(step_z):
        place = lax.rem(digit_z + step_z, 4)
        return z_forward_part(recv1[pl.ds(place * 16, 16)].reshape(32, 2 * N), wz[place])

    finish(recv1, slab_recv.at[0], 15)
    total = part1(0)
    finish(recv1, slab_recv.at[1], 32)
    total = total + part1(1) + part1(3)
    finish(recv1, slab_recv.at[2], 16)
    rows, edge = z_forward_end(total + part1(2))
    send2[...] = rows.reshape(GRP, 16, N)
    exchange_grp(send2, recv2, 0)
    edge2_out[...] = edge.reshape(GRP, 2, N)
    exchange_grp(edge2_out, edge2_in, 1)

    finish(recv2, recv_sems.at[0], GRP - 1)
    finish(edge2_in, recv_sems.at[1], GRP - 1)
    real, imag = y_forward(
        recv2[...].reshape(N, N), edge2_in[...].reshape(16, N), corner, wy[...], wl[...], we[...], tw
    )
    real, imag = operator(real, imag, own_real[...], own_imag[...], alpha[...], beta[...])
    rows, edge_real, edge_imag = y_inverse(real, imag, corner, wyi[...], wli[...], wei[...], tw)
    send3[...] = rows.reshape(GRP, 16, N)
    exchange_grp(send3, recv3, 2)
    edge3_out[:, 0:1, :] = edge_real.reshape(GRP, 1, N)
    edge3_out[:, 1:2, :] = edge_imag.reshape(GRP, 1, N)
    exchange_grp(edge3_out, edge3_in, 3)

    finish(recv3, recv_sems.at[2], GRP - 1)
    finish(edge3_in, recv_sems.at[3], GRP - 1)
    parts = z_inverse_begin(recv3[...].reshape(N, N), edge3_in[...].reshape(16, N))

    def part4(step_z):
        place = lax.rem(digit_z + step_z, 4)
        send4[pl.ds(place * 16, 16)] = z_inverse_part(parts, wzi[place]).reshape(16, 2, 2 * N)

    part4(2)
    send_slab(send4, recv4, 1, (2,))
    part4(1)
    part4(3)
    finish(send4, slab_send.at[5], 16)
    send_slab(send4, recv4, 1, (1, 3))
    part4(0)
    send_slab(send4, recv4, 1, (0,))
    recv4[my_slot] = send4[my_slot]

    for sem, count in ((3, 15), (4, 32), (5, 16)):
        finish(recv4, slab_recv.at[sem], count)
    green = gradients(x_inverse(recv4[...].reshape(N, 2 * N), wxi[...]))
    for i in range(9):
        total = jnp.concatenate([right_side[i, pl.ds(z2, 16, stride=2), :] for z2 in range(2)], axis=0)
        for j in range(9):
            total = total - coef[j * 9 + i] * green[j]
        for z2 in range(2):
            out[i, pl.ds(z2, 16, stride=2), :] = total[z2 * 16 : z2 * 16 + 16]

    for which, sent in enumerate((send1, send4)):
        for sem, count in enumerate((15, 32)):
            finish(sent, slab_send.at[which * 3 + sem], count)
    finish(send1, slab_send.at[2], 16)
    for sem, sent in enumerate((send2, edge2_out, send3, edge3_out)):
        finish(sent, send_sems.at[sem], GRP - 1)


def per_device(adjoint, source, contrast, phase_id, grain_id, orientation):
    table = constants()
    vmem = pl.BlockSpec(memory_space=pltpu.VMEM)
    hbm = pl.BlockSpec(memory_space=pltpu.HBM)
    flat = (9, 32, N)
    result = pl.pallas_call(
        kernel,
        out_shape=pltpu.VMEM(flat, F32),
        in_specs=[hbm] * (6 + len(CONSTANTS)),
        out_specs=vmem,
        scratch_shapes=[
            pltpu.VMEM((128, 384), BF16),
            pltpu.VMEM((384, 128), BF16),
            pltpu.VMEM((4, 256, 288), BF16),
            pltpu.VMEM((4, 96, 768), BF16),
            pltpu.VMEM((144, 384), BF16),
            pltpu.VMEM((128, 432), BF16),
            pltpu.VMEM((1152, 256), BF16),
            pltpu.VMEM((768, 384), BF16),
            pltpu.VMEM((32, 16), F32),
            pltpu.VMEM((16, 8), F32),
            pltpu.VMEM((2, 72, N), F32),
            pltpu.VMEM((2, 8, N), F32),
            pltpu.VMEM((2, 72, N), F32),
            pltpu.VMEM((2, 16, N), F32),
            pltpu.VMEM(flat, F32),
            pltpu.VMEM(flat, F32),
            pltpu.SMEM((9, 7, 9), F32),
            pltpu.VMEM((32, N), jnp.int32),
            pltpu.VMEM((32, N), jnp.int32),
            pltpu.VMEM((32, N), jnp.int32),
            pltpu.VMEM((SLAB, 2, 2 * N), F32),
            pltpu.VMEM((SLAB, 2, 2 * N), F32),
            pltpu.VMEM((GRP, 16, N), F32),
            pltpu.VMEM((GRP, 16, N), F32),
            pltpu.VMEM((GRP, 16, N), F32),
            pltpu.VMEM((GRP, 16, N), F32),
            pltpu.VMEM((SLAB, 2, 2 * N), F32),
            pltpu.VMEM((SLAB, 2, 2 * N), F32),
            pltpu.VMEM((GRP, 2, N), F32),
            pltpu.VMEM((GRP, 2, N), F32),
            pltpu.VMEM((GRP, 2, N), F32),
            pltpu.VMEM((GRP, 2, N), F32),
            pltpu.VMEM((81, 32, N), F32),
            pltpu.VMEM((72, N), F32),
            pltpu.VMEM((72, N), F32),
            pltpu.VMEM((72, N), F32),
            pltpu.VMEM((72, N), F32),
            pltpu.SemaphoreType.DMA((20,)),
            pltpu.SemaphoreType.DMA((4,)),
            pltpu.SemaphoreType.DMA((4,)),
            pltpu.SemaphoreType.DMA((6,)),
            pltpu.SemaphoreType.DMA((6,)),
        ],
        compiler_params=pltpu.CompilerParams(
            collective_id=0, has_side_effects=True, vmem_limit_bytes=60 * 1024 * 1024
        ),
    )(
        adjoint.reshape(flat),
        source.reshape(flat),
        contrast.transpose(1, 0, 2),
        phase_id.reshape(32, N),
        grain_id.reshape(32, N),
        orientation.reshape(32, N),
        *[jnp.asarray(table[name]) for name in CONSTANTS],
    )
    return result.reshape(adjoint.shape)


def solution(mesh):
    placed = (
        P(None, "grp", "slab", None),
        P(None, "grp", "slab", None),
        P(),
        P("grp", "slab", None),
        P("grp", "slab", None),
        P(),
    )
    return jax.shard_map(
        per_device,
        mesh=mesh,
        in_specs=placed,
        out_specs=P(None, "grp", "slab", None),
        check_vma=False,
    )
```

```python
import functools

import jax
import jax.numpy as jnp
import ml_dtypes
import numpy as np
from jax import lax
from jax.experimental import pallas as pl
from jax.experimental.pallas import tpu as pltpu
from jax.sharding import PartitionSpec as P

N = 128
GRP = 8
SLAB = 64
F32 = jnp.float32
BF16 = jnp.bfloat16
ROOT_HALF = float(np.sqrt(0.5))
MESH = pl.DeviceIdType.MESH
SLOTS = np.arange(SLAB).reshape(4, 4, 4).transpose(1, 0, 2).reshape(SLAB)


def split_const(matrix, axis):
    high = matrix.astype(ml_dtypes.bfloat16)
    low = (matrix - high.astype(np.float64)).astype(ml_dtypes.bfloat16)
    return np.concatenate([high, high, low], axis=axis)


def angle(a, b, length=N):
    return 2.0 * np.pi * ((np.asarray(a) * np.asarray(b)) % length) / length


def x_tables():
    x = np.arange(N)
    forward = np.zeros((SLAB, 2, N))
    inverse = np.zeros((SLAB, 2, N))
    for k in range(1, SLAB):
        forward[k, 0] = np.cos(angle(k, x))
        forward[k, 1] = -np.sin(angle(k, x))
    forward[0, 0] = 1.0
    forward[0, 1] = (-1.0) ** x
    inverse[1:] = 2.0 * forward[1:]
    inverse[0] = forward[0]
    return forward[SLOTS].reshape(N, N), inverse[SLOTS].reshape(N, N)


def z_tables(first):
    z = (2 * np.arange(SLAB)[:, None] + np.arange(3)[None, :]) % N
    forward = np.zeros((2, GRP, 2, 8, 3, SLAB, 2))
    inverse = np.zeros((3, SLAB, 2, 2, GRP, 2, 8))
    for m in range(SLAB):
        hi, lo = divmod(m, 8)
        for h in range(2):
            for z2 in range(3):
                if first:
                    cos, sin = np.cos(angle(m, z[:, z2])), np.sin(angle(m, z[:, z2]))
                    if m == 0:
                        alt = (-1.0) ** z[:, z2]
                        forward[h, hi, 0, lo, z2, :, h] = 1.0
                        forward[h, hi, 1, lo, z2, :, h] = alt
                        inverse[z2, :, h, h, hi, 0, lo] = 1.0
                        inverse[z2, :, h, h, hi, 1, lo] = alt
                    else:
                        forward[h, hi, 0, lo, z2, :, h] = cos
                        forward[h, hi, 1, lo, z2, :, h] = -sin
                        inverse[z2, :, h, h, hi, 0, lo] = 2.0 * cos
                        inverse[z2, :, h, h, hi, 1, lo] = -2.0 * sin
                else:
                    k = m if h == 0 else (64 if m == 0 else N - m)
                    cos, sin = np.cos(angle(k, z[:, z2])), np.sin(angle(k, z[:, z2]))
                    forward[h, hi, 0, lo, z2, :, 0] = cos
                    forward[h, hi, 0, lo, z2, :, 1] = sin
                    forward[h, hi, 1, lo, z2, :, 0] = -sin
                    forward[h, hi, 1, lo, z2, :, 1] = cos
                    inverse[z2, :, 0, h, hi, 0, lo] = cos
                    inverse[z2, :, 0, h, hi, 1, lo] = -sin
                    inverse[z2, :, 1, h, hi, 0, lo] = sin
                    inverse[z2, :, 1, h, hi, 1, lo] = cos
    forward = forward[..., SLOTS, :].reshape(256, 3, 4, 32).transpose(2, 0, 1, 3).reshape(4, 256, 96)
    inverse = inverse[:, SLOTS].reshape(3, 4, 32, 256).transpose(1, 0, 2, 3).reshape(4, 96, 256)
    return forward, inverse


def y_outer_tables(corner):
    forward = np.zeros((2, 72, GRP, 2, 8))
    inverse = np.zeros((GRP, 2, 8, 2, 72))
    g = np.arange(GRP)
    for k1 in range(8):
        cos, sin = np.cos(angle(k1, g, 8)), np.sin(angle(k1, g, 8))
        for kz in range(8):
            row = k1 * 8 + kz
            if corner and kz == 0:
                for source, target in ((0, row), (1, 64 + k1)):
                    forward[0, target, :, source, kz] = cos
                    forward[1, target, :, source, kz] = -sin
                    inverse[:, source, kz, 0, target] = cos
                    inverse[:, source, kz, 1, target] = -sin
            else:
                forward[0, row, :, 0, kz] = cos
                forward[0, row, :, 1, kz] = sin
                forward[1, row, :, 0, kz] = -sin
                forward[1, row, :, 1, kz] = cos
                inverse[:, 0, kz, 0, row] = cos
                inverse[:, 0, kz, 1, row] = -sin
                inverse[:, 1, kz, 0, row] = sin
                inverse[:, 1, kz, 1, row] = cos
    return forward.reshape(144, 128), inverse.reshape(128, 144)


def y_edge_tables():
    turn = angle(np.arange(8)[:, None], np.arange(8)[None, :] + 1, 8)
    forward = np.zeros((2, 2, 8, 8, 2))
    for ri in range(2):
        forward[ri, 0, :, :, ri] = np.cos(turn)
        forward[ri, 1, :, :, ri] = np.sin(turn)
    inverse = np.concatenate([np.cos(turn).T, np.sin(turn).T])
    return forward.reshape(32, 16).astype(np.float32), inverse.astype(np.float32)


def lane_parts():
    lane = np.arange(N)
    return lane // 16 % 4, lane % 16, lane // 64


def edge_parts():
    lane = np.arange(N)
    return lane // 8 % 4, lane // 32 % 2, lane // 64


def y_inner_tables():
    c, y, h = lane_parts()
    same = (c[:, None] == c[None, :]) & (h[:, None] == h[None, :])
    cos = np.where(same, np.cos(angle(y[:, None], y[None, :], 16)), 0.0)
    sin = np.where(same, np.sin(angle(y[:, None], y[None, :], 16)), 0.0)
    edge_c, edge_h, edge_real = edge_parts()
    meet = (edge_c[:, None] == c[None, :]) & (edge_h[:, None] == h[None, :])
    to_real = (meet & (edge_real[:, None] == 1)).astype(np.float64)
    to_imag = (meet & (edge_real[:, None] == 0)).astype(np.float64)
    forward = np.block([[cos, -sin], [sin, cos], [to_real, to_imag]])
    inverse = np.block([[cos, sin, to_real.T], [-sin, cos, to_imag.T]])
    return forward, inverse


def row_k1():
    return np.concatenate([np.repeat(np.arange(8), 8), np.arange(8)])


def twiddle_tables():
    _, y, _ = lane_parts()
    turn = angle(row_k1()[:, None], y[None, :])
    return np.stack([np.cos(turn), np.sin(turn)]).astype(np.float32)


def symbol(k):
    turn = 2.0 * np.pi * (np.asarray(k) % N) / N
    return np.stack([np.cos(turn) - 1.0, np.sin(turn)]).astype(np.float32)


def symbol_tables():
    _, k2, h = lane_parts()
    along_y = symbol(row_k1()[:, None] + 8 * k2[None, :])
    along_x = np.zeros((SLAB, 2, 8, N), np.float32)
    for s in range(SLAB):
        k = np.where(h == 0, 0, 64) if s == 0 else np.full(N, s)
        along_x[s] = np.broadcast_to(symbol(k)[:, None, :], (2, 8, N))
    along_z = np.zeros((2 * GRP, 2, 16, N), np.float32)
    for first in range(2):
        for g in range(GRP):
            for row in range(16):
                m = g * 8 + row
                if row >= 8:
                    k = np.full(N, 64)
                elif first:
                    k = np.full(N, m)
                else:
                    k = np.where(h == 0, m, 64 if m == 0 else N - m)
                along_z[first * GRP + g, :, row] = symbol(k)
    return along_x, along_y, along_z


@functools.cache
def constants():
    x_forward, x_inverse = x_tables()
    z_pairs = [z_tables(first) for first in (False, True)]
    y_pairs = [y_outer_tables(corner) for corner in (False, True)]
    inner_forward, inner_inverse = y_inner_tables()
    along_x, along_y, along_z = symbol_tables()
    return dict(
        wx=split_const(x_forward, 1),
        wxi=split_const(x_inverse, 0),
        wz=np.stack([split_const(pair[0], 2) for pair in z_pairs]),
        wzi=np.stack([split_const(pair[1], 2) for pair in z_pairs]),
        wy=np.stack([split_const(pair[0], 1) for pair in y_pairs]),
        wyi=np.stack([split_const(pair[1], 1) for pair in y_pairs]),
        wl=split_const(inner_forward, 0),
        wli=split_const(inner_inverse, 0),
        we=y_edge_tables()[0],
        wei=y_edge_tables()[1],
        tw=twiddle_tables(),
        dx=along_x,
        dy=along_y,
        dz=along_z,
    )


CONSTANTS = ("wx", "wxi", "wz", "wzi", "wy", "wyi", "wl", "wli", "we", "wei", "tw", "dx", "dy", "dz")


def thirds(value, axis):
    high = value.astype(BF16)
    low = (value - high.astype(F32)).astype(BF16)
    return jnp.concatenate([high, low, high], axis=axis)


def dot(left, right, contract):
    return lax.dot_general(left, right, (contract, ((), ())), preferred_element_type=F32)


def lanes(shape):
    return lax.broadcasted_iota(jnp.int32, shape, len(shape) - 1)


def sublanes(shape):
    return lax.broadcasted_iota(jnp.int32, shape, len(shape) - 2)


def force_lines(take):
    edge = sublanes((16, N)) == 0

    def along_x(part, z2):
        value = take(part, z2)
        return jnp.roll(value, 1, axis=1) - value

    def along_y(part, z2):
        value = take(part, z2)
        return jnp.where(edge, 0.0, jnp.roll(value, 1, axis=0)) - value

    def along_z(part, z2):
        return take(part, 0) - take(part, 1) if z2 == 1 else -take(part, 0)

    lines = []
    for z2 in range(2):
        lines += [
            along_x(0, z2) + ROOT_HALF * (along_z(4, z2) + along_y(5, z2)),
            along_y(1, z2) + ROOT_HALF * (along_z(3, z2) + along_x(5, z2)),
            along_z(2, z2) + ROOT_HALF * (along_y(3, z2) + along_x(4, z2)),
            -(along_x(6, z2) + along_y(7, z2) + along_z(8, z2)),
        ]
    lines += [ROOT_HALF * take(4, 1), ROOT_HALF * take(3, 1), take(2, 1), -take(8, 1)]
    for z2 in range(2):
        for scale, part in ((ROOT_HALF, 5), (1.0, 1), (ROOT_HALF, 3), (-1.0, 7)):
            lines.append(jnp.broadcast_to(scale * take(part, z2)[15:16], (8, N)))
    return jnp.concatenate(lines, axis=0)


def x_forward(lines, wx):
    return dot(wx, thirds(lines, 1), ((1,), (1,)))


def x_inverse(rows, wxi):
    return dot(thirds(rows.T, 1), wxi, ((1,), (0,)))


def z_forward_part(rows, wz):
    low = lanes((32, N)) < 64
    main, rest = rows[:, :N], rows[:, N:]
    parts = jnp.concatenate(
        [
            jnp.where(low, main, rest),
            jnp.where(low, jnp.roll(main, 64, axis=1), jnp.roll(rest, 96, axis=1)),
            jnp.where(low, rest, 0.0),
        ],
        axis=0,
    )
    return dot(wz, thirds(parts, 0), ((1,), (0,)))


def z_forward_end(both):
    lane = lanes((N, N))
    first, second = both[:N], both[N:]
    edge = jnp.where(lane < 96, first, jnp.roll(second, 32, axis=1))
    edge = jnp.where((lane % 8 == sublanes((N, N)) % 8) & (lane >= 64), edge, 0.0)
    return jnp.where(lane < 64, first, jnp.roll(second, 64, axis=1)), edge.reshape(16, 8, N).sum(axis=1)


def z_inverse_begin(rows, edge):
    lane = lanes((N, N))
    low = lane < 64
    edge = jnp.broadcast_to(edge[:, None, :], (16, 8, N)).reshape(N, N)
    edge = jnp.where(lane % 8 == sublanes((N, N)) % 8, edge, 0.0)
    parts = jnp.concatenate(
        [jnp.where(low, rows, edge), jnp.where(low, jnp.roll(rows, 64, axis=1), jnp.roll(edge, 96, axis=1))], axis=0
    )
    return thirds(parts, 0)


def z_inverse_part(parts, wzi):
    lane = lanes((32, N))
    low = lane < 64
    planes = dot(wzi, parts, ((1,), (0,)))
    first, second, third = planes[:32], planes[32:64], planes[64:]
    main = jnp.where(low, first, jnp.roll(second, 64, axis=1))
    rest = jnp.where(low, third, jnp.where(lane < 96, first, jnp.roll(second, 32, axis=1)))
    return jnp.concatenate([main, rest], axis=1)


def exact_dot(left, right):
    return lax.dot_general(
        left, right, (((1,), (0,)), ((), ())), precision=lax.Precision.HIGHEST, preferred_element_type=F32
    )


def y_forward(rows, edge, corner, wy, wl, we, tw):
    outer = dot(wy, thirds(rows, 0), ((1,), (0,)))
    real, imag = outer[:72], outer[72:]
    turns = exact_dot(we, edge)
    lane = lanes((8, N))
    packed = (lane % 8 == 0) & (corner == 1)
    edge_real = turns[:8] + jnp.where(packed, 0.0, turns[24:])
    edge_imag = jnp.where(packed, 0.0, turns[16:24]) - turns[8:16]
    mixed = jnp.where(lane < 64, jnp.roll(edge_imag, 64, axis=1), edge_real)
    extra = jnp.where(packed, jnp.where(lane < 64, -jnp.roll(turns[24:], 64, axis=1), turns[16:24]), 0.0)
    spread = jnp.broadcast_to(mixed[:, None, :], (8, 8, N)).reshape(64, N)
    spread = jnp.where(lanes((64, N)) % 8 == sublanes((64, N)) % 8, spread, 0.0)
    turned = jnp.concatenate(
        [real * tw[0] + imag * tw[1], imag * tw[0] - real * tw[1], jnp.concatenate([spread, extra], axis=0)], axis=1
    )
    inner = dot(thirds(turned, 1), wl, ((1,), (0,)))
    return inner[:, :N], inner[:, N:]


def y_inverse(real, imag, corner, wyi, wli, wei, tw):
    inner = dot(thirds(jnp.concatenate([real, imag], axis=1), 1), wli, ((1,), (0,)))
    real, imag, mixed = inner[:, :N], inner[:, N : 2 * N], inner[:, 2 * N :]
    turned = jnp.concatenate([real * tw[0] - imag * tw[1], imag * tw[0] + real * tw[1]], axis=0)
    rows = dot(wyi, thirds(turned, 0), ((1,), (0,)))
    lane = lanes((8, N))
    packed = (lane % 8 == 0) & (corner == 1)
    spread = jnp.where(lanes((64, N)) % 8 == sublanes((64, N)) % 8, mixed[:64], 0.0)
    turns = exact_dot(wei, jnp.concatenate([spread.reshape(8, 8, N).sum(axis=1), mixed[64:]], axis=1))
    edge_real = turns[:8, :N] - jnp.roll(turns[8:, :N], 64, axis=1)
    edge_imag = turns[8:, :N] + jnp.roll(turns[:8, :N], 64, axis=1)
    extra = turns[:8, N:] - jnp.roll(turns[8:, N:], 64, axis=1)
    return rows, edge_real, jnp.where(packed, extra, edge_imag)


def gradients(lines):
    last = sublanes((16, N)) == 15
    grad_x, grad_y, grad_z = [], [], []
    for c in range(4):
        along = [[], [], []]
        for z2 in range(2):
            start = z2 * 64 + c * 16
            value = lines[start : start + 16]
            above = lines[start + 64 : start + 80]
            begin = 192 + z2 * 32 + c * 8
            edge = jnp.sum(lines[begin : begin + 8], axis=0, keepdims=True)
            along[0].append(jnp.roll(value, N - 1, axis=1) - value)
            along[1].append(jnp.where(last, edge, jnp.roll(value, 15, axis=0)) - value)
            along[2].append(above - value)
        for grad, pair in zip((grad_x, grad_y, grad_z), along):
            grad.append(jnp.concatenate(pair, axis=0))
    return [
        grad_x[0],
        grad_y[1],
        grad_z[2],
        ROOT_HALF * (grad_y[2] + grad_z[1]),
        ROOT_HALF * (grad_x[2] + grad_z[0]),
        ROOT_HALF * (grad_x[1] + grad_y[0]),
        -grad_x[3],
        -grad_y[3],
        -grad_z[3],
    ]


def operator_tables(dx, dy, dz):
    def rows(main, extra):
        return jnp.concatenate([main] * 8 + [extra], axis=0)

    along_x = [rows(dx[i], dx[i]) for i in range(2)]
    along_z = [rows(dz[i][:8], dz[i][8:]) for i in range(2)]
    along_y = [dy[0], dy[1]]
    squares = (
        along_x[0] * along_x[0]
        + along_x[1] * along_x[1]
        + (along_y[0] * along_y[0] + along_y[1] * along_y[1])
        + (along_z[0] * along_z[0] + along_z[1] * along_z[1])
    )
    some = squares > 0.0
    inverse = jnp.where(some, 1.0 / jnp.where(some, squares, 1.0), 0.0)
    part = lanes(squares.shape) // 16 % 4
    own = [
        jnp.where(part == 0, along_x[i], jnp.where(part == 1, along_y[i], jnp.where(part == 2, along_z[i], 0.0)))
        for i in range(2)
    ]
    scale = 1.0 / (N * N * N)
    alpha = inverse * jnp.where(part == 3, scale / 0.8, scale / 1.5)
    beta = inverse * inverse * (scale / 3.0)
    return own[0], own[1], alpha, beta


def operator(real, imag, own_real, own_imag, alpha, beta):
    projected = []
    lane = lanes(real.shape)
    for value in (own_real * real + own_imag * imag, own_real * imag - own_imag * real):
        for width in (32, 16):
            lower = lane % (2 * width) < width
            value = value + jnp.where(lower, jnp.roll(value, N - width, axis=1), jnp.roll(value, width, axis=1))
        projected.append(value * beta)
    return (
        real * alpha - (own_real * projected[0] - own_imag * projected[1]),
        imag * alpha - (own_real * projected[1] + own_imag * projected[0]),
    )


def kernel(adjoint, source, contrast_in, phase_in, grain_in, orientation_in, *rest):
    tables = dict(zip(CONSTANTS, rest[: len(CONSTANTS)]))
    (
        out,
        wx, wxi, wz, wzi, wy, wyi, wl, wli, we, wei, tw, dx, dy, dz,
        fields, right_side, contrast, phase, grain, orientation,
        send1, recv1, send2, recv2, send3, recv3, send4, recv4,
        edge2_out, edge2_in, edge3_out, edge3_in,
        coef, own_real, own_imag, alpha, beta,
        load_sems, send_sems, recv_sems, slab_send, slab_recv,
    ) = rest[len(CONSTANTS):]
    g = lax.axis_index("grp")
    s = lax.axis_index("slab")
    first = jnp.where(s == 0, 1, 0)
    corner = jnp.where((s == 0) & (g == 0), 1, 0)

    pairs = [
        (adjoint, fields),
        (tables["wx"], wx),
        (orientation_in, orientation),
        (grain_in, grain),
        (phase_in, phase),
        (contrast_in, contrast),
        (tables["wz"].at[first], wz),
        (tables["dx"].at[s], dx),
        (tables["dy"], dy),
        (tables["dz"].at[first * GRP + g], dz),
        (tables["wy"].at[corner], wy),
        (tables["wl"], wl),
        (tables["we"], we),
        (tables["tw"], tw),
        (tables["wli"], wli),
        (tables["wyi"].at[corner], wyi),
        (tables["wei"], wei),
        (tables["wzi"].at[first], wzi),
        (tables["wxi"], wxi),
        (source, right_side),
    ]
    loads = [pltpu.make_async_copy(*pair, load_sems.at[i]) for i, pair in enumerate(pairs)]
    for load in loads:
        load.start()

    digit_y, digit_z, digit_x = s // 16, lax.rem(s // 4, 4), lax.rem(s, 4)

    my_slot = digit_z * 16 + digit_y * 4 + digit_x
    core = lax.rem(g, 2)

    def slab_peers(visit, steps_z):
        places = [lax.rem(digit_z + step_z, 4) for step_z in steps_z]

        def row(step_y, carry):
            y = lax.rem(digit_y + (step_y + 2 if steps_z != (0,) else step_y), 4)
            for step_x in (2, 1, 3, 0):
                x = lax.rem(digit_x + step_x, 4)
                for place in places:
                    visit(y * 16 + place * 4 + x, place * 16 + y * 4 + x)
            return carry

        if steps_z == (0,):
            for step_x in range(1, 4):
                x = lax.rem(digit_x + step_x, 4)
                visit(digit_y * 16 + digit_z * 4 + x, digit_z * 16 + digit_y * 4 + x)
        lax.fori_loop(1 if steps_z == (0,) else 0, 4, row, 0)

    def grp_peers(visit):
        def one(step, carry):
            visit(lax.rem(g + step, GRP))
            return carry

        lax.fori_loop(1, GRP, one, 0)

    barrier = pltpu.get_barrier_semaphore()
    for steps_z in ((2,), (1, 3), (0,)):
        slab_peers(
            lambda peer, slot: pl.semaphore_signal(barrier, inc=1, device_id={"slab": peer}, device_id_type=MESH),
            steps_z,
        )
    grp_peers(lambda peer: pl.semaphore_signal(barrier, inc=1, device_id={"grp": peer}, device_id_type=MESH))

    def send_slab(sent, landed, which, steps_z):
        sem = which * 3 + steps_z[0]

        def start(peer, slot):
            pltpu.make_async_remote_copy(
                sent.at[slot], landed.at[my_slot], slab_send.at[sem], slab_recv.at[sem],
                device_id={"slab": peer}, device_id_type=MESH,
            ).start()

        slab_peers(start, steps_z)

    def exchange_grp(sent, landed, sem):
        def start(peer):
            pltpu.make_async_remote_copy(
                sent.at[peer], landed.at[g], send_sems.at[sem], recv_sems.at[sem],
                device_id={"grp": peer}, device_id_type=MESH,
            ).start()

        grp_peers(start)
        landed[g] = sent[g]

    def finish(buffer, sem, count):
        block = buffer.at[pl.ds(0, count)]
        pltpu.make_async_copy(block, block, sem).wait()

    loads[0].wait()
    lines = force_lines(lambda part, z2: fields[part, pl.ds(z2, 16, stride=2), :])
    loads[1].wait()
    send1[...] = x_forward(lines, wx[...]).reshape(SLAB, 2, 2 * N)
    pl.semaphore_wait(barrier, SLAB - 1 + GRP - 1)

    send_slab(send1, recv1, 0, (2,))

    for load in loads[2:6]:
        load.wait()
    ids = jnp.concatenate([grain[pl.ds(z2, 16, stride=2), :] for z2 in range(2)], axis=0)
    high, low = ids // N, ids % N
    entry = jnp.zeros((32, N), jnp.int32)
    for row in range(32):
        line = jnp.broadcast_to(orientation[row : row + 1, :], (32, N))
        entry = jnp.where(high == row, jnp.take_along_axis(line, low, axis=1), entry)
    ceramic = jnp.concatenate([phase[pl.ds(z2, 16, stride=2), :] for z2 in range(2)], axis=0) == 1
    entry = jnp.where(ceramic, entry, 6)

    @pl.when(core == 0)
    def _():
        send_slab(send1, recv1, 0, (1, 3))

    masks = [entry == t for t in range(6)]
    for pair in range(81):
        value = jnp.full((32, N), contrast[pair // 9, 6, pair % 9], F32)
        for t in range(6):
            value = jnp.where(masks[t], contrast[pair // 9, t, pair % 9], value)
        coef[pair] = value

    @pl.when(core == 1)
    def _():
        send_slab(send1, recv1, 0, (1, 3))

    send_slab(send1, recv1, 0, (0,))
    recv1[my_slot] = send1[my_slot]
    for load in loads[6:]:
        load.wait()
    own_real[...], own_imag[...], alpha[...], beta[...] = operator_tables(dx, dy, dz)

    def part1(step_z):
        place = lax.rem(digit_z + step_z, 4)
        return z_forward_part(recv1[pl.ds(place * 16, 16)].reshape(32, 2 * N), wz[place])

    finish(recv1, slab_recv.at[0], 15)
    total = part1(0)
    finish(recv1, slab_recv.at[1], 32)
    total = total + part1(1) + part1(3)
    finish(recv1, slab_recv.at[2], 16)
    rows, edge = z_forward_end(total + part1(2))
    send2[...] = rows.reshape(GRP, 16, N)
    exchange_grp(send2, recv2, 0)
    edge2_out[...] = edge.reshape(GRP, 2, N)
    exchange_grp(edge2_out, edge2_in, 1)

    finish(recv2, recv_sems.at[0], GRP - 1)
    finish(edge2_in, recv_sems.at[1], GRP - 1)
    real, imag = y_forward(
        recv2[...].reshape(N, N), edge2_in[...].reshape(16, N), corner, wy[...], wl[...], we[...], tw
    )
    real, imag = operator(real, imag, own_real[...], own_imag[...], alpha[...], beta[...])
    rows, edge_real, edge_imag = y_inverse(real, imag, corner, wyi[...], wli[...], wei[...], tw)
    send3[...] = rows.reshape(GRP, 16, N)
    exchange_grp(send3, recv3, 2)
    edge3_out[:, 0:1, :] = edge_real.reshape(GRP, 1, N)
    edge3_out[:, 1:2, :] = edge_imag.reshape(GRP, 1, N)
    exchange_grp(edge3_out, edge3_in, 3)

    finish(recv3, recv_sems.at[2], GRP - 1)
    finish(edge3_in, recv_sems.at[3], GRP - 1)
    parts = z_inverse_begin(recv3[...].reshape(N, N), edge3_in[...].reshape(16, N))

    def part4(step_z):
        place = lax.rem(digit_z + step_z, 4)
        send4[pl.ds(place * 16, 16)] = z_inverse_part(parts, wzi[place]).reshape(16, 2, 2 * N)

    part4(2)
    send_slab(send4, recv4, 1, (2,))
    part4(1)
    part4(3)
    finish(send4, slab_send.at[5], 16)
    send_slab(send4, recv4, 1, (1, 3))
    part4(0)
    send_slab(send4, recv4, 1, (0,))
    recv4[my_slot] = send4[my_slot]

    for sem, count in ((3, 15), (4, 32), (5, 16)):
        finish(recv4, slab_recv.at[sem], count)
    green = gradients(x_inverse(recv4[...].reshape(N, 2 * N), wxi[...]))
    for i in range(9):
        total = jnp.concatenate([right_side[i, pl.ds(z2, 16, stride=2), :] for z2 in range(2)], axis=0)
        for j in range(9):
            total = total - coef[j * 9 + i] * green[j]
        for z2 in range(2):
            out[i, pl.ds(z2, 16, stride=2), :] = total[z2 * 16 : z2 * 16 + 16]

    for which, sent in enumerate((send1, send4)):
        for sem, count in enumerate((15, 32)):
            finish(sent, slab_send.at[which * 3 + sem], count)
    finish(send1, slab_send.at[2], 16)
    for sem, sent in enumerate((send2, edge2_out, send3, edge3_out)):
        finish(sent, send_sems.at[sem], GRP - 1)


def per_device(adjoint, source, contrast, phase_id, grain_id, orientation):
    table = constants()
    vmem = pl.BlockSpec(memory_space=pltpu.VMEM)
    hbm = pl.BlockSpec(memory_space=pltpu.HBM)
    flat = (9, 32, N)
    result = pl.pallas_call(
        kernel,
        out_shape=pltpu.VMEM(flat, F32),
        in_specs=[hbm] * (6 + len(CONSTANTS)),
        out_specs=vmem,
        scratch_shapes=[
            pltpu.VMEM((128, 384), BF16),
            pltpu.VMEM((384, 128), BF16),
            pltpu.VMEM((4, 256, 288), BF16),
            pltpu.VMEM((4, 96, 768), BF16),
            pltpu.VMEM((144, 384), BF16),
            pltpu.VMEM((128, 432), BF16),
            pltpu.VMEM((1152, 256), BF16),
            pltpu.VMEM((768, 384), BF16),
            pltpu.VMEM((32, 16), F32),
            pltpu.VMEM((16, 8), F32),
            pltpu.VMEM((2, 72, N), F32),
            pltpu.VMEM((2, 8, N), F32),
            pltpu.VMEM((2, 72, N), F32),
            pltpu.VMEM((2, 16, N), F32),
            pltpu.VMEM(flat, F32),
            pltpu.VMEM(flat, F32),
            pltpu.SMEM((9, 7, 9), F32),
            pltpu.VMEM((32, N), jnp.int32),
            pltpu.VMEM((32, N), jnp.int32),
            pltpu.VMEM((32, N), jnp.int32),
            pltpu.VMEM((SLAB, 2, 2 * N), F32),
            pltpu.VMEM((SLAB, 2, 2 * N), F32),
            pltpu.VMEM((GRP, 16, N), F32),
            pltpu.VMEM((GRP, 16, N), F32),
            pltpu.VMEM((GRP, 16, N), F32),
            pltpu.VMEM((GRP, 16, N), F32),
            pltpu.VMEM((SLAB, 2, 2 * N), F32),
            pltpu.VMEM((SLAB, 2, 2 * N), F32),
            pltpu.VMEM((GRP, 2, N), F32),
            pltpu.VMEM((GRP, 2, N), F32),
            pltpu.VMEM((GRP, 2, N), F32),
            pltpu.VMEM((GRP, 2, N), F32),
            pltpu.VMEM((81, 32, N), F32),
            pltpu.VMEM((72, N), F32),
            pltpu.VMEM((72, N), F32),
            pltpu.VMEM((72, N), F32),
            pltpu.VMEM((72, N), F32),
            pltpu.SemaphoreType.DMA((20,)),
            pltpu.SemaphoreType.DMA((4,)),
            pltpu.SemaphoreType.DMA((4,)),
            pltpu.SemaphoreType.DMA((6,)),
            pltpu.SemaphoreType.DMA((6,)),
        ],
        compiler_params=pltpu.CompilerParams(
            collective_id=0, has_side_effects=True, vmem_limit_bytes=60 * 1024 * 1024
        ),
    )(
        adjoint.reshape(flat),
        source.reshape(flat),
        contrast.transpose(1, 0, 2),
        phase_id.reshape(32, N),
        grain_id.reshape(32, N),
        orientation.reshape(32, N),
        *[jnp.asarray(table[name]) for name in CONSTANTS],
    )
    return result.reshape(adjoint.shape)


def solution(mesh):
    placed = (
        P(None, "grp", "slab", None),
        P(None, "grp", "slab", None),
        P(),
        P("grp", "slab", None),
        P("grp", "slab", None),
        P(),
    )
    return jax.shard_map(
        per_device,
        mesh=mesh,
        in_specs=placed,
        out_specs=P(None, "grp", "slab", None),
        check_vma=False,
    )
```

```python
import functools

import jax
import jax.numpy as jnp
import ml_dtypes
import numpy as np
from jax import lax
from jax.experimental import pallas as pl
from jax.experimental.pallas import tpu as pltpu
from jax.sharding import PartitionSpec as P

N = 128
GRP = 8
SLAB = 64
F32 = jnp.float32
BF16 = jnp.bfloat16
ROOT_HALF = float(np.sqrt(0.5))
MESH = pl.DeviceIdType.MESH
SLOTS = np.arange(SLAB).reshape(4, 4, 4).transpose(1, 0, 2).reshape(SLAB)


def split_const(matrix, axis):
    high = matrix.astype(ml_dtypes.bfloat16)
    low = (matrix - high.astype(np.float64)).astype(ml_dtypes.bfloat16)
    return np.concatenate([high, high, low], axis=axis)


def angle(a, b, length=N):
    return 2.0 * np.pi * ((np.asarray(a) * np.asarray(b)) % length) / length


def x_tables():
    x = np.arange(N)
    forward = np.zeros((SLAB, 2, N))
    inverse = np.zeros((SLAB, 2, N))
    for k in range(1, SLAB):
        forward[k, 0] = np.cos(angle(k, x))
        forward[k, 1] = -np.sin(angle(k, x))
    forward[0, 0] = 1.0
    forward[0, 1] = (-1.0) ** x
    inverse[1:] = 2.0 * forward[1:]
    inverse[0] = forward[0]
    return forward[SLOTS].reshape(N, N), inverse[SLOTS].reshape(N, N)


def z_tables(first):
    z = (2 * np.arange(SLAB)[:, None] + np.arange(3)[None, :]) % N
    forward = np.zeros((2, GRP, 2, 8, 3, SLAB, 2))
    inverse = np.zeros((3, SLAB, 2, 2, GRP, 2, 8))
    for m in range(SLAB):
        hi, lo = divmod(m, 8)
        for h in range(2):
            for z2 in range(3):
                if first:
                    cos, sin = np.cos(angle(m, z[:, z2])), np.sin(angle(m, z[:, z2]))
                    if m == 0:
                        alt = (-1.0) ** z[:, z2]
                        forward[h, hi, 0, lo, z2, :, h] = 1.0
                        forward[h, hi, 1, lo, z2, :, h] = alt
                        inverse[z2, :, h, h, hi, 0, lo] = 1.0
                        inverse[z2, :, h, h, hi, 1, lo] = alt
                    else:
                        forward[h, hi, 0, lo, z2, :, h] = cos
                        forward[h, hi, 1, lo, z2, :, h] = -sin
                        inverse[z2, :, h, h, hi, 0, lo] = 2.0 * cos
                        inverse[z2, :, h, h, hi, 1, lo] = -2.0 * sin
                else:
                    k = m if h == 0 else (64 if m == 0 else N - m)
                    cos, sin = np.cos(angle(k, z[:, z2])), np.sin(angle(k, z[:, z2]))
                    forward[h, hi, 0, lo, z2, :, 0] = cos
                    forward[h, hi, 0, lo, z2, :, 1] = sin
                    forward[h, hi, 1, lo, z2, :, 0] = -sin
                    forward[h, hi, 1, lo, z2, :, 1] = cos
                    inverse[z2, :, 0, h, hi, 0, lo] = cos
                    inverse[z2, :, 0, h, hi, 1, lo] = -sin
                    inverse[z2, :, 1, h, hi, 0, lo] = sin
                    inverse[z2, :, 1, h, hi, 1, lo] = cos
    forward = forward[..., SLOTS, :].reshape(256, 3, 4, 32).transpose(2, 0, 1, 3).reshape(4, 256, 96)
    inverse = inverse[:, SLOTS].reshape(3, 4, 32, 256).transpose(1, 0, 2, 3).reshape(4, 96, 256)
    return forward, inverse


def y_outer_tables(corner):
    forward = np.zeros((2, 72, GRP, 2, 8))
    inverse = np.zeros((GRP, 2, 8, 2, 72))
    g = np.arange(GRP)
    for k1 in range(8):
        cos, sin = np.cos(angle(k1, g, 8)), np.sin(angle(k1, g, 8))
        for kz in range(8):
            row = k1 * 8 + kz
            if corner and kz == 0:
                for source, target in ((0, row), (1, 64 + k1)):
                    forward[0, target, :, source, kz] = cos
                    forward[1, target, :, source, kz] = -sin
                    inverse[:, source, kz, 0, target] = cos
                    inverse[:, source, kz, 1, target] = -sin
            else:
                forward[0, row, :, 0, kz] = cos
                forward[0, row, :, 1, kz] = sin
                forward[1, row, :, 0, kz] = -sin
                forward[1, row, :, 1, kz] = cos
                inverse[:, 0, kz, 0, row] = cos
                inverse[:, 0, kz, 1, row] = -sin
                inverse[:, 1, kz, 0, row] = sin
                inverse[:, 1, kz, 1, row] = cos
    return forward.reshape(144, 128), inverse.reshape(128, 144)


def y_edge_tables():
    turn = angle(np.arange(8)[:, None], np.arange(8)[None, :] + 1, 8)
    forward = np.zeros((2, 2, 8, 8, 2))
    for ri in range(2):
        forward[ri, 0, :, :, ri] = np.cos(turn)
        forward[ri, 1, :, :, ri] = np.sin(turn)
    inverse = np.concatenate([np.cos(turn).T, np.sin(turn).T])
    return forward.reshape(32, 16).astype(np.float32), inverse.astype(np.float32)


def lane_parts():
    lane = np.arange(N)
    return lane // 16 % 4, lane % 16, lane // 64


def edge_parts():
    lane = np.arange(N)
    return lane // 8 % 4, lane // 32 % 2, lane // 64


def y_inner_tables():
    c, y, h = lane_parts()
    same = (c[:, None] == c[None, :]) & (h[:, None] == h[None, :])
    cos = np.where(same, np.cos(angle(y[:, None], y[None, :], 16)), 0.0)
    sin = np.where(same, np.sin(angle(y[:, None], y[None, :], 16)), 0.0)
    edge_c, edge_h, edge_real = edge_parts()
    meet = (edge_c[:, None] == c[None, :]) & (edge_h[:, None] == h[None, :])
    to_real = (meet & (edge_real[:, None] == 1)).astype(np.float64)
    to_imag = (meet & (edge_real[:, None] == 0)).astype(np.float64)
    forward = np.block([[cos, -sin], [sin, cos], [to_real, to_imag]])
    inverse = np.block([[cos, sin, to_real.T], [-sin, cos, to_imag.T]])
    return forward, inverse


def row_k1():
    return np.concatenate([np.repeat(np.arange(8), 8), np.arange(8)])


def twiddle_tables():
    _, y, _ = lane_parts()
    turn = angle(row_k1()[:, None], y[None, :])
    return np.stack([np.cos(turn), np.sin(turn)]).astype(np.float32)


def symbol(k):
    turn = 2.0 * np.pi * (np.asarray(k) % N) / N
    return np.stack([np.cos(turn) - 1.0, np.sin(turn)]).astype(np.float32)


def symbol_tables():
    _, k2, h = lane_parts()
    along_y = symbol(row_k1()[:, None] + 8 * k2[None, :])
    along_x = np.zeros((SLAB, 2, 8, N), np.float32)
    for s in range(SLAB):
        k = np.where(h == 0, 0, 64) if s == 0 else np.full(N, s)
        along_x[s] = np.broadcast_to(symbol(k)[:, None, :], (2, 8, N))
    along_z = np.zeros((2 * GRP, 2, 16, N), np.float32)
    for first in range(2):
        for g in range(GRP):
            for row in range(16):
                m = g * 8 + row
                if row >= 8:
                    k = np.full(N, 64)
                elif first:
                    k = np.full(N, m)
                else:
                    k = np.where(h == 0, m, 64 if m == 0 else N - m)
                along_z[first * GRP + g, :, row] = symbol(k)
    return along_x, along_y, along_z


@functools.cache
def constants():
    x_forward, x_inverse = x_tables()
    z_pairs = [z_tables(first) for first in (False, True)]
    y_pairs = [y_outer_tables(corner) for corner in (False, True)]
    inner_forward, inner_inverse = y_inner_tables()
    along_x, along_y, along_z = symbol_tables()
    return dict(
        wx=split_const(x_forward, 1),
        wxi=split_const(x_inverse, 0),
        wz=np.stack([split_const(pair[0], 2) for pair in z_pairs]),
        wzi=np.stack([split_const(pair[1], 2) for pair in z_pairs]),
        wy=np.stack([split_const(pair[0], 1) for pair in y_pairs]),
        wyi=np.stack([split_const(pair[1], 1) for pair in y_pairs]),
        wl=split_const(inner_forward, 0),
        wli=split_const(inner_inverse, 0),
        we=y_edge_tables()[0],
        wei=y_edge_tables()[1],
        tw=twiddle_tables(),
        dx=along_x,
        dy=along_y,
        dz=along_z,
    )


CONSTANTS = ("wx", "wxi", "wz", "wzi", "wy", "wyi", "wl", "wli", "we", "wei", "tw", "dx", "dy", "dz")


def thirds(value, axis):
    high = value.astype(BF16)
    low = (value - high.astype(F32)).astype(BF16)
    return jnp.concatenate([high, low, high], axis=axis)


def dot(left, right, contract):
    return lax.dot_general(left, right, (contract, ((), ())), preferred_element_type=F32)


def lanes(shape):
    return lax.broadcasted_iota(jnp.int32, shape, len(shape) - 1)


def sublanes(shape):
    return lax.broadcasted_iota(jnp.int32, shape, len(shape) - 2)


def force_lines(take):
    edge = sublanes((16, N)) == 0

    def along_x(part, z2):
        value = take(part, z2)
        return jnp.roll(value, 1, axis=1) - value

    def along_y(part, z2):
        value = take(part, z2)
        return jnp.where(edge, 0.0, jnp.roll(value, 1, axis=0)) - value

    def along_z(part, z2):
        return take(part, 0) - take(part, 1) if z2 == 1 else -take(part, 0)

    lines = []
    for z2 in range(2):
        lines += [
            along_x(0, z2) + ROOT_HALF * (along_z(4, z2) + along_y(5, z2)),
            along_y(1, z2) + ROOT_HALF * (along_z(3, z2) + along_x(5, z2)),
            along_z(2, z2) + ROOT_HALF * (along_y(3, z2) + along_x(4, z2)),
            -(along_x(6, z2) + along_y(7, z2) + along_z(8, z2)),
        ]
    lines += [ROOT_HALF * take(4, 1), ROOT_HALF * take(3, 1), take(2, 1), -take(8, 1)]
    for z2 in range(2):
        for scale, part in ((ROOT_HALF, 5), (1.0, 1), (ROOT_HALF, 3), (-1.0, 7)):
            lines.append(jnp.broadcast_to(scale * take(part, z2)[15:16], (8, N)))
    return jnp.concatenate(lines, axis=0)


def x_forward(lines, wx):
    return dot(wx, thirds(lines, 1), ((1,), (1,)))


def x_inverse(rows, wxi):
    return dot(thirds(rows.T, 1), wxi, ((1,), (0,)))


def z_forward_part(rows, wz):
    low = lanes((32, N)) < 64
    main, rest = rows[:, :N], rows[:, N:]
    parts = jnp.concatenate(
        [
            jnp.where(low, main, rest),
            jnp.where(low, jnp.roll(main, 64, axis=1), jnp.roll(rest, 96, axis=1)),
            jnp.where(low, rest, 0.0),
        ],
        axis=0,
    )
    return dot(wz, thirds(parts, 0), ((1,), (0,)))


def z_forward_end(both):
    lane = lanes((N, N))
    first, second = both[:N], both[N:]
    edge = jnp.where(lane < 96, first, jnp.roll(second, 32, axis=1))
    edge = jnp.where((lane % 8 == sublanes((N, N)) % 8) & (lane >= 64), edge, 0.0)
    return jnp.where(lane < 64, first, jnp.roll(second, 64, axis=1)), edge.reshape(16, 8, N).sum(axis=1)


def z_inverse_begin(rows, edge):
    lane = lanes((N, N))
    low = lane < 64
    edge = jnp.broadcast_to(edge[:, None, :], (16, 8, N)).reshape(N, N)
    edge = jnp.where(lane % 8 == sublanes((N, N)) % 8, edge, 0.0)
    parts = jnp.concatenate(
        [jnp.where(low, rows, edge), jnp.where(low, jnp.roll(rows, 64, axis=1), jnp.roll(edge, 96, axis=1))], axis=0
    )
    return thirds(parts, 0)


def z_inverse_part(parts, wzi):
    lane = lanes((32, N))
    low = lane < 64
    planes = dot(wzi, parts, ((1,), (0,)))
    first, second, third = planes[:32], planes[32:64], planes[64:]
    main = jnp.where(low, first, jnp.roll(second, 64, axis=1))
    rest = jnp.where(low, third, jnp.where(lane < 96, first, jnp.roll(second, 32, axis=1)))
    return jnp.concatenate([main, rest], axis=1)


def exact_dot(left, right):
    return lax.dot_general(
        left, right, (((1,), (0,)), ((), ())), precision=lax.Precision.HIGHEST, preferred_element_type=F32
    )


def y_forward(rows, edge, corner, wy, wl, we, tw):
    outer = dot(wy, thirds(rows, 0), ((1,), (0,)))
    real, imag = outer[:72], outer[72:]
    turns = exact_dot(we, edge)
    lane = lanes((8, N))
    packed = (lane % 8 == 0) & (corner == 1)
    edge_real = turns[:8] + jnp.where(packed, 0.0, turns[24:])
    edge_imag = jnp.where(packed, 0.0, turns[16:24]) - turns[8:16]
    mixed = jnp.where(lane < 64, jnp.roll(edge_imag, 64, axis=1), edge_real)
    extra = jnp.where(packed, jnp.where(lane < 64, -jnp.roll(turns[24:], 64, axis=1), turns[16:24]), 0.0)
    spread = jnp.broadcast_to(mixed[:, None, :], (8, 8, N)).reshape(64, N)
    spread = jnp.where(lanes((64, N)) % 8 == sublanes((64, N)) % 8, spread, 0.0)
    turned = jnp.concatenate(
        [real * tw[0] + imag * tw[1], imag * tw[0] - real * tw[1], jnp.concatenate([spread, extra], axis=0)], axis=1
    )
    inner = dot(thirds(turned, 1), wl, ((1,), (0,)))
    return inner[:, :N], inner[:, N:]


def y_inverse(real, imag, corner, wyi, wli, wei, tw):
    inner = dot(thirds(jnp.concatenate([real, imag], axis=1), 1), wli, ((1,), (0,)))
    real, imag, mixed = inner[:, :N], inner[:, N : 2 * N], inner[:, 2 * N :]
    turned = jnp.concatenate([real * tw[0] - imag * tw[1], imag * tw[0] + real * tw[1]], axis=0)
    rows = dot(wyi, thirds(turned, 0), ((1,), (0,)))
    lane = lanes((8, N))
    packed = (lane % 8 == 0) & (corner == 1)
    spread = jnp.where(lanes((64, N)) % 8 == sublanes((64, N)) % 8, mixed[:64], 0.0)
    turns = exact_dot(wei, jnp.concatenate([spread.reshape(8, 8, N).sum(axis=1), mixed[64:]], axis=1))
    edge_real = turns[:8, :N] - jnp.roll(turns[8:, :N], 64, axis=1)
    edge_imag = turns[8:, :N] + jnp.roll(turns[:8, :N], 64, axis=1)
    extra = turns[:8, N:] - jnp.roll(turns[8:, N:], 64, axis=1)
    return rows, edge_real, jnp.where(packed, extra, edge_imag)


def gradients(lines):
    last = sublanes((16, N)) == 15
    grad_x, grad_y, grad_z = [], [], []
    for c in range(4):
        along = [[], [], []]
        for z2 in range(2):
            start = z2 * 64 + c * 16
            value = lines[start : start + 16]
            above = lines[start + 64 : start + 80]
            begin = 192 + z2 * 32 + c * 8
            edge = jnp.sum(lines[begin : begin + 8], axis=0, keepdims=True)
            along[0].append(jnp.roll(value, N - 1, axis=1) - value)
            along[1].append(jnp.where(last, edge, jnp.roll(value, 15, axis=0)) - value)
            along[2].append(above - value)
        for grad, pair in zip((grad_x, grad_y, grad_z), along):
            grad.append(jnp.concatenate(pair, axis=0))
    return [
        grad_x[0],
        grad_y[1],
        grad_z[2],
        ROOT_HALF * (grad_y[2] + grad_z[1]),
        ROOT_HALF * (grad_x[2] + grad_z[0]),
        ROOT_HALF * (grad_x[1] + grad_y[0]),
        -grad_x[3],
        -grad_y[3],
        -grad_z[3],
    ]


def operator_tables(dx, dy, dz):
    def rows(main, extra):
        return jnp.concatenate([main] * 8 + [extra], axis=0)

    along_x = [rows(dx[i], dx[i]) for i in range(2)]
    along_z = [rows(dz[i][:8], dz[i][8:]) for i in range(2)]
    along_y = [dy[0], dy[1]]
    squares = (
        along_x[0] * along_x[0]
        + along_x[1] * along_x[1]
        + (along_y[0] * along_y[0] + along_y[1] * along_y[1])
        + (along_z[0] * along_z[0] + along_z[1] * along_z[1])
    )
    some = squares > 0.0
    inverse = jnp.where(some, 1.0 / jnp.where(some, squares, 1.0), 0.0)
    part = lanes(squares.shape) // 16 % 4
    own = [
        jnp.where(part == 0, along_x[i], jnp.where(part == 1, along_y[i], jnp.where(part == 2, along_z[i], 0.0)))
        for i in range(2)
    ]
    scale = 1.0 / (N * N * N)
    alpha = inverse * jnp.where(part == 3, scale / 0.8, scale / 1.5)
    beta = inverse * inverse * (scale / 3.0)
    return own[0], own[1], alpha, beta


def operator(real, imag, own_real, own_imag, alpha, beta):
    projected = []
    lane = lanes(real.shape)
    for value in (own_real * real + own_imag * imag, own_real * imag - own_imag * real):
        for width in (32, 16):
            lower = lane % (2 * width) < width
            value = value + jnp.where(lower, jnp.roll(value, N - width, axis=1), jnp.roll(value, width, axis=1))
        projected.append(value * beta)
    return (
        real * alpha - (own_real * projected[0] - own_imag * projected[1]),
        imag * alpha - (own_real * projected[1] + own_imag * projected[0]),
    )


def kernel(adjoint, source, contrast_in, phase_in, grain_in, orientation_in, *rest):
    tables = dict(zip(CONSTANTS, rest[: len(CONSTANTS)]))
    (
        out,
        wx, wxi, wz, wzi, wy, wyi, wl, wli, we, wei, tw, dx, dy, dz,
        fields, right_side, contrast, phase, grain, orientation,
        send1, recv1, send2, recv2, send3, recv3, send4, recv4,
        edge2_out, edge2_in, edge3_out, edge3_in,
        coef, own_real, own_imag, alpha, beta,
        load_sems, send_sems, recv_sems, slab_send, slab_recv,
    ) = rest[len(CONSTANTS):]
    g = lax.axis_index("grp")
    s = lax.axis_index("slab")
    first = jnp.where(s == 0, 1, 0)
    corner = jnp.where((s == 0) & (g == 0), 1, 0)

    pairs = [
        (adjoint, fields),
        (tables["wx"], wx),
        (orientation_in, orientation),
        (grain_in, grain),
        (phase_in, phase),
        (contrast_in, contrast),
        (tables["wz"].at[first], wz),
        (tables["dx"].at[s], dx),
        (tables["dy"], dy),
        (tables["dz"].at[first * GRP + g], dz),
        (tables["wy"].at[corner], wy),
        (tables["wl"], wl),
        (tables["we"], we),
        (tables["tw"], tw),
        (tables["wli"], wli),
        (tables["wyi"].at[corner], wyi),
        (tables["wei"], wei),
        (tables["wzi"].at[first], wzi),
        (tables["wxi"], wxi),
        (source, right_side),
    ]
    loads = [pltpu.make_async_copy(*pair, load_sems.at[i]) for i, pair in enumerate(pairs)]
    for load in loads:
        load.start()

    digit_y, digit_z, digit_x = s // 16, lax.rem(s // 4, 4), lax.rem(s, 4)

    my_slot = digit_z * 16 + digit_y * 4 + digit_x
    core = lax.rem(g, 2)

    def slab_peers(visit, steps_z):
        places = [lax.rem(digit_z + step_z, 4) for step_z in steps_z]

        def row(step_y, carry):
            y = lax.rem(digit_y + (step_y + 2 if steps_z != (0,) else step_y), 4)
            for step_x in (2, 1, 3, 0):
                x = lax.rem(digit_x + step_x, 4)
                for place in places:
                    visit(y * 16 + place * 4 + x, place * 16 + y * 4 + x)
            return carry

        if steps_z == (0,):
            for step_x in range(1, 4):
                x = lax.rem(digit_x + step_x, 4)
                visit(digit_y * 16 + digit_z * 4 + x, digit_z * 16 + digit_y * 4 + x)
        lax.fori_loop(1 if steps_z == (0,) else 0, 4, row, 0)

    def grp_peers(visit):
        def one(step, carry):
            visit(lax.rem(g + step, GRP))
            return carry

        lax.fori_loop(1, GRP, one, 0)

    barrier = pltpu.get_barrier_semaphore()
    for steps_z in ((2,), (1, 3), (0,)):
        slab_peers(
            lambda peer, slot: pl.semaphore_signal(barrier, inc=1, device_id={"slab": peer}, device_id_type=MESH),
            steps_z,
        )
    grp_peers(lambda peer: pl.semaphore_signal(barrier, inc=1, device_id={"grp": peer}, device_id_type=MESH))

    def send_slab(sent, landed, which, steps_z):
        sem = which * 3 + steps_z[0]

        def start(peer, slot):
            pltpu.make_async_remote_copy(
                sent.at[slot], landed.at[my_slot], slab_send.at[sem], slab_recv.at[sem],
                device_id={"slab": peer}, device_id_type=MESH,
            ).start()

        slab_peers(start, steps_z)

    def exchange_grp(sent, landed, sem):
        def start(peer):
            pltpu.make_async_remote_copy(
                sent.at[peer], landed.at[g], send_sems.at[sem], recv_sems.at[sem],
                device_id={"grp": peer}, device_id_type=MESH,
            ).start()

        grp_peers(start)
        landed[g] = sent[g]

    def finish(buffer, sem, count):
        block = buffer.at[pl.ds(0, count)]
        pltpu.make_async_copy(block, block, sem).wait()

    loads[0].wait()
    lines = force_lines(lambda part, z2: fields[part, pl.ds(z2, 16, stride=2), :])
    loads[1].wait()
    send1[...] = x_forward(lines, wx[...]).reshape(SLAB, 2, 2 * N)
    pl.semaphore_wait(barrier, SLAB - 1 + GRP - 1)

    send_slab(send1, recv1, 0, (2,))

    for load in loads[2:6]:
        load.wait()
    ids = jnp.concatenate([grain[pl.ds(z2, 16, stride=2), :] for z2 in range(2)], axis=0)
    high, low = ids // N, ids % N
    entry = jnp.zeros((32, N), jnp.int32)
    for row in range(32):
        line = jnp.broadcast_to(orientation[row : row + 1, :], (32, N))
        entry = jnp.where(high == row, jnp.take_along_axis(line, low, axis=1), entry)
    ceramic = jnp.concatenate([phase[pl.ds(z2, 16, stride=2), :] for z2 in range(2)], axis=0) == 1
    entry = jnp.where(ceramic, entry, 6)

    @pl.when(core == 0)
    def _():
        send_slab(send1, recv1, 0, (1, 3))

    masks = [entry == t for t in range(6)]
    for pair in range(81):
        value = jnp.full((32, N), contrast[pair // 9, 6, pair % 9], F32)
        for t in range(6):
            value = jnp.where(masks[t], contrast[pair // 9, t, pair % 9], value)
        coef[pair] = value

    @pl.when(core == 1)
    def _():
        send_slab(send1, recv1, 0, (1, 3))

    send_slab(send1, recv1, 0, (0,))
    recv1[my_slot] = send1[my_slot]
    for load in loads[6:]:
        load.wait()
    own_real[...], own_imag[...], alpha[...], beta[...] = operator_tables(dx, dy, dz)

    def part1(step_z):
        place = lax.rem(digit_z + step_z, 4)
        return z_forward_part(recv1[pl.ds(place * 16, 16)].reshape(32, 2 * N), wz[place])

    finish(recv1, slab_recv.at[0], 15)
    total = part1(0)
    finish(recv1, slab_recv.at[2], 16)
    total = total + part1(2)
    finish(recv1, slab_recv.at[1], 32)
    rows, edge = z_forward_end(total + part1(1) + part1(3))
    send2[...] = rows.reshape(GRP, 16, N)
    exchange_grp(send2, recv2, 0)
    edge2_out[...] = edge.reshape(GRP, 2, N)
    exchange_grp(edge2_out, edge2_in, 1)

    finish(recv2, recv_sems.at[0], GRP - 1)
    finish(edge2_in, recv_sems.at[1], GRP - 1)
    real, imag = y_forward(
        recv2[...].reshape(N, N), edge2_in[...].reshape(16, N), corner, wy[...], wl[...], we[...], tw
    )
    real, imag = operator(real, imag, own_real[...], own_imag[...], alpha[...], beta[...])
    rows, edge_real, edge_imag = y_inverse(real, imag, corner, wyi[...], wli[...], wei[...], tw)
    send3[...] = rows.reshape(GRP, 16, N)
    exchange_grp(send3, recv3, 2)
    edge3_out[:, 0:1, :] = edge_real.reshape(GRP, 1, N)
    edge3_out[:, 1:2, :] = edge_imag.reshape(GRP, 1, N)
    exchange_grp(edge3_out, edge3_in, 3)

    finish(recv3, recv_sems.at[2], GRP - 1)
    finish(edge3_in, recv_sems.at[3], GRP - 1)
    parts = z_inverse_begin(recv3[...].reshape(N, N), edge3_in[...].reshape(16, N))

    def part4(step_z):
        place = lax.rem(digit_z + step_z, 4)
        send4[pl.ds(place * 16, 16)] = z_inverse_part(parts, wzi[place]).reshape(16, 2, 2 * N)

    part4(2)
    send_slab(send4, recv4, 1, (2,))
    part4(1)
    part4(3)
    finish(send4, slab_send.at[5], 16)
    send_slab(send4, recv4, 1, (1, 3))
    part4(0)
    send_slab(send4, recv4, 1, (0,))
    recv4[my_slot] = send4[my_slot]

    for sem, count in ((3, 15), (4, 32), (5, 16)):
        finish(recv4, slab_recv.at[sem], count)
    green = gradients(x_inverse(recv4[...].reshape(N, 2 * N), wxi[...]))
    for i in range(9):
        total = jnp.concatenate([right_side[i, pl.ds(z2, 16, stride=2), :] for z2 in range(2)], axis=0)
        for j in range(9):
            total = total - coef[j * 9 + i] * green[j]
        for z2 in range(2):
            out[i, pl.ds(z2, 16, stride=2), :] = total[z2 * 16 : z2 * 16 + 16]

    for which, sent in enumerate((send1, send4)):
        for sem, count in enumerate((15, 32)):
            finish(sent, slab_send.at[which * 3 + sem], count)
    finish(send1, slab_send.at[2], 16)
    for sem, sent in enumerate((send2, edge2_out, send3, edge3_out)):
        finish(sent, send_sems.at[sem], GRP - 1)


def per_device(adjoint, source, contrast, phase_id, grain_id, orientation):
    table = constants()
    vmem = pl.BlockSpec(memory_space=pltpu.VMEM)
    hbm = pl.BlockSpec(memory_space=pltpu.HBM)
    flat = (9, 32, N)
    result = pl.pallas_call(
        kernel,
        out_shape=pltpu.VMEM(flat, F32),
        in_specs=[hbm] * (6 + len(CONSTANTS)),
        out_specs=vmem,
        scratch_shapes=[
            pltpu.VMEM((128, 384), BF16),
            pltpu.VMEM((384, 128), BF16),
            pltpu.VMEM((4, 256, 288), BF16),
            pltpu.VMEM((4, 96, 768), BF16),
            pltpu.VMEM((144, 384), BF16),
            pltpu.VMEM((128, 432), BF16),
            pltpu.VMEM((1152, 256), BF16),
            pltpu.VMEM((768, 384), BF16),
            pltpu.VMEM((32, 16), F32),
            pltpu.VMEM((16, 8), F32),
            pltpu.VMEM((2, 72, N), F32),
            pltpu.VMEM((2, 8, N), F32),
            pltpu.VMEM((2, 72, N), F32),
            pltpu.VMEM((2, 16, N), F32),
            pltpu.VMEM(flat, F32),
            pltpu.VMEM(flat, F32),
            pltpu.SMEM((9, 7, 9), F32),
            pltpu.VMEM((32, N), jnp.int32),
            pltpu.VMEM((32, N), jnp.int32),
            pltpu.VMEM((32, N), jnp.int32),
            pltpu.VMEM((SLAB, 2, 2 * N), F32),
            pltpu.VMEM((SLAB, 2, 2 * N), F32),
            pltpu.VMEM((GRP, 16, N), F32),
            pltpu.VMEM((GRP, 16, N), F32),
            pltpu.VMEM((GRP, 16, N), F32),
            pltpu.VMEM((GRP, 16, N), F32),
            pltpu.VMEM((SLAB, 2, 2 * N), F32),
            pltpu.VMEM((SLAB, 2, 2 * N), F32),
            pltpu.VMEM((GRP, 2, N), F32),
            pltpu.VMEM((GRP, 2, N), F32),
            pltpu.VMEM((GRP, 2, N), F32),
            pltpu.VMEM((GRP, 2, N), F32),
            pltpu.VMEM((81, 32, N), F32),
            pltpu.VMEM((72, N), F32),
            pltpu.VMEM((72, N), F32),
            pltpu.VMEM((72, N), F32),
            pltpu.VMEM((72, N), F32),
            pltpu.SemaphoreType.DMA((20,)),
            pltpu.SemaphoreType.DMA((4,)),
            pltpu.SemaphoreType.DMA((4,)),
            pltpu.SemaphoreType.DMA((6,)),
            pltpu.SemaphoreType.DMA((6,)),
        ],
        compiler_params=pltpu.CompilerParams(
            collective_id=0, has_side_effects=True, vmem_limit_bytes=60 * 1024 * 1024
        ),
    )(
        adjoint.reshape(flat),
        source.reshape(flat),
        contrast.transpose(1, 0, 2),
        phase_id.reshape(32, N),
        grain_id.reshape(32, N),
        orientation.reshape(32, N),
        *[jnp.asarray(table[name]) for name in CONSTANTS],
    )
    return result.reshape(adjoint.shape)


def solution(mesh):
    placed = (
        P(None, "grp", "slab", None),
        P(None, "grp", "slab", None),
        P(),
        P("grp", "slab", None),
        P("grp", "slab", None),
        P(),
    )
    return jax.shard_map(
        per_device,
        mesh=mesh,
        in_specs=placed,
        out_specs=P(None, "grp", "slab", None),
        check_vma=False,
    )
```
